32 devices in a mesh: layer: 8 (over z, x), box: 4 (over y, core).
Axes of the slice: x: 2, y: 2, z: 4, core: 2. Of those that a mesh axis runs over, the one named last changes fastest.
Arguments:
- box_maps: bfloat16 [8, 4096, 1024], P('layer', 'box'), may hold values from -0.1875 to 0.1875
- block_pattern: int32 [8, 32, 8], P('layer', 'box'), may hold values 0 or 1
- face_inverses: float32 [8, 3, 256, 256], P('layer'), may hold values from -0.375 to 0.375
- index_map: int32 [8, 1024], P('layer'), may hold values from 0 to 1023, each once within a row
- sources: float32 [8, 16, 1024], P('layer', 'box'), may hold values from -2.5 to 2.5
Outputs:
- merged: bfloat16 [8, 1024, 1024], P('layer')
- sweep_trace: float32 [8, 16, 1024], P('layer', 'box')
The draws below stay inside these ranges and needn't reach their ends.
Inputs may be any that keep to these rules, and one draw needn't show every extreme that they name: Each row of index_map is a permutation of 0 to 1023.
All inputs are finite; a program needn't handle non-finite values. No bound on the sum of `block_pattern` on one device may be relied on, other than what follows from the above.
Results may differ from the reference program's by a relative error of at most 0.025.
Values may be sent and summed in bfloat16 or wider, within the bound.
No kernel may reach another device: no remote copies, remote signals or barrier semaphores. Data moves between devices by JAX's collectives and lax.ppermute only.
A program may use at most 64 MiB of HBM per device.

```python
import math
import jax
import jax.numpy as jnp
from jax import lax

W = 1024
BLK = 128
K = 256
R = 16
WB = 8
LAYERS = 8
N_BOX = 4


def draw_box_maps(key, part):
    shape = (LAYERS, N_BOX * W, W)
    spread = 1.0 / math.sqrt(W)
    values = jnp.clip(jax.random.normal(key, shape, jnp.float32), -6.0, 6.0) * spread
    return values.astype(jnp.bfloat16)


def draw_face_inverses(key, part):
    shape = (LAYERS, N_BOX - 1, K, K)
    spread = 1.0 / math.sqrt(K)
    values = jnp.clip(jax.random.normal(key, shape, jnp.float32), -6.0, 6.0) * spread
    return values.astype(jnp.float32)


def touch_ends(entries, own_key, least, top_value):
    longest = entries.shape.index(max(entries.shape))
    spots = []
    for shift in (0, 1):
        where = [jax.random.randint(jax.random.fold_in(own_key, axis), (), 0, length) for axis, length in enumerate(entries.shape)]
        where[longest] = (where[longest] + shift) % entries.shape[longest]
        spots.append(tuple(where))
    return entries.at[spots[0]].set(least).at[spots[1]].set(top_value)


def shard_levels(key, extent, pieces, least, high):
    def one(position, parts):
        draws = jax.random.uniform(jax.random.fold_in(jax.random.fold_in(key, 6), position), (parts,), jnp.float32, least / len(pieces), high / len(pieces))
        return jnp.repeat(jnp.exp(draws), extent[position] // parts).reshape((-1,) + (1,) * (len(extent) - position - 1))

    gain = one(*pieces[0])
    for cut in pieces[1:]:
        gain = gain * one(*cut)
    return gain


def normal_values(rng, extent, scale, most, split=(), kind=jnp.bfloat16):
    loudness = shard_levels(rng, extent, split, -0.22, 0.18) if split else 1.0
    result = jax.random.normal(rng, extent, jnp.float32) * scale * loudness
    return jnp.minimum(jnp.maximum(result, -most), most).astype(kind)


def setup_inputs(seed: int = 0) -> dict:
    key_of = jax.random.split(jax.random.key(seed), 6)
    return {
        "box_maps": draw_box_maps(jax.random.fold_in(key_of[5], 71), 0),
        "block_pattern": touch_ends((jax.random.randint(key_of[1], (LAYERS, N_BOX * WB, WB), 0, 4) < 3).astype(jnp.int32), jax.random.fold_in(key_of[1], 1), 0, 1),
        "face_inverses": draw_face_inverses(jax.random.fold_in(key_of[5], 71), 0),
        "index_map": jax.vmap(lambda own: jax.random.permutation(own, W))(jax.random.split(key_of[3], LAYERS)).reshape((LAYERS, W)).astype(jnp.int32),
        "sources": normal_values(key_of[4], (LAYERS, R, W), 0.35, 2.5, ((0, 8), (1, 4)), jnp.float32),
    }


def mask_map(one_map, one_pattern):
    tiles = one_map.reshape(WB, BLK, WB, BLK)
    kept = one_pattern.astype(jnp.bfloat16)[:, None, :, None]
    return (tiles * kept).reshape(W, W)


def combine(first, second, inverse, level):
    joined = 0.5 * (first.astype(jnp.float32) + second.astype(jnp.float32))
    left_cols = joined[:, level * K:(level + 1) * K]
    right_rows = joined[level * K:(level + 1) * K, :]
    product = jnp.dot(left_cols, inverse, precision=lax.Precision.HIGHEST)
    return (joined - jnp.dot(product, right_rows, precision=lax.Precision.HIGHEST)).astype(jnp.bfloat16)


def merge_tree(maps_layer, pattern_layer, inverses_layer):
    tree_nodes = [mask_map(maps_layer[b * W:(b + 1) * W], pattern_layer[b * WB:(b + 1) * WB]) for b in range(N_BOX)]
    level = 0
    while len(tree_nodes) > 1:
        renewed = []
        for couple in range(len(tree_nodes) // 2):
            tree_node = (N_BOX >> (level + 1)) - 1 + couple
            renewed.append(combine(tree_nodes[2 * couple], tree_nodes[2 * couple + 1], inverses_layer[tree_node], level))
        tree_nodes = renewed
        level = level + 1
    return tree_nodes[0]


def reference(box_maps, block_pattern, face_inverses, index_map, sources):
    coupling = float(N_BOX) ** 0.5
    merged = lax.map(lambda t: merge_tree(t[0], t[1], t[2]), (box_maps, block_pattern, face_inverses))

    def down_step(previous, t):
        layer_map, order_map, source_rows = t
        gathered = previous[:, order_map].astype(jnp.bfloat16)
        current = source_rows + coupling * jnp.dot(gathered, layer_map.T, preferred_element_type=jnp.float32)
        return current, current

    initial = jnp.zeros((R, W), jnp.float32)
    _, downward = lax.scan(down_step, initial, (merged, index_map, sources))

    def up_step(following, t):
        layer_map, down_rows = t
        current = down_rows + coupling * jnp.dot(following.astype(jnp.bfloat16), layer_map, preferred_element_type=jnp.float32)
        return current, current

    _, upward = lax.scan(up_step, initial, (merged, downward), reverse=True)
    return merged, upward
```

```python
import functools

import jax
import jax.numpy as jnp
from jax import lax
from jax.experimental import pallas as pl
from jax.experimental.pallas import tpu as pltpu
from jax.sharding import PartitionSpec as P

AXES = ("layer", "box")


def combine_kernel(face_at, row_at, masked, is_face, *refs):
    refs = list(refs)
    if masked:
        own_pattern, other_pattern = refs.pop(0), refs.pop(0)
    own, other, inverse = refs.pop(0), refs.pop(0), refs.pop(0)
    face_rows = None if is_face else refs.pop(0)
    out = refs.pop(0)
    rows, width = own.shape
    face = inverse.shape[0]
    if masked:
        block = width // own_pattern.shape[1]
        strips = []
        for r in range(rows // block):
            tiles = []
            at = slice(r * block, (r + 1) * block)
            for c in range(width // block):
                cols = slice(c * block, (c + 1) * block)
                keep_own = 0.5 * own_pattern[row_at // block + r, c].astype(jnp.float32)
                keep_other = 0.5 * other_pattern[row_at // block + r, c].astype(jnp.float32)
                tiles.append(
                    own[at, cols].astype(jnp.float32) * keep_own
                    + other[at, cols].astype(jnp.float32) * keep_other
                )
            strips.append(jnp.concatenate(tiles, axis=1))
        joined = jnp.concatenate(strips, axis=0)
    else:
        joined = 0.5 * (own[...].astype(jnp.float32) + other[...].astype(jnp.float32))
    left = joined[:, face_at : face_at + face].astype(jnp.bfloat16)
    product = jnp.dot(left, inverse[...], preferred_element_type=jnp.float32)
    if is_face:
        right = joined.astype(jnp.bfloat16)
        refs.pop(0)[...] = right
    else:
        right = face_rows[...]
    out[...] = (
        joined
        - jnp.dot(product.astype(jnp.bfloat16), right, preferred_element_type=jnp.float32)
    ).astype(jnp.bfloat16)


def combine(own, other, inverse, face_rows, face_at, row_at, patterns):
    is_face = face_rows is None
    masked = patterns is not None
    rows, width = own.shape
    operands, specs = [], []
    if masked:
        operands += list(patterns)
        specs += [pl.BlockSpec(memory_space=pltpu.SMEM)] * 2
    operands += [own, other, inverse] + ([] if is_face else [face_rows])
    specs += [pl.BlockSpec(memory_space=pltpu.VMEM)] * (3 if is_face else 4)
    count = 2 if is_face else 1
    shape = jax.ShapeDtypeStruct((rows, width), jnp.bfloat16)
    result = pl.pallas_call(
        functools.partial(combine_kernel, face_at, row_at, masked, is_face),
        out_shape=[shape] * count,
        in_specs=specs,
        out_specs=[pl.BlockSpec(memory_space=pltpu.VMEM)] * count,
        compiler_params=pltpu.CompilerParams(vmem_limit_bytes=16 * 1024 * 1024),
        cost_estimate=pl.CostEstimate(
            flops=2 * rows * inverse.shape[0] * (width + inverse.shape[0]),
            bytes_accessed=2 * rows * width * 3,
            transcendentals=0,
        ),
    )(*operands)
    return result if is_face else (result[0], face_rows)


def row_times(rows, one_map):
    return jnp.dot(rows, one_map, preferred_element_type=jnp.float32)


def row_times_t(rows, one_map):
    return lax.dot_general(
        rows, one_map, (((1,), (1,)), ((), ())), preferred_element_type=jnp.float32
    )


def on_device(box_maps, block_pattern, face_inverses, index_map, sources):
    boxes = lax.axis_size("box")
    layers = lax.axis_size("layer")
    coupling = float(boxes) ** 0.5
    levels = boxes.bit_length() - 1
    face = face_inverses.shape[2]
    width = box_maps.shape[2]
    position = lax.axis_index("box")
    layer = lax.axis_index("layer")
    odd = layer % 2 == 1
    group = layer // 2
    groups = layers // 2
    leads = range(0, boxes, 2)

    def flat(at_layer, at_box):
        return at_layer * boxes + at_box

    def send(value, route):
        return lax.ppermute(value, AXES, route)

    to_lead = [(flat(i, b + 1), flat(i, b)) for i in range(layers) for b in leads]
    from_lead = [(target, source) for source, target in to_lead]
    to_pair = [(flat(i, b), flat(i ^ 1, b)) for i in range(layers) for b in leads]

    def to_box(level):
        return [(flat(i, b), flat(i, b ^ (1 << level))) for i in range(layers) for b in leads]

    def to_group(here, there):
        return [
            (flat(2 * here + side, b), flat(2 * there + side, b)) for side in (0, 1) for b in leads
        ]

    coarse = [(at, face) for at in range(0, width, face)]
    fine = coarse[:-1] + [(width - face, face // 2), (width - face // 2, face // 2)]

    inverses = face_inverses[0].astype(jnp.bfloat16)

    def inverse_of(level):
        node = (boxes >> (level + 1)) - 1 + (position >> (level + 1))
        return lax.dynamic_index_in_dim(inverses, node, 0, keepdims=False)

    raw = box_maps[0]
    patterns = (block_pattern[0], send(block_pattern[0], to_lead))
    raw_other = {at: send(raw[at : at + size], to_lead) for at, size in coarse}
    face_rows = None
    current = {}
    inverse = inverse_of(0)
    for at, size in coarse:
        current[at], face_rows = combine(
            raw[at : at + size], raw_other[at], inverse, face_rows, 0, at, patterns
        )

    pieces = coarse
    arrays = {}
    for level in range(1, levels):
        last = level == levels - 1
        wanted = fine if last else coarse
        first = [piece for piece in wanted if piece[0] == level * face and piece[1] == face]
        order = first + [piece for piece in wanted if piece not in first]
        held = {}
        for at, size in order:
            base = at // face * face
            held[at] = current[base][at - base : at - base + size]
        inverse = inverse_of(level)
        received = {at: send(held[at], to_box(level)) for at, size in order}
        face_rows = None
        current = {}
        for at, size in order:
            current[at], face_rows = combine(
                held[at], received[at], inverse, face_rows, level * face, 0, None
            )
        pieces = order

    rows_here = sources.shape[1]
    own_sources = lax.all_gather(sources[0], "box", axis=0, tiled=True)
    pair_sources = send(own_sources, to_pair)
    own_index = index_map[0]
    pair_index = send(index_map, to_pair)[0]
    place = lax.broadcasted_iota(jnp.int32, (width, width), 0)
    one_hot = []
    for side in (0, 1):
        index = jnp.where(odd == (side == 1), own_index, pair_index)
        one_hot.append((place == index[None, :]).astype(jnp.bfloat16))

    empty = jnp.zeros((width, width), jnp.bfloat16)
    maps = [empty, empty]
    permuted = [empty, empty]
    merged = empty
    for at, size in pieces:
        own = current[at]
        other = send(own, to_pair)
        merged = lax.dynamic_update_slice(merged, own, (at, 0))
        for side in (0, 1):
            piece = jnp.where(odd == (side == 1), own, other)
            maps[side] = lax.dynamic_update_slice(maps[side], piece, (at, 0))
            moved = row_times_t(piece, one_hot[side]).astype(jnp.bfloat16)
            permuted[side] = lax.dynamic_update_slice(permuted[side], moved, (at, 0))

    even_sources = jnp.where(odd, pair_sources, own_sources)
    odd_sources = jnp.where(odd, own_sources, pair_sources)

    arrived = None
    down_even = jnp.zeros(own_sources.shape, jnp.float32)
    down_odd = down_even
    for step in range(groups):
        here = group == step
        now_even = even_sources
        if arrived is not None:
            now_even = even_sources + coupling * row_times_t(arrived, permuted[0])
        now_odd = odd_sources + coupling * row_times_t(
            now_even.astype(jnp.bfloat16), permuted[1]
        )
        if step < groups - 1:
            arrived = send(now_odd.astype(jnp.bfloat16), to_group(step, step + 1))
        down_even = jnp.where(here, now_even, down_even)
        down_odd = jnp.where(here, now_odd, down_odd)

    arrived = None
    up_even = jnp.zeros(own_sources.shape, jnp.float32)
    up_odd = up_even
    for step in reversed(range(groups)):
        here = group == step
        now_odd = down_odd
        if arrived is not None:
            now_odd = down_odd + coupling * row_times(arrived, maps[1])
        now_even = down_even + coupling * row_times(now_odd.astype(jnp.bfloat16), maps[0])
        if step > 0:
            arrived = send(now_even.astype(jnp.bfloat16), to_group(step, step - 1))
        up_even = jnp.where(here, now_even, up_even)
        up_odd = jnp.where(here, now_odd, up_odd)

    up_own = jnp.where(odd, up_odd, up_even)
    lead_at = position // 2 * 2 * rows_here
    lead_rows = lax.dynamic_slice_in_dim(up_own, lead_at, rows_here, 0)
    next_rows = send(
        lax.dynamic_slice_in_dim(up_own, lead_at + rows_here, rows_here, 0), from_lead
    )
    is_lead = position % 2 == 0
    upward = jnp.where(is_lead, lead_rows, next_rows)
    merged = jnp.where(is_lead, merged, send(merged, from_lead))
    return (merged[None], upward[None])


def solution(mesh):
    return jax.shard_map(
        on_device,
        mesh=mesh,
        in_specs=(
            P("layer", "box", None),
            P("layer", "box", None),
            P("layer", None, None, None),
            P("layer", None),
            P("layer", "box", None),
        ),
        out_specs=(P("layer", None, None), P("layer", "box", None)),
        check_vma=False,
    )
```

```python
import functools

import jax
import jax.numpy as jnp
from jax import lax
from jax.experimental import pallas as pl
from jax.experimental.pallas import tpu as pltpu
from jax.sharding import PartitionSpec as P

AXES = ("layer", "box")
VMEM = pl.BlockSpec(memory_space=pltpu.VMEM)
SMEM = pl.BlockSpec(memory_space=pltpu.SMEM)
PARAMS = pltpu.CompilerParams(vmem_limit_bytes=24 * 1024 * 1024)
OWN, PAIR, EXTRA = 0, 1, 2


def cost(flops, moved):
    return pl.CostEstimate(flops=flops, bytes_accessed=moved, transcendentals=0)


def dot32(a, b):
    return jnp.dot(a, b, preferred_element_type=jnp.float32)


def dot32_t(a, b):
    return lax.dot_general(a, b, (((1,), (1,)), ((), ())), preferred_element_type=jnp.float32)


def minus_face(joined, face_at, inverse, right):
    face = inverse.shape[0]
    left = joined[:, face_at : face_at + face].astype(jnp.bfloat16)
    product = dot32(left, inverse).astype(jnp.bfloat16)
    return (joined - dot32(product, right)).astype(jnp.bfloat16)


def masked_mean(own, other, own_pattern, other_pattern, row_at, row_count, block_at):
    width = own.shape[1]
    block = width // own_pattern.shape[1]
    strips = []
    for r in range(row_count // block):
        tiles = []
        at = slice(row_at + r * block, row_at + (r + 1) * block)
        for c in range(width // block):
            cols = slice(c * block, (c + 1) * block)
            keep_own = 0.5 * own_pattern[block_at + r, c].astype(jnp.float32)
            keep_other = 0.5 * other_pattern[block_at + r, c].astype(jnp.float32)
            tiles.append(
                own[at, cols].astype(jnp.float32) * keep_own
                + other[at, cols].astype(jnp.float32) * keep_other
            )
        strips.append(jnp.concatenate(tiles, axis=1))
    return jnp.concatenate(strips, axis=0)


def leaf_kernel(first_row, is_face, own_pattern, other_pattern, own, other, inverse, *refs):
    refs = list(refs)
    face = inverse.shape[0]
    right = None if is_face else refs.pop(0)[...]
    block = own.shape[1] // own_pattern.shape[1]
    for i in range(own.shape[0] // face):
        joined = masked_mean(
            own, other, own_pattern, other_pattern, i * face, face, (first_row + i * face) // block
        )
        if right is None:
            right = joined.astype(jnp.bfloat16)
            refs[-1][...] = right
        refs[i][...] = minus_face(joined, 0, inverse[...], right)


def leaf_combine(own_pattern, other_pattern, own, other, inverse, face_rows, half):
    is_face = face_rows is None
    width = own.shape[1]
    rows = own.shape[0] // 2
    face = inverse.shape[0]
    count = rows // face
    piece = jax.ShapeDtypeStruct((face, width), jnp.bfloat16)
    map_spec = pl.BlockSpec((rows, width), lambda i: (half, 0))
    extra = [] if is_face else [face_rows]
    results = pl.pallas_call(
        functools.partial(leaf_kernel, half * rows, is_face),
        grid=(1,),
        out_shape=[piece] * (count + (1 if is_face else 0)),
        in_specs=[SMEM, SMEM, map_spec, map_spec, VMEM] + [VMEM] * len(extra),
        out_specs=[VMEM] * (count + (1 if is_face else 0)),
        compiler_params=PARAMS,
        cost_estimate=cost(2 * rows * face * (width + face), 6 * rows * width),
    )(own_pattern, other_pattern, own, other, inverse, *extra)
    return results


def combine_kernel(face_at, is_face, own, other, inverse, *refs):
    joined = 0.5 * (own[...].astype(jnp.float32) + other[...].astype(jnp.float32))
    if is_face:
        right = joined.astype(jnp.bfloat16)
        refs[1][...] = right
        refs[0][...] = minus_face(joined, face_at, inverse[...], right)
    else:
        refs[1][...] = minus_face(joined, face_at, inverse[...], refs[0][...])


def combine(own, other, inverse, face_rows, face_at):
    is_face = face_rows is None
    rows, width = own.shape
    extra = [] if is_face else [face_rows]
    shape = jax.ShapeDtypeStruct((rows, width), jnp.bfloat16)
    result = pl.pallas_call(
        functools.partial(combine_kernel, face_at, is_face),
        out_shape=[shape] * (2 if is_face else 1),
        in_specs=[VMEM] * (3 + len(extra)),
        out_specs=[VMEM] * (2 if is_face else 1),
        compiler_params=PARAMS,
        cost_estimate=cost(2 * rows * inverse.shape[0] * (width + inverse.shape[0]), 6 * rows * width),
    )(own, other, inverse, *extra)
    return (result[0], result[1]) if is_face else (result[0], face_rows)


def spread(pieces, rows):
    return jnp.concatenate([dot32_t(rows, piece[...]) for piece in pieces], axis=1)


def gather_sum(pieces, rows):
    at, total = 0, None
    for piece in pieces:
        size = piece.shape[0]
        term = dot32(rows[:, at : at + size], piece[...])
        total = term if total is None else total + term
        at += size
    return total


def segment_kernel(coupling, pieces_each, down_steps, up_steps, *refs):
    refs = list(refs)
    state = refs.pop(0)[...]
    maps, downs = {}, {}
    operands = []
    for slot in down_steps:
        operands.append((refs.pop(0), refs.pop(0)))
        maps[slot] = [refs.pop(0) for _ in range(pieces_each)]
    for slot in up_steps:
        if slot not in down_steps:
            downs[slot] = refs.pop(0)[...]
            maps[slot] = [refs.pop(0) for _ in range(pieces_each)]
    for slot, (source, one_hot) in zip(down_steps, operands):
        moved = dot32(state, one_hot[...]).astype(jnp.bfloat16)
        downs[slot] = source[...] + coupling * spread(maps[slot], moved)
        state = downs[slot].astype(jnp.bfloat16)
        refs.pop(0)[...] = downs[slot]
    for slot in up_steps:
        value = downs[slot] + coupling * gather_sum(maps[slot], state)
        state = value.astype(jnp.bfloat16)
        refs.pop(0)[...] = value
    refs.pop(0)[...] = state


def segment(coupling, arrived, sources, one_hots, downs, maps, down_steps, up_steps):
    operands = [arrived]
    for slot in down_steps:
        operands += [sources[slot], one_hots[slot], *maps[slot]]
    for slot in up_steps:
        if slot not in down_steps:
            operands += [downs[slot], *maps[slot]]
    rows = jax.ShapeDtypeStruct(arrived.shape, jnp.float32)
    steps = len(down_steps) + len(up_steps)
    results = pl.pallas_call(
        functools.partial(segment_kernel, coupling, len(maps[OWN]), down_steps, up_steps),
        out_shape=[rows] * steps + [jax.ShapeDtypeStruct(arrived.shape, jnp.bfloat16)],
        in_specs=[VMEM] * len(operands),
        out_specs=[VMEM] * (steps + 1),
        compiler_params=PARAMS,
        cost_estimate=cost(steps * 2 * 256 * 1024 * 1024, steps * 2 * 1024 * 1024),
    )(*operands)
    return results[:-1], results[-1]


def last_kernel(coupling, count, odd, from_pair, from_own, source, down_odd, *refs):
    own, pair, out = refs[:count], refs[count : 2 * count], refs[2 * count]
    total = gather_sum(pair, from_pair[...]) + gather_sum(own, from_own[...])
    up_odd = down_odd[...] + coupling * total
    up_even = source[...] + coupling * gather_sum(own, up_odd.astype(jnp.bfloat16))
    out[...] = jnp.where(odd[0] == 1, up_odd, up_even)


def on_device(box_maps, block_pattern, face_inverses, index_map, sources):
    boxes = lax.axis_size("box")
    layers = lax.axis_size("layer")
    coupling = float(boxes) ** 0.5
    levels = boxes.bit_length() - 1
    face = face_inverses.shape[2]
    width = box_maps.shape[2]
    rows_here = sources.shape[1]
    position = lax.axis_index("box")
    layer = lax.axis_index("layer")
    is_lead = position % 2 == 0
    pairs = layers // 2
    leads = range(0, boxes, 2)

    chain = []
    for p in range(1, pairs, 3):
        chain.append((2 * p, (OWN, PAIR, EXTRA)))
        chain.append((2 * (p + 2) + 1, (EXTRA, PAIR, OWN)))

    def route(moves, source_core=0, target_core=0):
        return [
            (a * boxes + b + source_core, z * boxes + b + target_core)
            for a, z in moves
            for b in leads
        ]

    def send(value, pairs_of_devices):
        return lax.ppermute(value, AXES, pairs_of_devices)

    every = [(i, i) for i in range(layers)]
    pair_moves = [(at ^ 1, at) for at, _ in chain]
    extra_moves = [(at + 2 if at % 2 == 0 else at - 2, at) for at, _ in chain]
    everywhere = [
        (i * boxes + b, i * boxes + (b ^ 1)) for i in range(layers) for b in range(boxes)
    ]

    raw = box_maps[0]
    pattern = block_pattern[0]
    raw_other = send(raw, everywhere)
    pattern_other = send(pattern, everywhere)
    next_sources = send(sources[0], route(every, 1, 0))

    def inverse_of(level):
        node = (boxes >> (level + 1)) - 1 + (position >> (level + 1))
        return lax.dynamic_index_in_dim(face_inverses[0], node, 0, keepdims=False).astype(
            jnp.bfloat16
        )

    inverse = inverse_of(0)
    half = width // 2 // face
    top = leaf_combine(pattern, pattern_other, raw, raw_other, inverse, None, 0)
    bottom = leaf_combine(pattern, pattern_other, raw, raw_other, inverse, top[-1], 1)
    current = list(top[:half]) + list(bottom)

    count = width // face
    order = list(range(count))
    for level in range(1, levels):
        mask = 1 << level
        if level == levels - 1:
            moves = [
                (i * boxes + b, i * boxes + (b ^ mask ^ 1)) for i in range(layers) for b in leads
            ]
        else:
            moves = [
                (i * boxes + b, i * boxes + (b ^ mask)) for i in range(layers) for b in range(boxes)
            ]
        inverse = inverse_of(level)
        order = [level] + [j for j in range(count) if j != level]
        received = {j: send(current[j], moves) for j in order}
        face_rows = None
        renewed = [None] * count
        for j in order:
            renewed[j], face_rows = combine(
                current[j], received[j], inverse, face_rows, level * face
            )
        before, current = current, renewed

    packed = jnp.concatenate(
        [sources[0], next_sources, index_map.astype(jnp.float32)], axis=0
    )
    packed, _ = lax.optimization_barrier((packed, before[count - 1]))
    small = [
        packed,
        send(packed, route(pair_moves + [(0, 1)])),
        send(packed, route(extra_moves)),
    ]
    place = lax.broadcasted_iota(jnp.int32, (width, width), 0)
    row_sources = [entry[: 2 * rows_here] for entry in small]
    one_hots = [
        (place == entry[2 * rows_here :].astype(jnp.int32)).astype(jnp.bfloat16)
        for entry in small
    ]

    maps = [[None] * count for _ in range(3)]
    for j in order:
        maps[PAIR][j] = send(current[j], route(pair_moves + [(1, 0)], 1, 0))
        maps[EXTRA][j] = send(current[j], route(extra_moves, 1, 0))
        maps[OWN][j] = send(current[j], route(every, 1, 0))
    merged = jnp.concatenate(
        [jnp.where(is_lead, maps[OWN][j], current[j]) for j in range(count)], axis=0
    )

    first = row_sources[PAIR].astype(jnp.bfloat16)
    (down_odd,), state = segment(
        coupling, first, row_sources, one_hots, {}, maps, (OWN,), ()
    )
    at = 1
    kept = []
    ups = {}
    for k, (target, slots) in enumerate(chain):
        arrived = send(state, route([(at, target)]))
        at = target
        turn = k == len(chain) - 1
        if turn:
            arrived, merged = lax.optimization_barrier((arrived, merged))
        rows, state = segment(
            coupling,
            arrived,
            row_sources,
            one_hots,
            {},
            maps,
            slots,
            tuple(reversed(slots))[1:] if turn else (),
        )
        kept.append(dict(zip(slots, rows)))
        if turn:
            ups[at] = dict(zip(tuple(reversed(slots))[1:], rows[len(slots) :]))
            ups[at][slots[-1]] = rows[len(slots) - 1]
    down_odd_pair = send(down_odd, route([(1, 0)]))
    down_odd = jnp.where(layer == 0, down_odd_pair, down_odd)

    for k in reversed(range(len(chain) - 1)):
        target, slots = chain[k]
        arrived = send(state, route([(at, target)]))
        at = target
        back = tuple(reversed(slots))
        rows, state = segment(
            coupling, arrived, row_sources, one_hots, kept[k], maps, (), back
        )
        ups[at] = dict(zip(back, rows))
    from_pair = send(state, route([(at, 0)]))
    from_own = send(state, route([(at, 1)]))

    mine = [jnp.zeros(row_sources[OWN].shape, jnp.float32)] * 3
    for target, values in ups.items():
        for slot in (OWN, PAIR, EXTRA):
            mine[slot] = jnp.where(layer == target, values[slot], mine[slot])
    settled = (
        mine[OWN]
        + send(mine[PAIR], route([(z, a) for a, z in pair_moves]))
        + send(mine[EXTRA], route([(z, a) for a, z in extra_moves]))
    )

    odd = (layer % 2).astype(jnp.int32)[None]
    last = pl.pallas_call(
        functools.partial(last_kernel, coupling, count),
        out_shape=jax.ShapeDtypeStruct(row_sources[OWN].shape, jnp.float32),
        in_specs=[SMEM] + [VMEM] * (4 + 2 * count),
        out_specs=VMEM,
        compiler_params=PARAMS,
        cost_estimate=cost(6 * 256 * 1024 * 1024, 6 * 1024 * 1024),
    )(odd, from_pair, from_own, row_sources[OWN], down_odd, *maps[OWN], *maps[PAIR])
    upward = jnp.where(layer < 2, last, settled)
    next_rows = send(upward[rows_here:], route(every, 0, 1))
    upward = jnp.where(is_lead, upward[:rows_here], next_rows)
    return (merged[None], upward[None])


def solution(mesh):
    return jax.shard_map(
        on_device,
        mesh=mesh,
        in_specs=(
            P("layer", "box", None),
            P("layer", "box", None),
            P("layer", None, None, None),
            P("layer", None),
            P("layer", "box", None),
        ),
        out_specs=(P("layer", None, None), P("layer", "box", None)),
        check_vma=False,
    )
```

```python
import functools

import jax
import jax.numpy as jnp
from jax import lax
from jax.experimental import pallas as pl
from jax.experimental.pallas import tpu as pltpu
from jax.sharding import PartitionSpec as P

AXES = ("layer", "box")
LAST_PIECES = ((0, 256), (256, 256), (512, 256), (768, 128), (896, 128))
Y_TIE = 2
X_TIE = 2
VMEM = pl.BlockSpec(memory_space=pltpu.VMEM)
SMEM = pl.BlockSpec(memory_space=pltpu.SMEM)
PARAMS = pltpu.CompilerParams(vmem_limit_bytes=24 * 1024 * 1024)
OWN, PAIR, EXTRA = 0, 1, 2


def cost(flops, moved):
    return pl.CostEstimate(flops=flops, bytes_accessed=moved, transcendentals=0)


def dot32(a, b):
    return jnp.dot(a, b, preferred_element_type=jnp.float32)


def dot32_t(a, b):
    return lax.dot_general(a, b, (((1,), (1,)), ((), ())), preferred_element_type=jnp.float32)


def minus_face(joined, face_at, inverse, right):
    face = inverse.shape[0]
    left = joined[:, face_at : face_at + face].astype(jnp.bfloat16)
    product = dot32(left, inverse).astype(jnp.bfloat16)
    return (joined - dot32(product, right)).astype(jnp.bfloat16)


def masked(values, pattern, row_at, row_count, block_at):
    width = values.shape[1]
    block = width // pattern.shape[1]
    strips = []
    for r in range(row_count // block):
        at = slice(row_at + r * block, row_at + (r + 1) * block)
        strips.append(
            jnp.concatenate(
                [
                    values[at, c * block : (c + 1) * block].astype(jnp.float32)
                    * (0.5 * pattern[block_at + r, c].astype(jnp.float32))
                    for c in range(width // block)
                ],
                axis=1,
            )
        )
    return jnp.concatenate(strips, axis=0)


def mask_kernel(pattern, values, out):
    block = values.shape[1] // pattern.shape[1]
    for r in range(values.shape[0] // block):
        out[r * block : (r + 1) * block] = masked(values, pattern, r * block, block, r).astype(
            jnp.bfloat16
        )


def leaf_kernel(first_row, is_face, pieces, other_pattern, own, other, inverse, *refs):
    refs = list(refs)
    face = inverse.shape[0]
    right = None if is_face else refs.pop(0)[...]
    block = own.shape[1] // other_pattern.shape[1]
    for i in range(own.shape[0] // face):
        at = first_row + i * face
        joined = own[i * face : (i + 1) * face].astype(jnp.float32) + masked(
            other, other_pattern, i * face, face, at // block
        )
        if right is None:
            right = joined.astype(jnp.bfloat16)
            refs[-1][...] = right
        result = minus_face(joined, 0, inverse[...], right)
        for ref, (start, size) in zip(refs, pieces):
            low, high = max(start, at), min(start + size, at + face)
            if low < high:
                ref[low - start : high - start] = result[low - at : high - at]


def leaf_combine(other_pattern, own, other, inverse, face_rows, half, pieces):
    is_face = face_rows is None
    width = own.shape[1]
    rows = own.shape[0] // 2
    face = inverse.shape[0]
    shapes = [jax.ShapeDtypeStruct((size, width), jnp.bfloat16) for _, size in pieces]
    if is_face:
        shapes.append(jax.ShapeDtypeStruct((face, width), jnp.bfloat16))
    map_spec = pl.BlockSpec((rows, width), lambda i: (half, 0))
    extra = [] if is_face else [face_rows]
    return pl.pallas_call(
        functools.partial(leaf_kernel, half * rows, is_face, pieces),
        grid=(1,),
        out_shape=shapes,
        in_specs=[SMEM, map_spec, map_spec, VMEM] + [VMEM] * len(extra),
        out_specs=[VMEM] * len(shapes),
        compiler_params=PARAMS,
        cost_estimate=cost(2 * rows * face * (width + face), 6 * rows * width),
    )(other_pattern, own, other, inverse, *extra)


def combine_kernel(face_at, is_face, whole_rows, own, other, inverse, *refs):
    refs = list(refs)
    joined = 0.5 * (own[...].astype(jnp.float32) + other[...].astype(jnp.float32))
    if is_face:
        right = joined.astype(jnp.bfloat16)
    else:
        right = refs.pop(0)[...]
        refs.pop(0)
    piece = minus_face(joined, face_at, inverse[...], right)
    refs[0][...] = piece
    refs[1][whole_rows, :] = piece
    if is_face:
        refs[2][...] = right


def combine(own, other, inverse, state, face_at, row_at):
    is_face = state is None
    rows, width = own.shape
    extra = [] if is_face else list(state)
    piece = jax.ShapeDtypeStruct((rows, width), jnp.bfloat16)
    whole = jax.ShapeDtypeStruct((width, width), jnp.bfloat16)
    result = pl.pallas_call(
        functools.partial(combine_kernel, face_at, is_face, slice(row_at, row_at + rows)),
        out_shape=[piece, whole] + ([piece] if is_face else []),
        in_specs=[VMEM] * (3 + len(extra)),
        out_specs=[VMEM] * (3 if is_face else 2),
        input_output_aliases={} if is_face else {4: 1},
        compiler_params=PARAMS,
        cost_estimate=cost(0, 0),
    )(own, other, inverse, *extra)
    return result[0], ((result[2] if is_face else state[0]), result[1])


def spread(pieces, rows):
    return jnp.concatenate([dot32_t(rows, piece[...]) for piece in pieces], axis=1)


def gather_sum(pieces, rows):
    at, total = 0, None
    for piece in pieces:
        size = piece.shape[0]
        term = dot32(rows[:, at : at + size], piece[...])
        total = term if total is None else total + term
        at += size
    return total


def lanes_at(rows, index_row):
    lanes = 128
    count, width = rows.shape
    parts = [rows[:, at : at + lanes] for at in range(0, width, lanes)]
    outs = []
    for at in range(0, width, lanes):
        index = jnp.broadcast_to(index_row[:, at : at + lanes].astype(jnp.int32), (count, lanes))
        lane, part = index % lanes, index // lanes
        total = jnp.zeros((count, lanes), rows.dtype)
        for k, values in enumerate(parts):
            total = jnp.where(part == k, jnp.take_along_axis(values, lane, axis=1), total)
        outs.append(total)
    return jnp.concatenate(outs, axis=1)


def segment_kernel(coupling, pieces_of, down_steps, up_steps, *refs):
    refs = list(refs)
    state = refs.pop(0)[...]
    maps, downs = {}, {}
    operands = []
    for slot in down_steps:
        operands.append(refs.pop(0))
        maps[slot] = [refs.pop(0) for _ in range(pieces_of[slot])]
    for slot in up_steps:
        if slot not in down_steps:
            downs[slot] = refs.pop(0)[...]
            maps[slot] = [refs.pop(0) for _ in range(pieces_of[slot])]
    for slot, packed in zip(down_steps, operands):
        count = state.shape[0]
        moved = lanes_at(state.astype(jnp.float32), packed[count:]).astype(jnp.bfloat16)
        downs[slot] = packed[:count] + coupling * spread(maps[slot], moved)
        state = downs[slot].astype(jnp.bfloat16)
        refs.pop(0)[...] = downs[slot]
    for slot in up_steps:
        value = downs[slot] + coupling * gather_sum(maps[slot], state)
        state = value.astype(jnp.bfloat16)
        refs.pop(0)[...] = value
    refs.pop(0)[...] = state


def segment(coupling, arrived, packed, downs, maps, down_steps, up_steps):
    operands = [arrived]
    for slot in down_steps:
        operands += [packed[slot], *maps[slot]]
    for slot in up_steps:
        if slot not in down_steps:
            operands += [downs[slot], *maps[slot]]
    rows = jax.ShapeDtypeStruct(arrived.shape, jnp.float32)
    steps = len(down_steps) + len(up_steps)
    results = pl.pallas_call(
        functools.partial(
            segment_kernel, coupling, [len(entry) for entry in maps], down_steps, up_steps
        ),
        out_shape=[rows] * steps + [jax.ShapeDtypeStruct(arrived.shape, jnp.bfloat16)],
        in_specs=[VMEM] * len(operands),
        out_specs=[VMEM] * (steps + 1),
        compiler_params=PARAMS,
        cost_estimate=cost(steps * 2 * 256 * 1024 * 1024, steps * 2 * 1024 * 1024),
    )(*operands)
    return results[:-1], results[-1]


def last_kernel(coupling, count, odd, from_pair, from_own, source, down_odd, *refs):
    own, pair, out = refs[:1], refs[1 : 1 + count], refs[1 + count]
    total = gather_sum(pair, from_pair[...]) + gather_sum(own, from_own[...])
    up_odd = down_odd[...] + coupling * total
    up_even = source[...] + coupling * gather_sum(own, up_odd.astype(jnp.bfloat16))
    out[...] = jnp.where(odd[0] == 1, up_odd, up_even)


def on_device(box_maps, block_pattern, face_inverses, index_map, sources):
    boxes = lax.axis_size("box")
    layers = lax.axis_size("layer")
    coupling = float(boxes) ** 0.5
    levels = boxes.bit_length() - 1
    face = face_inverses.shape[2]
    width = box_maps.shape[2]
    rows_here = sources.shape[1]
    position = lax.axis_index("box")
    layer = lax.axis_index("layer")
    is_lead = position % 2 == 1
    pairs = layers // 2

    chain = []
    for p in range(1, pairs, 3):
        chain.append((2 * p, (OWN, PAIR, EXTRA)))
        chain.append((2 * (p + 2) + 1, (EXTRA, PAIR, OWN)))

    def route(moves, source_core=1, target_core=1):
        return [
            (a * boxes + b + source_core, z * boxes + b + target_core)
            for a, z in moves
            for b in range(0, boxes, 2)
        ]

    def send(value, pairs_of_devices):
        return lax.ppermute(value, AXES, pairs_of_devices)

    def after(value, *others):
        return lax.optimization_barrier((value, *others))[0]

    every = [(i, i) for i in range(layers)]
    pair_moves = [(at ^ 1, at) for at, _ in chain]
    extra_moves = [(at + 2 if at % 2 == 0 else at - 2, at) for at, _ in chain]

    def over_box(change, starts):
        return [(i * boxes + b, i * boxes + (b ^ change)) for i in range(layers) for b in starts]

    raw = box_maps[0]
    pattern = block_pattern[0]
    raw_other = send(raw, over_box(1, range(boxes)))
    pattern_other = send(pattern, over_box(1, range(boxes)))
    next_sources = send(sources[0], route(every, 0, 1))
    own_half = pl.pallas_call(
        mask_kernel,
        out_shape=jax.ShapeDtypeStruct(raw.shape, jnp.bfloat16),
        in_specs=[SMEM, VMEM],
        out_specs=VMEM,
        compiler_params=PARAMS,
        cost_estimate=cost(width * width, 4 * width * width),
    )(pattern, raw)

    def inverse_of(level):
        node = (boxes >> (level + 1)) - 1 + (position >> (level + 1))
        return lax.dynamic_index_in_dim(face_inverses[0], node, 0, keepdims=False).astype(
            jnp.bfloat16
        )

    whole_faces = tuple((at, face) for at in range(0, width, face))
    last_face = (levels - 1) * face
    if last_face == face:
        parts = LAST_PIECES
    else:
        parts = whole_faces
    cuts = [tuple(parts)] if levels == 2 else [whole_faces] * (levels - 1)

    inverse = inverse_of(0)
    half = width // 2
    upper = tuple(piece for piece in cuts[0] if piece[0] < half)
    lower = tuple(piece for piece in cuts[0] if piece[0] >= half)
    top = leaf_combine(pattern_other, own_half, raw_other, inverse, None, 0, upper)
    bottom = leaf_combine(pattern_other, own_half, raw_other, inverse, top[-1], 1, lower)
    current = dict(zip(upper + lower, [*top[:-1], *bottom]))

    rows = -(-2 * rows_here // 8) * 8
    packed = jnp.concatenate(
        [
            next_sources,
            sources[0],
            jnp.zeros((rows - 2 * rows_here, width), jnp.float32),
            index_map.astype(jnp.float32),
        ],
        axis=0,
    )
    sendable = after(packed, bottom[0])
    small = [
        packed,
        send(sendable, route(pair_moves + [(0, 1)])),
        send(sendable, route(extra_moves)),
    ]

    maps = [[], [], []]
    for level in range(1, levels):
        final = level == levels - 1
        change = 1 << level
        if final:
            moves = over_box(change ^ 1, range(0, boxes, 2))
        else:
            moves = over_box(change, range(boxes))
        inverse = inverse_of(level)
        order = sorted(current, key=lambda piece: (piece[0] != level * face, piece[0]))
        received = {}
        for k, piece in enumerate(order):
            value = current[piece]
            if k >= Y_TIE:
                value = after(value, received[order[k - Y_TIE]])
            received[piece] = send(value, moves)
        state = None
        sent = {PAIR: {}, EXTRA: {}}
        renewed = {}
        for k, piece in enumerate(order):
            other = received[piece]
            if final and k == 0:
                other = after(other, small[PAIR], small[EXTRA])
            if final and k >= X_TIE:
                before = order[k - X_TIE]
                other = after(other, sent[PAIR][before], sent[EXTRA][before])
            renewed[piece], state = combine(
                current[piece], other, inverse, state, level * face, piece[0]
            )
            if final:
                sent[PAIR][piece] = send(renewed[piece], route(pair_moves + [(1, 0)]))
                sent[EXTRA][piece] = send(renewed[piece], route(extra_moves))
        current = renewed
    merged = state[1]
    inner = sorted(current)
    maps = [[merged]] + [[sent[slot][piece] for piece in inner] for slot in (PAIR, EXTRA)]

    first = small[PAIR][:rows].astype(jnp.bfloat16)
    (down_odd,), state = segment(coupling, first, small, {}, maps, (OWN,), ())
    at = 1
    kept = []
    ups = {}
    for k, (target, slots) in enumerate(chain):
        arrived = send(state, route([(at, target)]))
        at = target
        turn = k == len(chain) - 1
        back = tuple(reversed(slots))
        results, state = segment(
            coupling, arrived, small, {}, maps, slots, back[1:] if turn else ()
        )
        kept.append(dict(zip(slots, results)))
        if k == 0:
            copied = send(after(merged, state), route(every, 1, 0))
        if turn:
            ups[at] = dict(zip(back[1:], results[len(slots) :]))
            ups[at][back[0]] = results[len(slots) - 1]
    down_odd = jnp.where(layer == 0, send(after(down_odd, state), route([(1, 0)])), down_odd)
    merged = jnp.where(is_lead, merged, after(copied, state))

    for k in reversed(range(len(chain) - 1)):
        target, slots = chain[k]
        arrived = send(state, route([(at, target)]))
        if k == len(chain) - 2:
            arrived, merged = lax.optimization_barrier((arrived, merged))
        at = target
        back = tuple(reversed(slots))
        results, state = segment(coupling, arrived, small, kept[k], maps, (), back)
        ups[at] = dict(zip(back, results))
    from_pair = send(state, route([(at, 0)]))
    from_own = send(state, route([(at, 1)]))

    mine = [jnp.zeros((rows, width), jnp.float32)] * 3
    for target, values in ups.items():
        for slot in (OWN, PAIR, EXTRA):
            mine[slot] = jnp.where(layer == target, values[slot], mine[slot])
    settled = (
        mine[OWN]
        + send(mine[PAIR], route([(z, a) for a, z in pair_moves]))
        + send(mine[EXTRA], route([(z, a) for a, z in extra_moves]))
    )

    odd = (layer % 2).astype(jnp.int32)[None]
    last = pl.pallas_call(
        functools.partial(last_kernel, coupling, len(inner)),
        out_shape=jax.ShapeDtypeStruct((rows, width), jnp.float32),
        in_specs=[SMEM] + [VMEM] * (5 + len(inner)),
        out_specs=VMEM,
        compiler_params=PARAMS,
        cost_estimate=cost(6 * 256 * 1024 * 1024, 6 * 1024 * 1024),
    )(odd, from_pair, from_own, packed[:rows], down_odd, *maps[OWN], *maps[PAIR])
    upward = jnp.where(layer < 2, last, settled)
    lead_rows = upward[rows_here : 2 * rows_here]
    upward = jnp.where(is_lead, lead_rows, send(upward[:rows_here], route(every, 1, 0)))
    return (merged[None], upward[None])


def solution(mesh):
    return jax.shard_map(
        on_device,
        mesh=mesh,
        in_specs=(
            P("layer", "box", None),
            P("layer", "box", None),
            P("layer", None, None, None),
            P("layer", None),
            P("layer", "box", None),
        ),
        out_specs=(P("layer", None, None), P("layer", "box", None)),
        check_vma=False,
    )
```

```python
import functools

import jax
import jax.numpy as jnp
from jax import lax
from jax.experimental import pallas as pl
from jax.experimental.pallas import tpu as pltpu
from jax.sharding import PartitionSpec as P

AXES = ("layer", "box")
AHEAD = 2
SMALL_AT = 0
VMEM = pl.BlockSpec(memory_space=pltpu.VMEM)
SMEM = pl.BlockSpec(memory_space=pltpu.SMEM)
PARAMS = pltpu.CompilerParams(vmem_limit_bytes=10 * 1024 * 1024)
OWN, PAIR, EXTRA = 0, 1, 2


def cost(flops, moved):
    return pl.CostEstimate(flops=flops, bytes_accessed=moved, transcendentals=0)


def dot32(a, b):
    return jnp.dot(a, b, preferred_element_type=jnp.float32)


def dot32_t(a, b):
    return lax.dot_general(a, b, (((1,), (1,)), ((), ())), preferred_element_type=jnp.float32)


def minus_face(joined, face_at, inverse, right):
    face = inverse.shape[0]
    left = joined[:, face_at : face_at + face].astype(jnp.bfloat16)
    product = dot32(left, inverse).astype(jnp.bfloat16)
    return (joined - dot32(product, right)).astype(jnp.bfloat16)


def masked(values, pattern, row_at, row_count, block_at):
    width = values.shape[1]
    block = width // pattern.shape[1]
    strips = []
    for r in range(row_count // block):
        at = slice(row_at + r * block, row_at + (r + 1) * block)
        strips.append(
            jnp.concatenate(
                [
                    values[at, c * block : (c + 1) * block].astype(jnp.float32)
                    * (0.5 * pattern[block_at + r, c].astype(jnp.float32))
                    for c in range(width // block)
                ],
                axis=1,
            )
        )
    return jnp.concatenate(strips, axis=0)


def mask_kernel(pattern, values, out):
    block = values.shape[1] // pattern.shape[1]
    for r in range(values.shape[0] // block):
        out[r * block : (r + 1) * block] = masked(values, pattern, r * block, block, r).astype(
            jnp.bfloat16
        )


def leaf_kernel(first_row, is_face, pieces, other_pattern, own, other, inverse, *refs):
    refs = list(refs)
    face = inverse.shape[0]
    right = None if is_face else refs.pop(0)[...]
    block = own.shape[1] // other_pattern.shape[1]
    for i in range(own.shape[0] // face):
        at = first_row + i * face
        joined = own[i * face : (i + 1) * face].astype(jnp.float32) + masked(
            other, other_pattern, i * face, face, at // block
        )
        if right is None:
            right = joined.astype(jnp.bfloat16)
            refs[-1][...] = right
        result = minus_face(joined, 0, inverse[...], right)
        for ref, (start, size) in zip(refs, pieces):
            low, high = max(start, at), min(start + size, at + face)
            if low < high:
                ref[low - start : high - start] = result[low - at : high - at]


def leaf_combine(other_pattern, own, other, inverse, face_rows, half, pieces):
    is_face = face_rows is None
    width = own.shape[1]
    rows = own.shape[0] // 2
    face = inverse.shape[0]
    shapes = [jax.ShapeDtypeStruct((size, width), jnp.bfloat16) for _, size in pieces]
    if is_face:
        shapes.append(jax.ShapeDtypeStruct((face, width), jnp.bfloat16))
    map_spec = pl.BlockSpec((rows, width), lambda i: (half, 0))
    extra = [] if is_face else [face_rows]
    return pl.pallas_call(
        functools.partial(leaf_kernel, half * rows, is_face, pieces),
        grid=(1,),
        out_shape=shapes,
        in_specs=[SMEM, map_spec, map_spec, VMEM] + [VMEM] * len(extra),
        out_specs=[VMEM] * len(shapes),
        compiler_params=PARAMS,
        cost_estimate=cost(2 * rows * face * (width + face), 6 * rows * width),
    )(other_pattern, own, other, inverse, *extra)


def combine_kernel(face_at, is_face, with_next, whole_rows, is_second, own, other, inverse, *refs):
    refs = list(refs)
    following = refs.pop(0) if with_next else None
    joined = 0.5 * (own[...].astype(jnp.float32) + other[...].astype(jnp.float32))
    if is_face:
        right = joined.astype(jnp.bfloat16)
    else:
        right = refs.pop(0)[...]
        refs.pop(0)
    piece = minus_face(joined, face_at, inverse[...], right)
    refs[1][whole_rows, :] = piece
    if is_face:
        refs[2][...] = right
    refs[0][...] = piece
    if with_next:

        @pl.when(is_second[0] == 0)
        def _():
            refs[0][...] = following[...]


def combine(is_second, own, other, inverse, following, state, face_at, row_at):
    is_face = state is None
    rows, width = own.shape
    extra = [] if following is None else [following]
    aliases = {} if is_face else {4 + len(extra) + 1: 1}
    extra += [] if is_face else list(state)
    piece = jax.ShapeDtypeStruct((rows, width), jnp.bfloat16)
    whole = jax.ShapeDtypeStruct((width, width), jnp.bfloat16)
    result = pl.pallas_call(
        functools.partial(
            combine_kernel,
            face_at,
            is_face,
            following is not None,
            slice(row_at, row_at + rows),
        ),
        out_shape=[piece, whole] + ([piece] if is_face else []),
        in_specs=[SMEM] + [VMEM] * (3 + len(extra)),
        out_specs=[VMEM] * (3 if is_face else 2),
        input_output_aliases=aliases,
        compiler_params=PARAMS,
        cost_estimate=cost(0, 0),
    )(is_second, own, other, inverse, *extra)
    return result[0], ((result[2] if is_face else state[0]), result[1])


def spread(pieces, rows):
    return jnp.concatenate([dot32_t(rows, piece[...]) for piece in pieces], axis=1)


def gather_sum(pieces, rows):
    at, total = 0, None
    for piece in pieces:
        size = piece.shape[0]
        term = dot32(rows[:, at : at + size], piece[...])
        total = term if total is None else total + term
        at += size
    return total


def lanes_at(rows, index_row):
    lanes = 128
    count, width = rows.shape
    parts = [rows[:, at : at + lanes] for at in range(0, width, lanes)]
    outs = []
    for at in range(0, width, lanes):
        index = jnp.broadcast_to(index_row[:, at : at + lanes].astype(jnp.int32), (count, lanes))
        lane, part = index % lanes, index // lanes
        total = jnp.zeros((count, lanes), rows.dtype)
        for k, values in enumerate(parts):
            total = jnp.where(part == k, jnp.take_along_axis(values, lane, axis=1), total)
        outs.append(total)
    return jnp.concatenate(outs, axis=1)


def segment_kernel(coupling, pieces_of, down_steps, up_steps, *refs):
    refs = list(refs)
    state = refs.pop(0)[...]
    maps, downs = {}, {}
    operands = []
    for slot in down_steps:
        operands.append(refs.pop(0))
        maps[slot] = [refs.pop(0) for _ in range(pieces_of[slot])]
    for slot in up_steps:
        if slot not in down_steps:
            downs[slot] = refs.pop(0)[...]
            maps[slot] = [refs.pop(0) for _ in range(pieces_of[slot])]
    for slot, packed in zip(down_steps, operands):
        count = state.shape[0]
        moved = lanes_at(state.astype(jnp.float32), packed[count:]).astype(jnp.bfloat16)
        downs[slot] = packed[:count] + coupling * spread(maps[slot], moved)
        state = downs[slot].astype(jnp.bfloat16)
        refs.pop(0)[...] = downs[slot]
    for slot in up_steps:
        value = downs[slot] + coupling * gather_sum(maps[slot], state)
        state = value.astype(jnp.bfloat16)
        refs.pop(0)[...] = value
    refs.pop(0)[...] = state


def segment(coupling, arrived, packed, downs, maps, down_steps, up_steps):
    operands = [arrived]
    for slot in down_steps:
        operands += [packed[slot], *maps[slot]]
    for slot in up_steps:
        if slot not in down_steps:
            operands += [downs[slot], *maps[slot]]
    rows = jax.ShapeDtypeStruct(arrived.shape, jnp.float32)
    steps = len(down_steps) + len(up_steps)
    results = pl.pallas_call(
        functools.partial(
            segment_kernel, coupling, [len(entry) for entry in maps], down_steps, up_steps
        ),
        out_shape=[rows] * steps + [jax.ShapeDtypeStruct(arrived.shape, jnp.bfloat16)],
        in_specs=[VMEM] * len(operands),
        out_specs=[VMEM] * (steps + 1),
        compiler_params=PARAMS,
        cost_estimate=cost(steps * 2 * 256 * 1024 * 1024, steps * 2 * 1024 * 1024),
    )(*operands)
    return results[:-1], results[-1]


def last_kernel(coupling, count, odd, from_pair, from_own, source, down_odd, *refs):
    own, pair, out = refs[:1], refs[1 : 1 + count], refs[1 + count]
    total = gather_sum(pair, from_pair[...]) + gather_sum(own, from_own[...])
    up_odd = down_odd[...] + coupling * total
    up_even = source[...] + coupling * gather_sum(own, up_odd.astype(jnp.bfloat16))
    out[...] = jnp.where(odd[0] == 1, up_odd, up_even)


def on_device(box_maps, block_pattern, face_inverses, index_map, sources):
    boxes = lax.axis_size("box")
    layers = lax.axis_size("layer")
    coupling = float(boxes) ** 0.5
    levels = boxes.bit_length() - 1
    face = face_inverses.shape[2]
    width = box_maps.shape[2]
    rows_here = sources.shape[1]
    position = lax.axis_index("box")
    layer = lax.axis_index("layer")
    is_second = position % 2 == 1
    second_flag = is_second.astype(jnp.int32)[None]

    chain = [(layer_at, (OWN, PAIR)) for layer_at in range(2, layers, 2)]
    pair_moves = [(layer_at + 1, layer_at) for layer_at in range(0, layers, 2)]

    def route(moves, source_core=0, target_core=0):
        return [
            (a * boxes + b + source_core, z * boxes + b + target_core)
            for a, z in moves
            for b in range(0, boxes, 2)
        ]

    def over_box(change, starts):
        return [(i * boxes + b, i * boxes + (b ^ change)) for i in range(layers) for b in starts]

    def send(value, pairs_of_devices):
        return lax.ppermute(value, AXES, pairs_of_devices)

    def after(value, *others):
        return lax.optimization_barrier((value, *others))[0]

    every = [(i, i) for i in range(layers)]

    raw = box_maps[0]
    pattern = block_pattern[0]
    raw_other = send(raw, over_box(1, range(boxes)))
    pattern_other = send(pattern, over_box(1, range(boxes)))
    other_sources = send(sources[0], over_box(1, range(boxes)))
    own_half = pl.pallas_call(
        mask_kernel,
        out_shape=jax.ShapeDtypeStruct(raw.shape, jnp.bfloat16),
        in_specs=[SMEM, VMEM],
        out_specs=VMEM,
        compiler_params=PARAMS,
        cost_estimate=cost(width * width, 4 * width * width),
    )(after(pattern, other_sources), raw)

    def inverse_of(level):
        node = (boxes >> (level + 1)) - 1 + (position >> (level + 1))
        return lax.dynamic_index_in_dim(face_inverses[0], node, 0, keepdims=False).astype(
            jnp.bfloat16
        )

    rows = -(-2 * rows_here // 8) * 8
    packed = jnp.concatenate(
        [
            jnp.where(is_second, other_sources, sources[0]),
            jnp.where(is_second, sources[0], other_sources),
            jnp.zeros((rows - 2 * rows_here, width), jnp.float32),
            index_map.astype(jnp.float32),
        ],
        axis=0,
    )

    pieces = tuple((at, face) for at in range(0, width, face))
    upper = tuple(piece for piece in pieces if piece[0] < width // 2)
    lower = tuple(piece for piece in pieces if piece[0] >= width // 2)
    inverse = inverse_of(0)
    top = leaf_combine(pattern_other, own_half, raw_other, inverse, None, 0, upper)
    bottom = leaf_combine(pattern_other, own_half, raw_other, inverse, top[-1], 1, lower)
    current = dict(zip(upper + lower, [*top[:-1], *bottom]))

    for level in range(1, levels):
        final = level == levels - 1
        change = 1 << level
        inverse = inverse_of(level)
        order = sorted(pieces, key=lambda piece: (piece[0] != level * face, piece[0]))
        received = {}
        state = None
        if not final:
            for piece in order:
                received[piece] = send(current[piece], over_box(change, range(boxes)))
            renewed = {}
            for piece in order:
                renewed[piece], state = combine(
                    second_flag,
                    current[piece],
                    received[piece],
                    inverse,
                    None,
                    state,
                    level * face,
                    piece[0],
                )
            current = renewed
            continue
        over = over_box(change ^ 1, range(0, boxes, 2))
        forward = route(pair_moves, 1, 0)
        for piece in order[:AHEAD]:
            received[piece] = send(current[piece], over)
        pair_pieces = {}
        for k, piece in enumerate(order):
            following = order[k + AHEAD] if k + AHEAD < len(order) else None
            other = received[piece]
            if k == SMALL_AT + 2:
                other = after(other, pair_packed)
            if k > AHEAD:
                other = after(other, pair_pieces[order[k - 1]])
            payload, state = combine(
                second_flag,
                current[piece],
                other,
                inverse,
                None if following is None else current[following],
                state,
                level * face,
                piece[0],
            )
            pair_pieces[piece] = send(payload, forward + ([] if following is None else over))
            if following is not None:
                received[following] = pair_pieces[piece]
            if k == SMALL_AT:
                sendable = after(packed, payload)
                pair_packed = send(sendable, route(pair_moves[1:]) + route([(0, 1)], 1, 1))
    merged = state[1]
    small = [packed, pair_packed]
    pair_maps = [pair_pieces[piece] for piece in pieces]

    first = pair_packed[:rows].astype(jnp.bfloat16)
    (down_odd,), state = segment(
        coupling, first, small, {}, [[merged], pair_maps], (OWN,), ()
    )
    merged_first = send(after(merged, state), route(every, 1, 0))
    maps = [[merged_first], pair_maps]
    at, core = 1, 1
    kept = []
    ups = {}
    for k, (target, slots) in enumerate(chain):
        arrived = send(state, route([(at, target)], core, 0))
        at, core = target, 0
        turn = k == len(chain) - 1
        back = tuple(reversed(slots))
        results, state = segment(
            coupling, arrived, small, {}, maps, slots, back[1:] if turn else ()
        )
        kept.append(dict(zip(slots, results)))
        if k == 0:
            down_odd_first = send(after(down_odd, state), route([(1, 0)], 1, 0))
        if turn:
            ups[at] = dict(zip(back[1:], results[len(slots) :]))
            ups[at][back[0]] = results[len(slots) - 1]
    merged = jnp.where(is_second, merged, merged_first)
    down_odd = jnp.where(layer == 0, down_odd_first, down_odd)

    for k in reversed(range(len(chain) - 1)):
        target, slots = chain[k]
        arrived = send(state, route([(at, target)]))
        if k == len(chain) - 2:
            arrived, merged = lax.optimization_barrier((arrived, merged))
        at = target
        back = tuple(reversed(slots))
        results, state = segment(coupling, arrived, small, kept[k], maps, (), back)
        ups[at] = dict(zip(back, results))
    from_own = send(state, route([(at, 1)], 0, 1))
    from_pair = send(state, route([(at, 0)]))

    mine = [jnp.zeros((rows, width), jnp.float32)] * 2
    for target, values in ups.items():
        for slot in (OWN, PAIR):
            mine[slot] = jnp.where(layer == target, values[slot], mine[slot])
    settled = mine[OWN] + send(mine[PAIR], route([(z, a) for a, z in pair_moves[1:]]))

    odd = (layer % 2).astype(jnp.int32)[None]
    last = pl.pallas_call(
        functools.partial(last_kernel, coupling, len(pair_maps)),
        out_shape=jax.ShapeDtypeStruct((rows, width), jnp.float32),
        in_specs=[SMEM] + [VMEM] * (5 + len(pair_maps)),
        out_specs=VMEM,
        compiler_params=PARAMS,
        cost_estimate=cost(6 * 256 * 1024 * 1024, 6 * 1024 * 1024),
    )(odd, from_pair, from_own, packed[:rows], down_odd, merged, *pair_maps)
    upward = jnp.where(layer < 2, last, settled)
    ends = upward[:rows_here], upward[rows_here : 2 * rows_here]
    there = send(
        jnp.where(is_second, ends[0], ends[1]),
        route([(1, 1)], 1, 0) + route([move for move in every if move[0] != 1], 0, 1),
    )
    here = jnp.where(is_second, ends[1], ends[0])
    runs = jnp.logical_xor(is_second, layer != 1)
    return (merged[None], jnp.where(runs, here, there)[None])


def solution(mesh):
    return jax.shard_map(
        on_device,
        mesh=mesh,
        in_specs=(
            P("layer", "box", None),
            P("layer", "box", None),
            P("layer", None, None, None),
            P("layer", None),
            P("layer", "box", None),
        ),
        out_specs=(P("layer", None, None), P("layer", "box", None)),
        check_vma=False,
    )
```

```python
import functools

import jax
import jax.numpy as jnp
from jax import lax
from jax.experimental import pallas as pl
from jax.experimental.pallas import tpu as pltpu
from jax.sharding import PartitionSpec as P

AXES = ("layer", "box")
AHEAD = 2
SMALL_AT = 0
VMEM = pl.BlockSpec(memory_space=pltpu.VMEM)
SMEM = pl.BlockSpec(memory_space=pltpu.SMEM)
PARAMS = pltpu.CompilerParams(vmem_limit_bytes=24 * 1024 * 1024)
SWEEP_PARAMS = pltpu.CompilerParams(vmem_limit_bytes=10 * 1024 * 1024)
OWN, PAIR = 0, 1


def cost(flops, moved):
    return pl.CostEstimate(flops=flops, bytes_accessed=moved, transcendentals=0)


def dot32(a, b):
    return jnp.dot(a, b, preferred_element_type=jnp.float32)


def dot32_t(a, b):
    return lax.dot_general(a, b, (((1,), (1,)), ((), ())), preferred_element_type=jnp.float32)


def minus_face(joined, face_at, inverse, right):
    face = inverse.shape[0]
    left = joined[:, face_at : face_at + face].astype(jnp.bfloat16)
    product = dot32(left, inverse).astype(jnp.bfloat16)
    return (joined - dot32(product, right)).astype(jnp.bfloat16)


def masked(values, pattern, row_at, row_count, block_at):
    width = values.shape[1]
    block = width // pattern.shape[1]
    strips = []
    for r in range(row_count // block):
        at = slice(row_at + r * block, row_at + (r + 1) * block)
        strips.append(
            jnp.concatenate(
                [
                    values[at, c * block : (c + 1) * block].astype(jnp.float32)
                    * (0.5 * pattern[block_at + r, c].astype(jnp.float32))
                    for c in range(width // block)
                ],
                axis=1,
            )
        )
    return jnp.concatenate(strips, axis=0)


def mask_kernel(pattern, values, out):
    block = values.shape[1] // pattern.shape[1]
    for r in range(values.shape[0] // block):
        out[r * block : (r + 1) * block] = masked(values, pattern, r * block, block, r).astype(
            jnp.bfloat16
        )


def leaf_kernel(first_row, is_face, pieces, other_pattern, own, other, inverse, *refs):
    refs = list(refs)
    face = inverse.shape[0]
    right = None if is_face else refs.pop(0)[...]
    block = own.shape[1] // other_pattern.shape[1]
    for i in range(own.shape[0] // face):
        at = first_row + i * face
        joined = own[i * face : (i + 1) * face].astype(jnp.float32) + masked(
            other, other_pattern, i * face, face, at // block
        )
        if right is None:
            right = joined.astype(jnp.bfloat16)
            refs[-1][...] = right
        result = minus_face(joined, 0, inverse[...], right)
        for ref, (start, size) in zip(refs, pieces):
            low, high = max(start, at), min(start + size, at + face)
            if low < high:
                ref[low - start : high - start] = result[low - at : high - at]


def leaf_combine(other_pattern, own, other, inverse, face_rows, half, pieces):
    is_face = face_rows is None
    width = own.shape[1]
    rows = own.shape[0] // 2
    face = inverse.shape[0]
    shapes = [jax.ShapeDtypeStruct((size, width), jnp.bfloat16) for _, size in pieces]
    if is_face:
        shapes.append(jax.ShapeDtypeStruct((face, width), jnp.bfloat16))
    map_spec = pl.BlockSpec((rows, width), lambda i: (half, 0))
    extra = [] if is_face else [face_rows]
    return pl.pallas_call(
        functools.partial(leaf_kernel, half * rows, is_face, pieces),
        grid=(1,),
        out_shape=shapes,
        in_specs=[SMEM, map_spec, map_spec, VMEM] + [VMEM] * len(extra),
        out_specs=[VMEM] * len(shapes),
        compiler_params=PARAMS,
        cost_estimate=cost(2 * rows * face * (width + face), 6 * rows * width),
    )(other_pattern, own, other, inverse, *extra)


def combine_kernel(face_at, is_face, with_next, whole_rows, is_second, own, other, inverse, *refs):
    refs = list(refs)
    following = refs.pop(0) if with_next else None
    joined = 0.5 * (own[...].astype(jnp.float32) + other[...].astype(jnp.float32))
    if is_face:
        right = joined.astype(jnp.bfloat16)
    else:
        right = refs.pop(0)[...]
        refs.pop(0)
    piece = minus_face(joined, face_at, inverse[...], right)
    refs[1][whole_rows, :] = piece
    if is_face:
        refs[2][...] = right
    refs[0][...] = piece
    if with_next:

        @pl.when(is_second[0] == 0)
        def _():
            refs[0][...] = following[...]


def combine(is_second, own, other, inverse, following, state, face_at, row_at):
    is_face = state is None
    rows, width = own.shape
    extra = [] if following is None else [following]
    aliases = {} if is_face else {4 + len(extra) + 1: 1}
    extra += [] if is_face else list(state)
    piece = jax.ShapeDtypeStruct((rows, width), jnp.bfloat16)
    whole = jax.ShapeDtypeStruct((width, width), jnp.bfloat16)
    result = pl.pallas_call(
        functools.partial(
            combine_kernel,
            face_at,
            is_face,
            following is not None,
            slice(row_at, row_at + rows),
        ),
        out_shape=[piece, whole] + ([piece] if is_face else []),
        in_specs=[SMEM] + [VMEM] * (3 + len(extra)),
        out_specs=[VMEM] * (3 if is_face else 2),
        input_output_aliases=aliases,
        compiler_params=PARAMS,
        cost_estimate=cost(0, 0),
    )(is_second, own, other, inverse, *extra)
    return result[0], ((result[2] if is_face else state[0]), result[1])


def spread(pieces, rows):
    return jnp.concatenate([dot32_t(rows, piece[...]) for piece in pieces], axis=1)


def gather_sum(pieces, rows):
    at, total = 0, None
    for piece in pieces:
        size = piece.shape[0]
        term = dot32(rows[:, at : at + size], piece[...])
        total = term if total is None else total + term
        at += size
    return total


def lanes_at(rows, index_row):
    lanes = 128
    count, width = rows.shape
    parts = [rows[:, at : at + lanes] for at in range(0, width, lanes)]
    outs = []
    for at in range(0, width, lanes):
        index = jnp.broadcast_to(index_row[:, at : at + lanes].astype(jnp.int32), (count, lanes))
        lane, part = index % lanes, index // lanes
        total = jnp.zeros((count, lanes), rows.dtype)
        for k, values in enumerate(parts):
            total = jnp.where(part == k, jnp.take_along_axis(values, lane, axis=1), total)
        outs.append(total)
    return jnp.concatenate(outs, axis=1)


def segment_kernel(coupling, pieces_of, down_steps, up_steps, *refs):
    refs = list(refs)
    state = refs.pop(0)[...]
    maps, downs = {}, {}
    operands = []
    for slot in down_steps:
        operands.append(refs.pop(0))
        maps[slot] = [refs.pop(0) for _ in range(pieces_of[slot])]
    for slot in up_steps:
        if slot not in down_steps:
            downs[slot] = refs.pop(0)[...]
            maps[slot] = [refs.pop(0) for _ in range(pieces_of[slot])]
    for slot, packed in zip(down_steps, operands):
        count = state.shape[0]
        moved = lanes_at(state.astype(jnp.float32), packed[count:]).astype(jnp.bfloat16)
        downs[slot] = packed[:count] + coupling * spread(maps[slot], moved)
        state = downs[slot].astype(jnp.bfloat16)
        refs.pop(0)[...] = downs[slot]
    for slot in up_steps:
        value = downs[slot] + coupling * gather_sum(maps[slot], state)
        state = value.astype(jnp.bfloat16)
        refs.pop(0)[...] = value
    refs.pop(0)[...] = state


def segment(coupling, arrived, packed, downs, maps, down_steps, up_steps):
    operands = [arrived]
    for slot in down_steps:
        operands += [packed[slot], *maps[slot]]
    for slot in up_steps:
        if slot not in down_steps:
            operands += [downs[slot], *maps[slot]]
    rows = jax.ShapeDtypeStruct(arrived.shape, jnp.float32)
    steps = len(down_steps) + len(up_steps)
    results = pl.pallas_call(
        functools.partial(
            segment_kernel, coupling, [len(entry) for entry in maps], down_steps, up_steps
        ),
        out_shape=[rows] * steps + [jax.ShapeDtypeStruct(arrived.shape, jnp.bfloat16)],
        in_specs=[VMEM] * len(operands),
        out_specs=[VMEM] * (steps + 1),
        compiler_params=SWEEP_PARAMS,
        cost_estimate=cost(steps * 2 * 256 * 1024 * 1024, steps * 2 * 1024 * 1024),
    )(*operands)
    return results[:-1], results[-1]


def last_kernel(coupling, count, odd, from_pair, from_own, source, down_odd, *refs):
    own, pair, out = refs[:1], refs[1 : 1 + count], refs[1 + count]
    total = gather_sum(pair, from_pair[...]) + gather_sum(own, from_own[...])
    up_odd = down_odd[...] + coupling * total
    up_even = source[...] + coupling * gather_sum(own, up_odd.astype(jnp.bfloat16))
    out[...] = jnp.where(odd[0] == 1, up_odd, up_even)


def on_device(box_maps, block_pattern, face_inverses, index_map, sources):
    boxes = lax.axis_size("box")
    layers = lax.axis_size("layer")
    coupling = float(boxes) ** 0.5
    levels = boxes.bit_length() - 1
    face = face_inverses.shape[2]
    width = box_maps.shape[2]
    rows_here = sources.shape[1]
    position = lax.axis_index("box")
    layer = lax.axis_index("layer")
    is_second = position % 2 == 1
    second_flag = is_second.astype(jnp.int32)[None]

    chain = [(layer_at, (OWN, PAIR)) for layer_at in range(2, layers, 2)]
    pair_moves = [(layer_at + 1, layer_at) for layer_at in range(0, layers, 2)]

    def route(moves, source_core=0, target_core=0):
        return [
            (a * boxes + b + source_core, z * boxes + b + target_core)
            for a, z in moves
            for b in range(0, boxes, 2)
        ]

    def over_box(change, starts):
        return [(i * boxes + b, i * boxes + (b ^ change)) for i in range(layers) for b in starts]

    def send(value, pairs_of_devices):
        return lax.ppermute(value, AXES, pairs_of_devices)

    def after(value, *others):
        return lax.optimization_barrier((value, *others))[0]

    every = [(i, i) for i in range(layers)]

    raw = box_maps[0]
    pattern = block_pattern[0]
    raw_other = send(raw, over_box(1, range(boxes)))
    pattern_other = send(pattern, over_box(1, range(boxes)))
    other_sources = send(sources[0], over_box(1, range(boxes)))
    own_half = pl.pallas_call(
        mask_kernel,
        out_shape=jax.ShapeDtypeStruct(raw.shape, jnp.bfloat16),
        in_specs=[SMEM, VMEM],
        out_specs=VMEM,
        compiler_params=PARAMS,
        cost_estimate=cost(width * width, 4 * width * width),
    )(pattern, raw)

    def inverse_of(level):
        node = (boxes >> (level + 1)) - 1 + (position >> (level + 1))
        return lax.dynamic_index_in_dim(face_inverses[0], node, 0, keepdims=False).astype(
            jnp.bfloat16
        )

    rows = -(-2 * rows_here // 8) * 8
    packed = jnp.concatenate(
        [
            jnp.where(is_second, other_sources, sources[0]),
            jnp.where(is_second, sources[0], other_sources),
            jnp.zeros((rows - 2 * rows_here, width), jnp.float32),
            index_map.astype(jnp.float32),
        ],
        axis=0,
    )

    pieces = tuple((at, face) for at in range(0, width, face))
    upper = tuple(piece for piece in pieces if piece[0] < width // 2)
    lower = tuple(piece for piece in pieces if piece[0] >= width // 2)
    inverse = inverse_of(0)
    top = leaf_combine(pattern_other, own_half, raw_other, inverse, None, 0, upper)
    bottom = leaf_combine(pattern_other, own_half, raw_other, inverse, top[-1], 1, lower)
    current = dict(zip(upper + lower, [*top[:-1], *bottom]))

    for level in range(1, levels):
        final = level == levels - 1
        change = 1 << level
        inverse = inverse_of(level)
        order = sorted(pieces, key=lambda piece: (piece[0] != level * face, piece[0]))
        received = {}
        state = None
        if not final:
            for piece in order:
                received[piece] = send(current[piece], over_box(change, range(boxes)))
            renewed = {}
            for piece in order:
                renewed[piece], state = combine(
                    second_flag,
                    current[piece],
                    received[piece],
                    inverse,
                    None,
                    state,
                    level * face,
                    piece[0],
                )
            current = renewed
            continue
        over = over_box(change ^ 1, range(0, boxes, 2))
        forward = route(pair_moves, 1, 0)
        for piece in order[:AHEAD]:
            received[piece] = send(current[piece], over)
        pair_pieces = {}
        for k, piece in enumerate(order):
            following = order[k + AHEAD] if k + AHEAD < len(order) else None
            other = received[piece]
            if k == SMALL_AT + 2:
                other = after(other, pair_packed)
            if k > AHEAD:
                other = after(other, pair_pieces[order[k - 1]])
            payload, state = combine(
                second_flag,
                current[piece],
                other,
                inverse,
                None if following is None else current[following],
                state,
                level * face,
                piece[0],
            )
            pair_pieces[piece] = send(payload, forward + ([] if following is None else over))
            if following is not None:
                received[following] = pair_pieces[piece]
            if k == SMALL_AT:
                sendable = after(packed, payload)
                pair_packed = send(sendable, route(pair_moves[1:]) + route([(0, 1)], 1, 1))
    merged = state[1]
    small = [packed, pair_packed]
    pair_maps = [pair_pieces[piece] for piece in pieces]

    first = pair_packed[:rows].astype(jnp.bfloat16)
    (down_odd,), state = segment(
        coupling, first, small, {}, [[merged], pair_maps], (OWN,), ()
    )
    merged_first = send(after(merged, state), route(every, 1, 0))
    maps = [[merged_first], pair_maps]
    at, core = 1, 1
    kept = []
    ups = {}
    for k, (target, slots) in enumerate(chain):
        arrived = send(state, route([(at, target)], core, 0))
        at, core = target, 0
        turn = k == len(chain) - 1
        back = tuple(reversed(slots))
        results, state = segment(
            coupling, arrived, small, {}, maps, slots, back[1:] if turn else ()
        )
        kept.append(dict(zip(slots, results)))
        if k == 0:
            down_odd_first = send(after(down_odd, state), route([(1, 0)], 1, 0))
        if turn:
            ups[at] = dict(zip(back[1:], results[len(slots) :]))
            ups[at][back[0]] = results[len(slots) - 1]
    merged = jnp.where(is_second, merged, merged_first)
    down_odd = jnp.where(layer == 0, down_odd_first, down_odd)

    for k in reversed(range(len(chain) - 1)):
        target, slots = chain[k]
        arrived = send(state, route([(at, target)]))
        if k == len(chain) - 2:
            arrived, merged = lax.optimization_barrier((arrived, merged))
        at = target
        back = tuple(reversed(slots))
        results, state = segment(coupling, arrived, small, kept[k], maps, (), back)
        ups[at] = dict(zip(back, results))
    from_own = send(state, route([(at, 1)], 0, 1))
    from_pair = send(state, route([(at, 0)]))

    mine = [jnp.zeros((rows, width), jnp.float32)] * 2
    for target, values in ups.items():
        for slot in (OWN, PAIR):
            mine[slot] = jnp.where(layer == target, values[slot], mine[slot])
    settled = mine[OWN] + send(mine[PAIR], route([(z, a) for a, z in pair_moves[1:]]))

    odd = (layer % 2).astype(jnp.int32)[None]
    last = pl.pallas_call(
        functools.partial(last_kernel, coupling, len(pair_maps)),
        out_shape=jax.ShapeDtypeStruct((rows, width), jnp.float32),
        in_specs=[SMEM] + [VMEM] * (5 + len(pair_maps)),
        out_specs=VMEM,
        compiler_params=SWEEP_PARAMS,
        cost_estimate=cost(6 * 256 * 1024 * 1024, 6 * 1024 * 1024),
    )(odd, from_pair, from_own, packed[:rows], down_odd, merged, *pair_maps)
    upward = jnp.where(layer < 2, last, settled)
    ends = upward[:rows_here], upward[rows_here : 2 * rows_here]
    there = send(
        jnp.where(is_second, ends[0], ends[1]),
        route([(1, 1)], 1, 0) + route([move for move in every if move[0] != 1], 0, 1),
    )
    here = jnp.where(is_second, ends[1], ends[0])
    runs = jnp.logical_xor(is_second, layer != 1)
    return (merged[None], jnp.where(runs, here, there)[None])


def solution(mesh):
    return jax.shard_map(
        on_device,
        mesh=mesh,
        in_specs=(
            P("layer", "box", None),
            P("layer", "box", None),
            P("layer", None, None, None),
            P("layer", None),
            P("layer", "box", None),
        ),
        out_specs=(P("layer", None, None), P("layer", "box", None)),
        check_vma=False,
    )
```

```python
import functools

import jax
import jax.numpy as jnp
from jax import lax
from jax.experimental import pallas as pl
from jax.experimental.pallas import tpu as pltpu
from jax.sharding import PartitionSpec as P

AXES = ("layer", "box")
AHEAD = 2
SMALL_AT = 0
VMEM = pl.BlockSpec(memory_space=pltpu.VMEM)
SMEM = pl.BlockSpec(memory_space=pltpu.SMEM)
PARAMS = pltpu.CompilerParams(vmem_limit_bytes=24 * 1024 * 1024)
SWEEP_PARAMS = pltpu.CompilerParams(vmem_limit_bytes=10 * 1024 * 1024)
OWN, PAIR = 0, 1


def cost(flops, moved):
    return pl.CostEstimate(flops=flops, bytes_accessed=moved, transcendentals=0)


def dot32(a, b):
    return jnp.dot(a, b, preferred_element_type=jnp.float32)


def dot32_t(a, b):
    return lax.dot_general(a, b, (((1,), (1,)), ((), ())), preferred_element_type=jnp.float32)


def minus_face(joined, face_at, inverse, right):
    face = inverse.shape[0]
    left = joined[:, face_at : face_at + face].astype(jnp.bfloat16)
    product = dot32(left, inverse).astype(jnp.bfloat16)
    return (joined - dot32(product, right)).astype(jnp.bfloat16)


def masked(values, pattern, row_at, row_count, block_at):
    width = values.shape[1]
    block = width // pattern.shape[1]
    strips = []
    for r in range(row_count // block):
        at = slice(row_at + r * block, row_at + (r + 1) * block)
        strips.append(
            jnp.concatenate(
                [
                    values[at, c * block : (c + 1) * block].astype(jnp.float32)
                    * (0.5 * pattern[block_at + r, c].astype(jnp.float32))
                    for c in range(width // block)
                ],
                axis=1,
            )
        )
    return jnp.concatenate(strips, axis=0)


def mask_kernel(pattern, values, out):
    block = values.shape[1] // pattern.shape[1]
    for r in range(values.shape[0] // block):
        out[r * block : (r + 1) * block] = masked(values, pattern, r * block, block, r).astype(
            jnp.bfloat16
        )


def leaf_kernel(other_pattern, own, other_there, inverse, *refs):
    *outs, other, sems = refs
    count, face, width = other.shape
    block = width // other_pattern.shape[1]
    copies = [
        pltpu.make_async_copy(other_there.at[pl.ds(i * face, face)], other.at[i], sems.at[i])
        for i in range(count)
    ]
    for copy in copies:
        copy.start()
    right = None
    for i in range(count):
        copies[i].wait()
        joined = own[i * face : (i + 1) * face].astype(jnp.float32) + masked(
            other.at[i], other_pattern, 0, face, i * face // block
        )
        if right is None:
            right = joined.astype(jnp.bfloat16)
        outs[i][...] = minus_face(joined, 0, inverse[...], right)


def leaf_combine(other_pattern, own, other, inverse):
    width = own.shape[1]
    face = inverse.shape[0]
    count = width // face
    return pl.pallas_call(
        leaf_kernel,
        out_shape=[jax.ShapeDtypeStruct((face, width), jnp.bfloat16)] * count,
        in_specs=[SMEM, VMEM, pl.BlockSpec(memory_space=pl.ANY), VMEM],
        out_specs=[VMEM] * count,
        scratch_shapes=[
            pltpu.VMEM((count, face, width), jnp.bfloat16),
            pltpu.SemaphoreType.DMA((count,)),
        ],
        compiler_params=PARAMS,
        cost_estimate=cost(2 * width * face * (width + face), 6 * width * width),
    )(other_pattern, own, other, inverse)


def combine_kernel(face_at, is_face, with_next, with_rest, is_second, own, other, inverse, *refs):
    refs = list(refs)
    following = refs.pop(0) if with_next else None
    right = None if is_face else refs.pop(0)[...]
    before = refs.pop(0) if with_rest else None
    out = refs.pop(0)
    joined = 0.5 * (own[...].astype(jnp.float32) + other[...].astype(jnp.float32))
    if is_face:
        right = joined.astype(jnp.bfloat16)
        refs.pop(0)[...] = right
    at = 0
    if with_rest:
        at = before.shape[0]
        out[:at] = before[...]
    out[at:] = minus_face(joined, face_at, inverse[...], right)
    if with_next:

        @pl.when(is_second[0] == 0)
        def _():
            out[...] = following[...]


def combine(is_second, own, other, inverse, following, right, face_at, before=None):
    is_face = right is None
    rows, width = own.shape
    extra = [value for value in (following, right, before) if value is not None]
    out_rows = rows if before is None else rows + before.shape[0]
    outs = [jax.ShapeDtypeStruct((out_rows, width), jnp.bfloat16)]
    if is_face:
        outs.append(jax.ShapeDtypeStruct((rows, width), jnp.bfloat16))
    result = pl.pallas_call(
        functools.partial(
            combine_kernel, face_at, is_face, following is not None, before is not None
        ),
        out_shape=outs,
        in_specs=[SMEM] + [VMEM] * (3 + len(extra)),
        out_specs=[VMEM] * len(outs),
        compiler_params=PARAMS,
        cost_estimate=cost(0, 0),
    )(is_second, own, other, inverse, *extra)
    return result[0], (result[1] if is_face else right)


def assemble_kernel(*refs):
    *parts, out = refs
    at = 0
    for part in parts:
        out[at : at + part.shape[0]] = part[...]
        at += part.shape[0]


def assemble(parts):
    rows, width = sum(part.shape[0] for part in parts), parts[0].shape[1]
    return pl.pallas_call(
        assemble_kernel,
        out_shape=jax.ShapeDtypeStruct((rows, width), jnp.bfloat16),
        in_specs=[VMEM] * len(parts),
        out_specs=VMEM,
        compiler_params=PARAMS,
        cost_estimate=cost(0, 4 * rows * width),
    )(*parts)


def spread(pieces, rows):
    return jnp.concatenate([dot32_t(rows, piece[...]) for piece in pieces], axis=1)


def gather_sum(pieces, rows):
    at, total = 0, None
    for piece in pieces:
        size = piece.shape[0]
        term = dot32(rows[:, at : at + size], piece[...])
        total = term if total is None else total + term
        at += size
    return total


def lanes_at(rows, index_row):
    lanes = 128
    count, width = rows.shape
    parts = [rows[:, at : at + lanes] for at in range(0, width, lanes)]
    outs = []
    for at in range(0, width, lanes):
        index = jnp.broadcast_to(index_row[:, at : at + lanes].astype(jnp.int32), (count, lanes))
        lane, part = index % lanes, index // lanes
        total = jnp.zeros((count, lanes), rows.dtype)
        for k, values in enumerate(parts):
            total = jnp.where(part == k, jnp.take_along_axis(values, lane, axis=1), total)
        outs.append(total)
    return jnp.concatenate(outs, axis=1)


def segment_kernel(coupling, pieces_of, down_steps, up_steps, active, *refs):
    @pl.when(active[0] == 1)
    def _():
        run_segment(coupling, pieces_of, down_steps, up_steps, *refs)


def run_segment(coupling, pieces_of, down_steps, up_steps, *refs):
    refs = list(refs)
    state = refs.pop(0)[...]
    maps, downs = {}, {}
    operands = []
    for slot in down_steps:
        operands.append(refs.pop(0))
        maps[slot] = [refs.pop(0) for _ in range(pieces_of[slot])]
    for slot in up_steps:
        if slot not in down_steps:
            downs[slot] = refs.pop(0)[...]
            maps[slot] = [refs.pop(0) for _ in range(pieces_of[slot])]
    for slot, packed in zip(down_steps, operands):
        count = state.shape[0]
        moved = lanes_at(state.astype(jnp.float32), packed[count:]).astype(jnp.bfloat16)
        downs[slot] = packed[:count] + coupling * spread(maps[slot], moved)
        state = downs[slot].astype(jnp.bfloat16)
        refs.pop(0)[...] = downs[slot]
    for slot in up_steps:
        value = downs[slot] + coupling * gather_sum(maps[slot], state)
        state = value.astype(jnp.bfloat16)
        refs.pop(0)[...] = value
    refs.pop(0)[...] = state


def segment(coupling, active, arrived, packed, downs, maps, down_steps, up_steps):
    operands = [active.astype(jnp.int32)[None], arrived]
    for slot in down_steps:
        operands += [packed[slot], *maps[slot]]
    for slot in up_steps:
        if slot not in down_steps:
            operands += [downs[slot], *maps[slot]]
    rows = jax.ShapeDtypeStruct(arrived.shape, jnp.float32)
    steps = len(down_steps) + len(up_steps)
    results = pl.pallas_call(
        functools.partial(
            segment_kernel, coupling, [len(entry) for entry in maps], down_steps, up_steps
        ),
        out_shape=[rows] * steps + [jax.ShapeDtypeStruct(arrived.shape, jnp.bfloat16)],
        in_specs=[SMEM] + [VMEM] * (len(operands) - 1),
        out_specs=[VMEM] * (steps + 1),
        compiler_params=SWEEP_PARAMS,
        cost_estimate=cost(steps * 2 * 256 * 1024 * 1024, steps * 2 * 1024 * 1024),
    )(*operands)
    return results[:-1], results[-1]


def last_kernel(coupling, count, odd, from_pair, from_own, source, down_odd, *refs):
    own, pair, out = refs[:count], refs[count : 2 * count], refs[2 * count]
    total = gather_sum(pair, from_pair[...]) + gather_sum(own, from_own[...])
    up_odd = down_odd[...] + coupling * total
    up_even = source[...] + coupling * gather_sum(own, up_odd.astype(jnp.bfloat16))
    out[...] = jnp.where(odd[0] == 1, up_odd, up_even)


def on_device(box_maps, block_pattern, face_inverses, index_map, sources):
    boxes = lax.axis_size("box")
    layers = lax.axis_size("layer")
    coupling = float(boxes) ** 0.5
    levels = boxes.bit_length() - 1
    face = face_inverses.shape[2]
    width = box_maps.shape[2]
    rows_here = sources.shape[1]
    position = lax.axis_index("box")
    layer = lax.axis_index("layer")
    is_second = position % 2 == 1
    second_flag = is_second.astype(jnp.int32)[None]

    chain = [(layer_at, (OWN, PAIR)) for layer_at in range(2, layers, 2)]
    pair_moves = [(layer_at + 1, layer_at) for layer_at in range(0, layers, 2)]

    def route(moves, source_core=1, target_core=1):
        return [
            (a * boxes + b + source_core, z * boxes + b + target_core)
            for a, z in moves
            for b in range(0, boxes, 2)
        ]

    def over_box(change, starts):
        return [(i * boxes + b, i * boxes + (b ^ change)) for i in range(layers) for b in starts]

    def send(value, pairs_of_devices):
        return lax.ppermute(value, AXES, pairs_of_devices)

    def after(value, *others):
        return lax.optimization_barrier((value, *others))[0]

    every = [(i, i) for i in range(layers)]

    raw = box_maps[0]
    pattern = block_pattern[0]
    raw_other = send(raw, over_box(1, range(boxes)))
    pattern_other = send(pattern, over_box(1, range(boxes)))
    first_sources = send(sources[0], route(every, 0, 1))
    own_half = pl.pallas_call(
        mask_kernel,
        out_shape=jax.ShapeDtypeStruct(raw.shape, jnp.bfloat16),
        in_specs=[SMEM, VMEM],
        out_specs=VMEM,
        compiler_params=PARAMS,
        cost_estimate=cost(width * width, 4 * width * width),
    )(pattern, raw)

    def inverse_of(level):
        node = (boxes >> (level + 1)) - 1 + (position >> (level + 1))
        return lax.dynamic_index_in_dim(face_inverses[0], node, 0, keepdims=False).astype(
            jnp.bfloat16
        )

    rows = -(-2 * rows_here // 8) * 8
    packed = jnp.concatenate(
        [
            first_sources,
            sources[0],
            jnp.zeros((rows - 2 * rows_here, width), jnp.float32),
            index_map.astype(jnp.float32),
        ],
        axis=0,
    )

    pieces = tuple((at, face) for at in range(0, width, face))
    current = dict(
        zip(pieces, leaf_combine(pattern_other, own_half, raw_other, inverse_of(0)))
    )

    for level in range(1, levels):
        final = level == levels - 1
        change = 1 << level
        inverse = inverse_of(level)
        near = (level * face, (level ^ 1) * face)
        order = [(at, face) for at in near] + [piece for piece in pieces if piece[0] not in near]
        received = {}
        right = None
        if not final:
            for piece in order:
                received[piece] = send(current[piece], over_box(change, range(boxes)))
            renewed = {}
            for piece in order:
                renewed[piece], right = combine(
                    second_flag,
                    current[piece],
                    received[piece],
                    inverse,
                    None,
                    right,
                    level * face,
                )
            current = renewed
            continue
        over = over_box(change ^ 1, range(0, boxes, 2))
        evens = [(target, target) for _, target in pair_moves]
        for piece in order[:AHEAD]:
            received[piece] = send(current[piece], over)
        pair_pieces = []
        own_pieces = []
        rest = None
        for k, piece in enumerate(order):
            following = order[k + AHEAD] if k + AHEAD < len(order) else None
            other = received[piece]
            if k == SMALL_AT + 2:
                other = after(other, pair_packed)
            if k == len(order) - 1:
                other = after(other, pair_pieces[0][1])
            payload, right = combine(
                second_flag,
                current[piece],
                other,
                inverse,
                None if following is None else current[following],
                right,
                level * face,
                rest,
            )
            if following is None:
                rest = payload
            else:
                received[following] = send(payload, route(pair_moves, 1, 0) + over)
                pair_pieces.append((piece[0], send(received[following], route(evens, 0, 1))))
                own_pieces.append((piece[0], payload))
            if k == SMALL_AT:
                sendable = after(packed, payload)
                pair_packed = send(sendable, route(pair_moves[1:] + [(0, 1)]))
    rest_at = order[AHEAD][0]
    own_pieces.append((rest_at, rest))
    pair_pieces.append((rest_at, send(rest, route(pair_moves))))
    own_maps, pair_maps = [
        [value for _, value in sorted(entries, key=lambda entry: entry[0])]
        for entries in (own_pieces, pair_pieces)
    ]
    merged = assemble(own_maps)
    small = [packed, pair_packed]

    maps = [own_maps, pair_maps]
    first = after(pair_packed[:rows].astype(jnp.bfloat16), merged)
    (down_odd,), state = segment(
        coupling, is_second & (layer == 1), first, small, {}, maps, (OWN,), ()
    )
    at = 1
    kept = []
    ups = {}
    for k, (target, slots) in enumerate(chain):
        arrived = send(state, route([(at, target)]))
        at = target
        turn = k == len(chain) - 1
        back = tuple(reversed(slots))
        results, state = segment(
            coupling,
            is_second & (layer == at),
            arrived,
            small,
            {},
            maps,
            slots,
            back[1:] if turn else (),
        )
        kept.append(dict(zip(slots, results)))
        if k == 0:
            down_odd_pair = send(after(down_odd, state), route([(1, 0)]))
            merged_first = send(after(merged, state), route(every, 1, 0))
        if turn:
            ups[at] = dict(zip(back[1:], results[len(slots) :]))
            ups[at][back[0]] = results[len(slots) - 1]
    result = jnp.where(is_second, merged, after(merged_first, state))
    down_odd = jnp.where(layer == 0, down_odd_pair, down_odd)

    for k in reversed(range(len(chain) - 1)):
        target, slots = chain[k]
        arrived = send(state, route([(at, target)]))
        at = target
        back = tuple(reversed(slots))
        results, state = segment(
            coupling, is_second & (layer == at), arrived, small, kept[k], maps, (), back
        )
        ups[at] = dict(zip(back, results))
    from_own = send(state, route([(at, 1)]))
    from_pair = send(state, route([(at, 0)]))

    mine = [jnp.zeros((rows, width), jnp.float32)] * 2
    for target, values in ups.items():
        for slot in (OWN, PAIR):
            mine[slot] = jnp.where(layer == target, values[slot], mine[slot])
    settled = mine[OWN] + send(mine[PAIR], route([(z, a) for a, z in pair_moves[1:]]))

    odd = (layer % 2).astype(jnp.int32)[None]
    last = pl.pallas_call(
        functools.partial(last_kernel, coupling, len(pair_maps)),
        out_shape=jax.ShapeDtypeStruct((rows, width), jnp.float32),
        in_specs=[SMEM] + [VMEM] * (4 + 2 * len(pair_maps)),
        out_specs=VMEM,
        compiler_params=SWEEP_PARAMS,
        cost_estimate=cost(6 * 256 * 1024 * 1024, 6 * 1024 * 1024),
    )(odd, from_pair, from_own, packed[:rows], down_odd, *own_maps, *pair_maps)
    upward = jnp.where(layer < 2, last, settled)
    first_rows = send(upward[:rows_here], route(every, 1, 0))
    upward = jnp.where(is_second, upward[rows_here : 2 * rows_here], first_rows)
    return (result[None], upward[None])


def solution(mesh):
    return jax.shard_map(
        on_device,
        mesh=mesh,
        in_specs=(
            P("layer", "box", None),
            P("layer", "box", None),
            P("layer", None, None, None),
            P("layer", None),
            P("layer", "box", None),
        ),
        out_specs=(P("layer", None, None), P("layer", "box", None)),
        check_vma=False,
    )
```

```python
import functools

import jax
import jax.numpy as jnp
from jax import lax
from jax.experimental import pallas as pl
from jax.experimental.pallas import tpu as pltpu
from jax.sharding import PartitionSpec as P

AXES = ("layer", "box")
AHEAD = 2
SMALL_AT = 0
VMEM = pl.BlockSpec(memory_space=pltpu.VMEM)
SMEM = pl.BlockSpec(memory_space=pltpu.SMEM)
PARAMS = pltpu.CompilerParams(vmem_limit_bytes=24 * 1024 * 1024)
SWEEP_PARAMS = pltpu.CompilerParams(vmem_limit_bytes=10 * 1024 * 1024)
OWN, PAIR = 0, 1


def cost(flops, moved):
    return pl.CostEstimate(flops=flops, bytes_accessed=moved, transcendentals=0)


def dot32(a, b):
    return jnp.dot(a, b, preferred_element_type=jnp.float32)


def dot32_t(a, b):
    return lax.dot_general(a, b, (((1,), (1,)), ((), ())), preferred_element_type=jnp.float32)


def minus_face(joined, face_at, inverse, right):
    face = inverse.shape[0]
    left = joined[:, face_at : face_at + face].astype(jnp.bfloat16)
    product = dot32(left, inverse).astype(jnp.bfloat16)
    return (joined - dot32(product, right)).astype(jnp.bfloat16)


def masked(values, pattern, row_at, row_count, block_at):
    width = values.shape[1]
    block = width // pattern.shape[1]
    strips = []
    for r in range(row_count // block):
        at = slice(row_at + r * block, row_at + (r + 1) * block)
        strips.append(
            jnp.concatenate(
                [
                    values[at, c * block : (c + 1) * block].astype(jnp.float32)
                    * (0.5 * pattern[block_at + r, c].astype(jnp.float32))
                    for c in range(width // block)
                ],
                axis=1,
            )
        )
    return jnp.concatenate(strips, axis=0)


def mask_kernel(pattern, values, out):
    block = values.shape[1] // pattern.shape[1]
    for r in range(values.shape[0] // block):
        out[r * block : (r + 1) * block] = masked(values, pattern, r * block, block, r).astype(
            jnp.bfloat16
        )


def leaf_kernel(first_row, is_face, pieces, other_pattern, own, other, inverse, *refs):
    refs = list(refs)
    face = inverse.shape[0]
    right = None if is_face else refs.pop(0)[...]
    block = own.shape[1] // other_pattern.shape[1]
    for i in range(own.shape[0] // face):
        at = first_row + i * face
        joined = own[i * face : (i + 1) * face].astype(jnp.float32) + masked(
            other, other_pattern, i * face, face, at // block
        )
        if right is None:
            right = joined.astype(jnp.bfloat16)
            refs[-1][...] = right
        result = minus_face(joined, 0, inverse[...], right)
        for ref, (start, size) in zip(refs, pieces):
            low, high = max(start, at), min(start + size, at + face)
            if low < high:
                ref[low - start : high - start] = result[low - at : high - at]


def leaf_combine(other_pattern, own, other, inverse, face_rows, half, pieces):
    is_face = face_rows is None
    width = own.shape[1]
    rows = own.shape[0] // 2
    face = inverse.shape[0]
    shapes = [jax.ShapeDtypeStruct((size, width), jnp.bfloat16) for _, size in pieces]
    if is_face:
        shapes.append(jax.ShapeDtypeStruct((face, width), jnp.bfloat16))
    map_spec = pl.BlockSpec((rows, width), lambda i: (half, 0))
    extra = [] if is_face else [face_rows]
    return pl.pallas_call(
        functools.partial(leaf_kernel, half * rows, is_face, pieces),
        grid=(1,),
        out_shape=shapes,
        in_specs=[SMEM, map_spec, map_spec, VMEM] + [VMEM] * len(extra),
        out_specs=[VMEM] * len(shapes),
        compiler_params=PARAMS,
        cost_estimate=cost(0, 8 * rows * width),
    )(other_pattern, own, other, inverse, *extra)


def combine_kernel(face_at, is_face, with_next, whole_rows, is_second, own, other, inverse, *refs):
    refs = list(refs)
    following = refs.pop(0) if with_next else None
    joined = 0.5 * (own[...].astype(jnp.float32) + other[...].astype(jnp.float32))
    if is_face:
        right = joined.astype(jnp.bfloat16)
    else:
        right = refs.pop(0)[...]
        refs.pop(0)
    piece = minus_face(joined, face_at, inverse[...], right)
    refs[1][whole_rows, :] = piece
    if is_face:
        refs[2][...] = right
    refs[0][...] = piece
    if with_next:

        @pl.when(is_second[0] == 0)
        def _():
            refs[0][...] = following[...]


def combine(is_second, own, other, inverse, following, state, face_at, row_at):
    is_face = state is None
    rows, width = own.shape
    extra = [] if following is None else [following]
    aliases = {} if is_face else {4 + len(extra) + 1: 1}
    extra += [] if is_face else list(state)
    piece = jax.ShapeDtypeStruct((rows, width), jnp.bfloat16)
    whole = jax.ShapeDtypeStruct((width, width), jnp.bfloat16)
    result = pl.pallas_call(
        functools.partial(
            combine_kernel,
            face_at,
            is_face,
            following is not None,
            slice(row_at, row_at + rows),
        ),
        out_shape=[piece, whole] + ([piece] if is_face else []),
        in_specs=[SMEM] + [VMEM] * (3 + len(extra)),
        out_specs=[VMEM] * (3 if is_face else 2),
        input_output_aliases=aliases,
        compiler_params=PARAMS,
        cost_estimate=cost(0, 8 * rows * width),
    )(is_second, own, other, inverse, *extra)
    return result[0], ((result[2] if is_face else state[0]), result[1])


def spread(pieces, rows):
    return jnp.concatenate([dot32_t(rows, piece[...]) for piece in pieces], axis=1)


def gather_sum(pieces, rows):
    at, total = 0, None
    for piece in pieces:
        size = piece.shape[0]
        term = dot32(rows[:, at : at + size], piece[...])
        total = term if total is None else total + term
        at += size
    return total


def lanes_at(rows, index_row):
    lanes = 128
    count, width = rows.shape
    parts = [rows[:, at : at + lanes] for at in range(0, width, lanes)]
    outs = []
    for at in range(0, width, lanes):
        index = jnp.broadcast_to(index_row[:, at : at + lanes].astype(jnp.int32), (count, lanes))
        lane, part = index % lanes, index // lanes
        total = jnp.zeros((count, lanes), rows.dtype)
        for k, values in enumerate(parts):
            total = jnp.where(part == k, jnp.take_along_axis(values, lane, axis=1), total)
        outs.append(total)
    return jnp.concatenate(outs, axis=1)


def segment_kernel(coupling, pieces_of, down_steps, up_steps, active, *refs):
    @pl.when(active[0] == 1)
    def _():
        run_segment(coupling, pieces_of, down_steps, up_steps, *refs)


def run_segment(coupling, pieces_of, down_steps, up_steps, *refs):
    refs = list(refs)
    state = refs.pop(0)[...]
    maps, downs = {}, {}
    operands = []
    for slot in down_steps:
        operands.append(refs.pop(0))
        maps[slot] = [refs.pop(0) for _ in range(pieces_of[slot])]
    for slot in up_steps:
        if slot not in down_steps:
            downs[slot] = refs.pop(0)[...]
            maps[slot] = [refs.pop(0) for _ in range(pieces_of[slot])]
    for slot, packed in zip(down_steps, operands):
        count = state.shape[0]
        moved = lanes_at(state.astype(jnp.float32), packed[count:]).astype(jnp.bfloat16)
        downs[slot] = packed[:count] + coupling * spread(maps[slot], moved)
        state = downs[slot].astype(jnp.bfloat16)
        refs.pop(0)[...] = downs[slot]
    for slot in up_steps:
        value = downs[slot] + coupling * gather_sum(maps[slot], state)
        state = value.astype(jnp.bfloat16)
        refs.pop(0)[...] = value
    refs.pop(0)[...] = state


def segment(coupling, active, arrived, packed, downs, maps, down_steps, up_steps):
    operands = [active.astype(jnp.int32)[None], arrived]
    for slot in down_steps:
        operands += [packed[slot], *maps[slot]]
    for slot in up_steps:
        if slot not in down_steps:
            operands += [downs[slot], *maps[slot]]
    rows = jax.ShapeDtypeStruct(arrived.shape, jnp.float32)
    steps = len(down_steps) + len(up_steps)
    results = pl.pallas_call(
        functools.partial(
            segment_kernel, coupling, [len(entry) for entry in maps], down_steps, up_steps
        ),
        out_shape=[rows] * steps + [jax.ShapeDtypeStruct(arrived.shape, jnp.bfloat16)],
        in_specs=[SMEM] + [VMEM] * (len(operands) - 1),
        out_specs=[VMEM] * (steps + 1),
        compiler_params=SWEEP_PARAMS,
        cost_estimate=cost(0, steps * 4 * 1024 * 1024),
    )(*operands)
    return results[:-1], results[-1]


def last_kernel(coupling, count, odd, from_pair, from_own, source, down_odd, *refs):
    own, pair, out = refs[:1], refs[1 : 1 + count], refs[1 + count]
    total = gather_sum(pair, from_pair[...]) + gather_sum(own, from_own[...])
    up_odd = down_odd[...] + coupling * total
    up_even = source[...] + coupling * gather_sum(own, up_odd.astype(jnp.bfloat16))
    out[...] = jnp.where(odd[0] == 1, up_odd, up_even)


def on_device(box_maps, block_pattern, face_inverses, index_map, sources):
    boxes = lax.axis_size("box")
    layers = lax.axis_size("layer")
    coupling = float(boxes) ** 0.5
    levels = boxes.bit_length() - 1
    face = face_inverses.shape[2]
    width = box_maps.shape[2]
    rows_here = sources.shape[1]
    position = lax.axis_index("box")
    layer = lax.axis_index("layer")
    is_second = position % 2 == 1
    second_flag = is_second.astype(jnp.int32)[None]

    chain = [(layer_at, (OWN, PAIR)) for layer_at in range(2, layers, 2)]
    pair_moves = [(layer_at + 1, layer_at) for layer_at in range(0, layers, 2)]

    def route(moves, source_core=0, target_core=0):
        return [
            (a * boxes + b + source_core, z * boxes + b + target_core)
            for a, z in moves
            for b in range(0, boxes, 2)
        ]

    def over_box(change, starts):
        return [(i * boxes + b, i * boxes + (b ^ change)) for i in range(layers) for b in starts]

    def send(value, pairs_of_devices):
        return lax.ppermute(value, AXES, pairs_of_devices)

    def after(value, *others):
        return lax.optimization_barrier((value, *others))[0]

    every = [(i, i) for i in range(layers)]

    raw = box_maps[0]
    pattern = block_pattern[0]
    raw_other = send(raw, over_box(1, range(boxes)))
    pattern_other = send(pattern, over_box(1, range(boxes)))
    other_sources = send(sources[0], over_box(1, range(boxes)))
    own_half = pl.pallas_call(
        mask_kernel,
        out_shape=jax.ShapeDtypeStruct(raw.shape, jnp.bfloat16),
        in_specs=[SMEM, VMEM],
        out_specs=VMEM,
        compiler_params=PARAMS,
        cost_estimate=cost(0, 4 * width * width),
    )(pattern, raw)

    def inverse_of(level):
        node = (boxes >> (level + 1)) - 1 + (position >> (level + 1))
        return lax.dynamic_index_in_dim(face_inverses[0], node, 0, keepdims=False).astype(
            jnp.bfloat16
        )

    rows = -(-2 * rows_here // 8) * 8
    packed = jnp.concatenate(
        [
            jnp.where(is_second, other_sources, sources[0]),
            jnp.where(is_second, sources[0], other_sources),
            jnp.zeros((rows - 2 * rows_here, width), jnp.float32),
            index_map.astype(jnp.float32),
        ],
        axis=0,
    )

    pieces = tuple((at, face) for at in range(0, width, face))
    upper = tuple(piece for piece in pieces if piece[0] < width // 2)
    lower = tuple(piece for piece in pieces if piece[0] >= width // 2)
    inverse = inverse_of(0)
    top = leaf_combine(pattern_other, own_half, raw_other, inverse, None, 0, upper)
    bottom = leaf_combine(pattern_other, own_half, raw_other, inverse, top[-1], 1, lower)
    current = dict(zip(upper + lower, [*top[:-1], *bottom]))

    for level in range(1, levels):
        final = level == levels - 1
        change = 1 << level
        inverse = inverse_of(level)
        order = sorted(pieces, key=lambda piece: (piece[0] != level * face, piece[0]))
        received = {}
        state = None
        if not final:
            for piece in order:
                received[piece] = send(current[piece], over_box(change, range(boxes)))
            renewed = {}
            for piece in order:
                renewed[piece], state = combine(
                    second_flag,
                    current[piece],
                    received[piece],
                    inverse,
                    None,
                    state,
                    level * face,
                    piece[0],
                )
            current = renewed
            continue
        over = over_box(change ^ 1, range(0, boxes, 2))
        forward = route(pair_moves, 1, 0)
        for piece in order[:AHEAD]:
            received[piece] = send(current[piece], over)
        pair_pieces = {}
        for k, piece in enumerate(order):
            following = order[k + AHEAD] if k + AHEAD < len(order) else None
            other = received[piece]
            if k == SMALL_AT + 2:
                other = after(other, pair_packed)
            if k > AHEAD:
                other = after(other, pair_pieces[order[k - 1]])
            payload, state = combine(
                second_flag,
                current[piece],
                other,
                inverse,
                None if following is None else current[following],
                state,
                level * face,
                piece[0],
            )
            pair_pieces[piece] = send(payload, forward + ([] if following is None else over))
            if following is not None:
                received[following] = pair_pieces[piece]
            if k == SMALL_AT:
                sendable = after(packed, payload)
                pair_packed = send(sendable, route(pair_moves[1:]) + route([(0, 1)], 1, 1))
    merged = state[1]
    small = [packed, pair_packed]
    pair_maps = [pair_pieces[piece] for piece in pieces]

    first = pair_packed[:rows].astype(jnp.bfloat16)
    (down_odd,), state = segment(
        coupling, is_second & (layer == 1), first, small, {}, [[merged], pair_maps], (OWN,), ()
    )
    merged_first = send(after(merged, state), route(every, 1, 0))
    maps = [[merged_first], pair_maps]
    at, core = 1, 1
    kept = []
    ups = {}
    for k, (target, slots) in enumerate(chain):
        arrived = send(state, route([(at, target)], core, 0))
        at, core = target, 0
        turn = k == len(chain) - 1
        back = tuple(reversed(slots))
        results, state = segment(
            coupling, layer == at, arrived, small, {}, maps, slots, back[1:] if turn else ()
        )
        kept.append(dict(zip(slots, results)))
        if k == 0:
            down_odd_first = send(after(down_odd, state), route([(1, 0)], 1, 0))
        if turn:
            ups[at] = dict(zip(back[1:], results[len(slots) :]))
            ups[at][back[0]] = results[len(slots) - 1]
    merged = jnp.where(is_second, merged, merged_first)
    down_odd = jnp.where(layer == 0, down_odd_first, down_odd)

    for k in reversed(range(len(chain) - 1)):
        target, slots = chain[k]
        arrived = send(state, route([(at, target)]))
        if k == len(chain) - 2:
            arrived, merged = lax.optimization_barrier((arrived, merged))
        at = target
        back = tuple(reversed(slots))
        results, state = segment(coupling, layer == at, arrived, small, kept[k], maps, (), back)
        ups[at] = dict(zip(back, results))
    from_own = send(state, route([(at, 1)], 0, 1))
    from_pair = send(state, route([(at, 0)]))

    mine = [jnp.zeros((rows, width), jnp.float32)] * 2
    for target, values in ups.items():
        for slot in (OWN, PAIR):
            mine[slot] = jnp.where(layer == target, values[slot], mine[slot])
    settled = mine[OWN] + send(mine[PAIR], route([(z, a) for a, z in pair_moves[1:]]))

    odd = (layer % 2).astype(jnp.int32)[None]
    last = pl.pallas_call(
        functools.partial(last_kernel, coupling, len(pair_maps)),
        out_shape=jax.ShapeDtypeStruct((rows, width), jnp.float32),
        in_specs=[SMEM] + [VMEM] * (5 + len(pair_maps)),
        out_specs=VMEM,
        compiler_params=SWEEP_PARAMS,
        cost_estimate=cost(0, 8 * 1024 * 1024),
    )(odd, from_pair, from_own, packed[:rows], down_odd, merged, *pair_maps)
    upward = jnp.where(layer < 2, last, settled)
    ends = upward[:rows_here], upward[rows_here : 2 * rows_here]
    there = send(
        jnp.where(is_second, ends[0], ends[1]),
        route([(1, 1)], 1, 0) + route([move for move in every if move[0] != 1], 0, 1),
    )
    here = jnp.where(is_second, ends[1], ends[0])
    runs = jnp.logical_xor(is_second, layer != 1)
    return (merged[None], jnp.where(runs, here, there)[None])


def solution(mesh):
    return jax.shard_map(
        on_device,
        mesh=mesh,
        in_specs=(
            P("layer", "box", None),
            P("layer", "box", None),
            P("layer", None, None, None),
            P("layer", None),
            P("layer", "box", None),
        ),
        out_specs=(P("layer", None, None), P("layer", "box", None)),
        check_vma=False,
    )
```

```python
import functools

import jax
import jax.numpy as jnp
from jax import lax
from jax.experimental import pallas as pl
from jax.experimental.pallas import tpu as pltpu
from jax.sharding import PartitionSpec as P

AXES = ("layer", "box")
AHEAD = 2
SMALL_AT = 0
VMEM = pl.BlockSpec(memory_space=pltpu.VMEM)
SMEM = pl.BlockSpec(memory_space=pltpu.SMEM)
PARAMS = pltpu.CompilerParams(vmem_limit_bytes=24 * 1024 * 1024)
SWEEP_PARAMS = pltpu.CompilerParams(vmem_limit_bytes=10 * 1024 * 1024)
OWN, PAIR = 0, 1


def cost(flops, moved):
    return pl.CostEstimate(flops=flops, bytes_accessed=moved, transcendentals=0)


def dot32(a, b):
    return jnp.dot(a, b, preferred_element_type=jnp.float32)


def dot32_t(a, b):
    return lax.dot_general(a, b, (((1,), (1,)), ((), ())), preferred_element_type=jnp.float32)


def minus_face(joined, face_at, inverse, right):
    face = inverse.shape[0]
    left = joined[:, face_at : face_at + face].astype(jnp.bfloat16)
    product = dot32(left, inverse).astype(jnp.bfloat16)
    return (joined - dot32(product, right)).astype(jnp.bfloat16)


def masked(values, pattern, row_at, row_count, block_at):
    width = values.shape[1]
    block = width // pattern.shape[1]
    strips = []
    for r in range(row_count // block):
        at = slice(row_at + r * block, row_at + (r + 1) * block)
        strips.append(
            jnp.concatenate(
                [
                    values[at, c * block : (c + 1) * block].astype(jnp.float32)
                    * (0.5 * pattern[block_at + r, c].astype(jnp.float32))
                    for c in range(width // block)
                ],
                axis=1,
            )
        )
    return jnp.concatenate(strips, axis=0)


def mask_kernel(pattern, values, out):
    block = values.shape[1] // pattern.shape[1]
    for r in range(values.shape[0] // block):
        out[r * block : (r + 1) * block] = masked(values, pattern, r * block, block, r).astype(
            jnp.bfloat16
        )


def leaf_kernel(first_row, is_face, pieces, other_pattern, own, other, inverse, *refs):
    refs = list(refs)
    face = inverse.shape[0]
    right = None if is_face else refs.pop(0)[...]
    block = own.shape[1] // other_pattern.shape[1]
    for i in range(own.shape[0] // face):
        at = first_row + i * face
        joined = own[i * face : (i + 1) * face].astype(jnp.float32) + masked(
            other, other_pattern, i * face, face, at // block
        )
        if right is None:
            right = joined.astype(jnp.bfloat16)
            refs[-1][...] = right
        result = minus_face(joined, 0, inverse[...], right)
        for ref, (start, size) in zip(refs, pieces):
            low, high = max(start, at), min(start + size, at + face)
            if low < high:
                ref[low - start : high - start] = result[low - at : high - at]


def leaf_combine(other_pattern, own, other, inverse, face_rows, half, pieces):
    is_face = face_rows is None
    width = own.shape[1]
    rows = own.shape[0] // 2
    face = inverse.shape[0]
    shapes = [jax.ShapeDtypeStruct((size, width), jnp.bfloat16) for _, size in pieces]
    if is_face:
        shapes.append(jax.ShapeDtypeStruct((face, width), jnp.bfloat16))
    map_spec = pl.BlockSpec((rows, width), lambda i: (half, 0))
    extra = [] if is_face else [face_rows]
    return pl.pallas_call(
        functools.partial(leaf_kernel, half * rows, is_face, pieces),
        grid=(1,),
        out_shape=shapes,
        in_specs=[SMEM, map_spec, map_spec, VMEM] + [VMEM] * len(extra),
        out_specs=[VMEM] * len(shapes),
        compiler_params=PARAMS,
        cost_estimate=cost(2 * rows * face * (width + face), 6 * rows * width),
    )(other_pattern, own, other, inverse, *extra)


def combine_kernel(face_at, is_face, with_next, whole_rows, is_second, own, other, inverse, *refs):
    refs = list(refs)
    following = refs.pop(0) if with_next else None
    joined = 0.5 * (own[...].astype(jnp.float32) + other[...].astype(jnp.float32))
    if is_face:
        right = joined.astype(jnp.bfloat16)
    else:
        right = refs.pop(0)[...]
        refs.pop(0)
    piece = minus_face(joined, face_at, inverse[...], right)
    refs[1][whole_rows, :] = piece
    if is_face:
        refs[2][...] = right
    refs[0][...] = piece
    if with_next:

        @pl.when(is_second[0] == 0)
        def _():
            refs[0][...] = following[...]


def combine(is_second, own, other, inverse, following, state, face_at, row_at):
    is_face = state is None
    rows, width = own.shape
    extra = [] if following is None else [following]
    aliases = {} if is_face else {4 + len(extra) + 1: 1}
    extra += [] if is_face else list(state)
    piece = jax.ShapeDtypeStruct((rows, width), jnp.bfloat16)
    whole = jax.ShapeDtypeStruct((width, width), jnp.bfloat16)
    result = pl.pallas_call(
        functools.partial(
            combine_kernel,
            face_at,
            is_face,
            following is not None,
            slice(row_at, row_at + rows),
        ),
        out_shape=[piece, whole] + ([piece] if is_face else []),
        in_specs=[SMEM] + [VMEM] * (3 + len(extra)),
        out_specs=[VMEM] * (3 if is_face else 2),
        input_output_aliases=aliases,
        compiler_params=PARAMS,
        cost_estimate=cost(
            2 * rows * inverse.shape[0] * (width + inverse.shape[0]), 6 * rows * width
        ),
    )(is_second, own, other, inverse, *extra)
    return result[0], ((result[2] if is_face else state[0]), result[1])


def spread(pieces, rows):
    return jnp.concatenate([dot32_t(rows, piece[...]) for piece in pieces], axis=1)


def gather_sum(pieces, rows):
    at, total = 0, None
    for piece in pieces:
        size = piece.shape[0]
        term = dot32(rows[:, at : at + size], piece[...])
        total = term if total is None else total + term
        at += size
    return total


def lanes_at(rows, index_row):
    lanes = 128
    count, width = rows.shape
    parts = [rows[:, at : at + lanes] for at in range(0, width, lanes)]
    outs = []
    for at in range(0, width, lanes):
        index = jnp.broadcast_to(index_row[:, at : at + lanes].astype(jnp.int32), (count, lanes))
        lane, part = index % lanes, index // lanes
        total = jnp.zeros((count, lanes), rows.dtype)
        for k, values in enumerate(parts):
            total = jnp.where(part == k, jnp.take_along_axis(values, lane, axis=1), total)
        outs.append(total)
    return jnp.concatenate(outs, axis=1)


def segment_kernel(coupling, pieces_of, down_steps, up_steps, active, *refs):
    @pl.when(active[0] == 1)
    def _():
        run_segment(coupling, pieces_of, down_steps, up_steps, *refs)


def run_segment(coupling, pieces_of, down_steps, up_steps, *refs):
    refs = list(refs)
    state = refs.pop(0)[...]
    maps, downs = {}, {}
    operands = []
    for slot in down_steps:
        operands.append(refs.pop(0))
        maps[slot] = [refs.pop(0) for _ in range(pieces_of[slot])]
    for slot in up_steps:
        if slot not in down_steps:
            downs[slot] = refs.pop(0)[...]
            maps[slot] = [refs.pop(0) for _ in range(pieces_of[slot])]
    for slot, packed in zip(down_steps, operands):
        count = state.shape[0]
        moved = lanes_at(state.astype(jnp.float32), packed[count:]).astype(jnp.bfloat16)
        downs[slot] = packed[:count] + coupling * spread(maps[slot], moved)
        state = downs[slot].astype(jnp.bfloat16)
        refs.pop(0)[...] = downs[slot]
    for slot in up_steps:
        value = downs[slot] + coupling * gather_sum(maps[slot], state)
        state = value.astype(jnp.bfloat16)
        refs.pop(0)[...] = value
    refs.pop(0)[...] = state


def segment(coupling, active, arrived, packed, downs, maps, down_steps, up_steps):
    operands = [active.astype(jnp.int32)[None], arrived]
    for slot in down_steps:
        operands += [packed[slot], *maps[slot]]
    for slot in up_steps:
        if slot not in down_steps:
            operands += [downs[slot], *maps[slot]]
    rows = jax.ShapeDtypeStruct(arrived.shape, jnp.float32)
    steps = len(down_steps) + len(up_steps)
    results = pl.pallas_call(
        functools.partial(
            segment_kernel, coupling, [len(entry) for entry in maps], down_steps, up_steps
        ),
        out_shape=[rows] * steps + [jax.ShapeDtypeStruct(arrived.shape, jnp.bfloat16)],
        in_specs=[SMEM] + [VMEM] * (len(operands) - 1),
        out_specs=[VMEM] * (steps + 1),
        compiler_params=SWEEP_PARAMS,
        cost_estimate=cost(steps * 2 * 256 * 1024 * 1024, steps * 2 * 1024 * 1024),
    )(*operands)
    return results[:-1], results[-1]


def last_kernel(coupling, count, odd, from_pair, from_own, source, down_odd, *refs):
    own, pair, out = refs[:1], refs[1 : 1 + count], refs[1 + count]
    total = gather_sum(pair, from_pair[...]) + gather_sum(own, from_own[...])
    up_odd = down_odd[...] + coupling * total
    up_even = source[...] + coupling * gather_sum(own, up_odd.astype(jnp.bfloat16))
    out[...] = jnp.where(odd[0] == 1, up_odd, up_even)


def on_device(box_maps, block_pattern, face_inverses, index_map, sources):
    boxes = lax.axis_size("box")
    layers = lax.axis_size("layer")
    coupling = float(boxes) ** 0.5
    levels = boxes.bit_length() - 1
    face = face_inverses.shape[2]
    width = box_maps.shape[2]
    rows_here = sources.shape[1]
    position = lax.axis_index("box")
    layer = lax.axis_index("layer")
    is_second = position % 2 == 1
    second_flag = is_second.astype(jnp.int32)[None]

    chain = [(layer_at, (OWN, PAIR)) for layer_at in range(2, layers, 2)]
    pair_moves = [(layer_at + 1, layer_at) for layer_at in range(0, layers, 2)]

    def route(moves, source_core=0, target_core=0):
        return [
            (a * boxes + b + source_core, z * boxes + b + target_core)
            for a, z in moves
            for b in range(0, boxes, 2)
        ]

    def over_box(change, starts):
        return [(i * boxes + b, i * boxes + (b ^ change)) for i in range(layers) for b in starts]

    def send(value, pairs_of_devices):
        return lax.ppermute(value, AXES, pairs_of_devices)

    def after(value, *others):
        return lax.optimization_barrier((value, *others))[0]

    every = [(i, i) for i in range(layers)]

    raw = box_maps[0]
    pattern = block_pattern[0]
    raw_other = send(raw, over_box(1, range(boxes)))
    pattern_other = send(pattern, over_box(1, range(boxes)))
    other_sources = send(sources[0], over_box(1, range(boxes)))
    own_half = pl.pallas_call(
        mask_kernel,
        out_shape=jax.ShapeDtypeStruct(raw.shape, jnp.bfloat16),
        in_specs=[SMEM, VMEM],
        out_specs=VMEM,
        compiler_params=PARAMS,
        cost_estimate=cost(width * width, 4 * width * width),
    )(pattern, raw)

    def inverse_of(level):
        node = (boxes >> (level + 1)) - 1 + (position >> (level + 1))
        return lax.dynamic_index_in_dim(face_inverses[0], node, 0, keepdims=False).astype(
            jnp.bfloat16
        )

    rows = -(-2 * rows_here // 8) * 8
    packed = jnp.concatenate(
        [
            jnp.where(is_second, other_sources, sources[0]),
            jnp.where(is_second, sources[0], other_sources),
            jnp.zeros((rows - 2 * rows_here, width), jnp.float32),
            index_map.astype(jnp.float32),
        ],
        axis=0,
    )

    pieces = tuple((at, face) for at in range(0, width, face))
    upper = tuple(piece for piece in pieces if piece[0] < width // 2)
    lower = tuple(piece for piece in pieces if piece[0] >= width // 2)
    inverse = inverse_of(0)
    top = leaf_combine(pattern_other, own_half, raw_other, inverse, None, 0, upper)
    bottom = leaf_combine(pattern_other, own_half, raw_other, inverse, top[-1], 1, lower)
    current = dict(zip(upper + lower, [*top[:-1], *bottom]))

    for level in range(1, levels):
        final = level == levels - 1
        change = 1 << level
        inverse = inverse_of(level)
        order = sorted(pieces, key=lambda piece: (piece[0] != level * face, piece[0]))
        received = {}
        state = None
        if not final:
            for piece in order:
                received[piece] = send(current[piece], over_box(change, range(boxes)))
            renewed = {}
            for piece in order:
                renewed[piece], state = combine(
                    second_flag,
                    current[piece],
                    received[piece],
                    inverse,
                    None,
                    state,
                    level * face,
                    piece[0],
                )
            current = renewed
            continue
        over = over_box(change ^ 1, range(0, boxes, 2))
        forward = route(pair_moves, 1, 0)
        for piece in order[:AHEAD]:
            received[piece] = send(current[piece], over)
        pair_pieces = {}
        for k, piece in enumerate(order):
            following = order[k + AHEAD] if k + AHEAD < len(order) else None
            other = received[piece]
            if k == SMALL_AT + 2:
                other = after(other, pair_packed)
            if k > AHEAD:
                other = after(other, pair_pieces[order[k - 1]])
            payload, state = combine(
                second_flag,
                current[piece],
                other,
                inverse,
                None if following is None else current[following],
                state,
                level * face,
                piece[0],
            )
            pair_pieces[piece] = send(payload, forward + ([] if following is None else over))
            if following is not None:
                received[following] = pair_pieces[piece]
            if k == SMALL_AT:
                sendable = after(packed, payload)
                pair_packed = send(sendable, route(pair_moves[1:]) + route([(0, 1)], 1, 1))
    merged = state[1]
    small = [packed, pair_packed]
    pair_maps = [pair_pieces[piece] for piece in pieces]

    first = pair_packed[:rows].astype(jnp.bfloat16)
    (down_odd,), state = segment(
        coupling, is_second & (layer == 1), first, small, {}, [[merged], pair_maps], (OWN,), ()
    )
    merged_first = send(after(merged, state), route(every, 1, 0))
    maps = [[merged_first], pair_maps]
    at, core = 1, 1
    kept = []
    ups = {}
    for k, (target, slots) in enumerate(chain):
        arrived = send(state, route([(at, target)], core, 0))
        at, core = target, 0
        turn = k == len(chain) - 1
        back = tuple(reversed(slots))
        results, state = segment(
            coupling, layer == at, arrived, small, {}, maps, slots, back[1:] if turn else ()
        )
        kept.append(dict(zip(slots, results)))
        if k == 0:
            down_odd_first = send(after(down_odd, state), route([(1, 0)], 1, 0))
        if turn:
            ups[at] = dict(zip(back[1:], results[len(slots) :]))
            ups[at][back[0]] = results[len(slots) - 1]
    merged = jnp.where(is_second, merged, merged_first)
    down_odd = jnp.where(layer == 0, down_odd_first, down_odd)

    for k in reversed(range(len(chain) - 1)):
        target, slots = chain[k]
        arrived = send(state, route([(at, target)]))
        if k == len(chain) - 2:
            arrived, merged = lax.optimization_barrier((arrived, merged))
        at = target
        back = tuple(reversed(slots))
        results, state = segment(coupling, layer == at, arrived, small, kept[k], maps, (), back)
        ups[at] = dict(zip(back, results))
    from_own = send(state, route([(at, 1)], 0, 1))
    from_pair = send(state, route([(at, 0)]))

    mine = [jnp.zeros((rows, width), jnp.float32)] * 2
    for target, values in ups.items():
        for slot in (OWN, PAIR):
            mine[slot] = jnp.where(layer == target, values[slot], mine[slot])
    settled = mine[OWN] + send(mine[PAIR], route([(z, a) for a, z in pair_moves[1:]]))

    odd = (layer % 2).astype(jnp.int32)[None]
    last = pl.pallas_call(
        functools.partial(last_kernel, coupling, len(pair_maps)),
        out_shape=jax.ShapeDtypeStruct((rows, width), jnp.float32),
        in_specs=[SMEM] + [VMEM] * (5 + len(pair_maps)),
        out_specs=VMEM,
        compiler_params=SWEEP_PARAMS,
        cost_estimate=cost(6 * 256 * 1024 * 1024, 6 * 1024 * 1024),
    )(odd, from_pair, from_own, packed[:rows], down_odd, merged, *pair_maps)
    upward = jnp.where(layer < 2, last, settled)
    ends = upward[:rows_here], upward[rows_here : 2 * rows_here]
    there = send(
        jnp.where(is_second, ends[0], ends[1]),
        route([(1, 1)], 1, 0) + route([move for move in every if move[0] != 1], 0, 1),
    )
    here = jnp.where(is_second, ends[1], ends[0])
    runs = jnp.logical_xor(is_second, layer != 1)
    return (merged[None], jnp.where(runs, here, there)[None])


def solution(mesh):
    return jax.shard_map(
        on_device,
        mesh=mesh,
        in_specs=(
            P("layer", "box", None),
            P("layer", "box", None),
            P("layer", None, None, None),
            P("layer", None),
            P("layer", "box", None),
        ),
        out_specs=(P("layer", None, None), P("layer", "box", None)),
        check_vma=False,
    )
```

```python
import functools

import jax
import jax.numpy as jnp
from jax import lax
from jax.experimental import pallas as pl
from jax.experimental.pallas import tpu as pltpu
from jax.sharding import PartitionSpec as P

AXES = ("layer", "box")
AHEAD = 2
SMALL_AT = 0
VMEM = pl.BlockSpec(memory_space=pltpu.VMEM)
SMEM = pl.BlockSpec(memory_space=pltpu.SMEM)
PARAMS = pltpu.CompilerParams(vmem_limit_bytes=24 * 1024 * 1024)
SWEEP_PARAMS = pltpu.CompilerParams(vmem_limit_bytes=10 * 1024 * 1024)
OWN, PAIR = 0, 1


def cost(flops, moved):
    return pl.CostEstimate(flops=flops, bytes_accessed=moved, transcendentals=0)


def dot32(a, b):
    return jnp.dot(a, b, preferred_element_type=jnp.float32)


def dot32_t(a, b):
    return lax.dot_general(a, b, (((1,), (1,)), ((), ())), preferred_element_type=jnp.float32)


def minus_face(joined, face_at, inverse, right):
    face = inverse.shape[0]
    left = joined[:, face_at : face_at + face].astype(jnp.bfloat16)
    product = dot32(left, inverse).astype(jnp.bfloat16)
    return (joined - dot32(product, right)).astype(jnp.bfloat16)


def masked(values, pattern, row_at, row_count, block_at):
    width = values.shape[1]
    block = width // pattern.shape[1]
    strips = []
    for r in range(row_count // block):
        at = slice(row_at + r * block, row_at + (r + 1) * block)
        strips.append(
            jnp.concatenate(
                [
                    values[at, c * block : (c + 1) * block].astype(jnp.float32)
                    * (0.5 * pattern[block_at + r, c].astype(jnp.float32))
                    for c in range(width // block)
                ],
                axis=1,
            )
        )
    return jnp.concatenate(strips, axis=0)


def leaf_kernel(first_row, is_face, own_pattern, other_pattern, own, other, inverse, *refs):
    refs = list(refs)
    face = inverse.shape[0]
    right = None if is_face else refs.pop(0)[...]
    block = own.shape[1] // own_pattern.shape[1]
    for i in range(own.shape[0] // face):
        block_at = (first_row + i * face) // block
        joined = masked(own, own_pattern, i * face, face, block_at) + masked(
            other, other_pattern, i * face, face, block_at
        )
        if right is None:
            right = joined.astype(jnp.bfloat16)
            refs[-1][...] = right
        refs[i][...] = minus_face(joined, 0, inverse[...], right)


def leaf_combine(own_pattern, other_pattern, own, other, inverse, face_rows, half):
    is_face = face_rows is None
    width = own.shape[1]
    rows = own.shape[0] // 2
    face = inverse.shape[0]
    count = rows // face
    piece = jax.ShapeDtypeStruct((face, width), jnp.bfloat16)
    map_spec = pl.BlockSpec((rows, width), lambda i: (half, 0))
    extra = [] if is_face else [face_rows]
    return pl.pallas_call(
        functools.partial(leaf_kernel, half * rows, is_face),
        grid=(1,),
        out_shape=[piece] * (count + (1 if is_face else 0)),
        in_specs=[SMEM, SMEM, map_spec, map_spec, VMEM] + [VMEM] * len(extra),
        out_specs=[VMEM] * (count + (1 if is_face else 0)),
        compiler_params=PARAMS,
        cost_estimate=cost(2 * rows * face * (width + face), 6 * rows * width),
    )(own_pattern, other_pattern, own, other, inverse, *extra)


def combine_kernel(face_at, is_face, with_next, whole_rows, own, other, inverse, *refs):
    refs = list(refs)
    following = refs.pop(0) if with_next else None
    joined = 0.5 * (own[...].astype(jnp.float32) + other[...].astype(jnp.float32))
    if is_face:
        right = joined.astype(jnp.bfloat16)
    else:
        right = refs.pop(0)[...]
        refs.pop(0)
    piece = minus_face(joined, face_at, inverse[...], right)
    refs[1][whole_rows, :] = piece
    if is_face:
        refs[2][...] = right
    refs[0][...] = piece
    if with_next:

        @pl.when(lax.axis_index("box") % 2 == 0)
        def _():
            refs[0][...] = following[...]


def combine(own, other, inverse, following, state, face_at, row_at):
    is_face = state is None
    rows, width = own.shape
    extra = [] if following is None else [following]
    aliases = {} if is_face else {3 + len(extra) + 1: 1}
    extra += [] if is_face else list(state)
    piece = jax.ShapeDtypeStruct((rows, width), jnp.bfloat16)
    whole = jax.ShapeDtypeStruct((width, width), jnp.bfloat16)
    result = pl.pallas_call(
        functools.partial(
            combine_kernel,
            face_at,
            is_face,
            following is not None,
            slice(row_at, row_at + rows),
        ),
        out_shape=[piece, whole] + ([piece] if is_face else []),
        in_specs=[VMEM] * (3 + len(extra)),
        out_specs=[VMEM] * (3 if is_face else 2),
        input_output_aliases=aliases,
        compiler_params=PARAMS,
        cost_estimate=cost(0, 0),
    )(own, other, inverse, *extra)
    return result[0], ((result[2] if is_face else state[0]), result[1])


def spread(pieces, rows):
    return jnp.concatenate([dot32_t(rows, piece[...]) for piece in pieces], axis=1)


def gather_sum(pieces, rows):
    at, total = 0, None
    for piece in pieces:
        size = piece.shape[0]
        term = dot32(rows[:, at : at + size], piece[...])
        total = term if total is None else total + term
        at += size
    return total


def lanes_at(rows, index_row):
    lanes = 128
    count, width = rows.shape
    parts = [rows[:, at : at + lanes] for at in range(0, width, lanes)]
    outs = []
    for at in range(0, width, lanes):
        index = jnp.broadcast_to(index_row[:, at : at + lanes].astype(jnp.int32), (count, lanes))
        lane, part = index % lanes, index // lanes
        total = jnp.zeros((count, lanes), rows.dtype)
        for k, values in enumerate(parts):
            total = jnp.where(part == k, jnp.take_along_axis(values, lane, axis=1), total)
        outs.append(total)
    return jnp.concatenate(outs, axis=1)


def segment_kernel(coupling, at, pieces_of, down_steps, up_steps, *refs):
    @pl.when(lax.axis_index("layer") == at)
    def _():
        run_segment(coupling, pieces_of, down_steps, up_steps, *refs)


def run_segment(coupling, pieces_of, down_steps, up_steps, *refs):
    refs = list(refs)
    state = refs.pop(0)[...]
    maps, downs = {}, {}
    operands = []
    for slot in down_steps:
        operands.append(refs.pop(0))
        maps[slot] = [refs.pop(0) for _ in range(pieces_of[slot])]
    for slot in up_steps:
        if slot not in down_steps:
            downs[slot] = refs.pop(0)[...]
            maps[slot] = [refs.pop(0) for _ in range(pieces_of[slot])]
    for slot, packed in zip(down_steps, operands):
        count = state.shape[0]
        moved = lanes_at(state.astype(jnp.float32), packed[count:]).astype(jnp.bfloat16)
        downs[slot] = packed[:count] + coupling * spread(maps[slot], moved)
        state = downs[slot].astype(jnp.bfloat16)
        refs.pop(0)[...] = downs[slot]
    for slot in up_steps:
        value = downs[slot] + coupling * gather_sum(maps[slot], state)
        state = value.astype(jnp.bfloat16)
        refs.pop(0)[...] = value
    refs.pop(0)[...] = state


def segment(coupling, at, arrived, packed, downs, maps, down_steps, up_steps):
    operands = [arrived]
    for slot in down_steps:
        operands += [packed[slot], *maps[slot]]
    for slot in up_steps:
        if slot not in down_steps:
            operands += [downs[slot], *maps[slot]]
    rows = jax.ShapeDtypeStruct(arrived.shape, jnp.float32)
    steps = len(down_steps) + len(up_steps)
    results = pl.pallas_call(
        functools.partial(
            segment_kernel, coupling, at, [len(entry) for entry in maps], down_steps, up_steps
        ),
        out_shape=[rows] * steps + [jax.ShapeDtypeStruct(arrived.shape, jnp.bfloat16)],
        in_specs=[VMEM] * len(operands),
        out_specs=[VMEM] * (steps + 1),
        compiler_params=SWEEP_PARAMS,
        cost_estimate=cost(steps * 2 * 256 * 1024 * 1024, steps * 2 * 1024 * 1024),
    )(*operands)
    return results[:-1], results[-1]


def last_kernel(coupling, count, odd, from_pair, from_own, source, down_odd, *refs):
    own, pair, out = refs[:1], refs[1 : 1 + count], refs[1 + count]
    total = gather_sum(pair, from_pair[...]) + gather_sum(own, from_own[...])
    up_odd = down_odd[...] + coupling * total
    up_even = source[...] + coupling * gather_sum(own, up_odd.astype(jnp.bfloat16))
    out[...] = jnp.where(odd[0] == 1, up_odd, up_even)


def on_device(box_maps, block_pattern, face_inverses, index_map, sources):
    boxes = lax.axis_size("box")
    layers = lax.axis_size("layer")
    coupling = float(boxes) ** 0.5
    levels = boxes.bit_length() - 1
    face = face_inverses.shape[2]
    width = box_maps.shape[2]
    rows_here = sources.shape[1]
    position = lax.axis_index("box")
    layer = lax.axis_index("layer")
    is_second = position % 2 == 1

    chain = [(layer_at, (OWN, PAIR)) for layer_at in range(2, layers, 2)]
    pair_moves = [(layer_at + 1, layer_at) for layer_at in range(0, layers, 2)]

    def route(moves, source_core=0, target_core=0):
        return [
            (a * boxes + b + source_core, z * boxes + b + target_core)
            for a, z in moves
            for b in range(0, boxes, 2)
        ]

    def over_box(change, starts):
        return [(i * boxes + b, i * boxes + (b ^ change)) for i in range(layers) for b in starts]

    def send(value, pairs_of_devices):
        return lax.ppermute(value, AXES, pairs_of_devices)

    def after(value, *others):
        return lax.optimization_barrier((value, *others))[0]

    every = [(i, i) for i in range(layers)]

    raw = box_maps[0]
    pattern = block_pattern[0]
    raw_other = send(raw, over_box(1, range(boxes)))
    pattern_other = send(pattern, over_box(1, range(boxes)))
    other_sources = send(sources[0], over_box(1, range(boxes)))
    def inverse_of(level):
        node = (boxes >> (level + 1)) - 1 + (position >> (level + 1))
        return lax.dynamic_index_in_dim(face_inverses[0], node, 0, keepdims=False).astype(
            jnp.bfloat16
        )

    rows = -(-2 * rows_here // 8) * 8
    packed = jnp.concatenate(
        [
            jnp.where(is_second, other_sources, sources[0]),
            jnp.where(is_second, sources[0], other_sources),
            jnp.zeros((rows - 2 * rows_here, width), jnp.float32),
            index_map.astype(jnp.float32),
        ],
        axis=0,
    )

    pieces = tuple((at, face) for at in range(0, width, face))
    upper = tuple(piece for piece in pieces if piece[0] < width // 2)
    lower = tuple(piece for piece in pieces if piece[0] >= width // 2)
    inverse = inverse_of(0)
    top = leaf_combine(pattern, pattern_other, raw, raw_other, inverse, None, 0)
    bottom = leaf_combine(pattern, pattern_other, raw, raw_other, inverse, top[-1], 1)
    current = dict(zip(upper + lower, [*top[:-1], *bottom]))

    for level in range(1, levels):
        final = level == levels - 1
        change = 1 << level
        inverse = inverse_of(level)
        order = sorted(pieces, key=lambda piece: (piece[0] != level * face, piece[0]))
        received = {}
        state = None
        if not final:
            for piece in order:
                received[piece] = send(current[piece], over_box(change, range(boxes)))
            renewed = {}
            for piece in order:
                renewed[piece], state = combine(
                    current[piece],
                    received[piece],
                    inverse,
                    None,
                    state,
                    level * face,
                    piece[0],
                )
            current = renewed
            continue
        over = over_box(change ^ 1, range(0, boxes, 2))
        forward = route(pair_moves, 1, 0)
        for piece in order[:AHEAD]:
            received[piece] = send(current[piece], over)
        pair_pieces = {}
        for k, piece in enumerate(order):
            following = order[k + AHEAD] if k + AHEAD < len(order) else None
            other = received[piece]
            if k == SMALL_AT + 2:
                other = after(other, pair_packed)
            if k > AHEAD:
                other = after(other, pair_pieces[order[k - 1]])
            payload, state = combine(
                current[piece],
                other,
                inverse,
                None if following is None else current[following],
                state,
                level * face,
                piece[0],
            )
            pair_pieces[piece] = send(payload, forward + ([] if following is None else over))
            if following is not None:
                received[following] = pair_pieces[piece]
            if k == SMALL_AT:
                sendable = after(packed, payload)
                pair_packed = send(sendable, route(pair_moves[1:]) + route([(0, 1)], 1, 1))
    merged = state[1]
    small = [packed, pair_packed]
    pair_maps = [pair_pieces[piece] for piece in pieces]

    first = pair_packed[:rows].astype(jnp.bfloat16)
    (down_odd,), state = segment(
        coupling, 1, first, small, {}, [[merged], pair_maps], (OWN,), ()
    )
    merged_first = send(after(merged, state), route(every, 1, 0))
    maps = [[merged_first], pair_maps]
    at, core = 1, 1
    kept = []
    ups = {}
    for k, (target, slots) in enumerate(chain):
        arrived = send(state, route([(at, target)], core, 0))
        at, core = target, 0
        turn = k == len(chain) - 1
        back = tuple(reversed(slots))
        results, state = segment(
            coupling, at, arrived, small, {}, maps, slots, back[1:] if turn else ()
        )
        kept.append(dict(zip(slots, results)))
        if k == 0:
            down_odd_first = send(after(down_odd, state), route([(1, 0)], 1, 0))
        if turn:
            ups[at] = dict(zip(back[1:], results[len(slots) :]))
            ups[at][back[0]] = results[len(slots) - 1]
    merged = jnp.where(is_second, merged, merged_first)
    down_odd = jnp.where(layer == 0, down_odd_first, down_odd)

    for k in reversed(range(len(chain) - 1)):
        target, slots = chain[k]
        arrived = send(state, route([(at, target)]))
        if k == len(chain) - 2:
            arrived, merged = lax.optimization_barrier((arrived, merged))
        at = target
        back = tuple(reversed(slots))
        results, state = segment(coupling, at, arrived, small, kept[k], maps, (), back)
        ups[at] = dict(zip(back, results))
    from_own = send(state, route([(at, 1)], 0, 1))
    from_pair = send(state, route([(at, 0)]))

    mine = [jnp.zeros((rows, width), jnp.float32)] * 2
    for target, values in ups.items():
        for slot in (OWN, PAIR):
            mine[slot] = jnp.where(layer == target, values[slot], mine[slot])
    settled = mine[OWN] + send(mine[PAIR], route([(z, a) for a, z in pair_moves[1:]]))

    odd = (layer % 2).astype(jnp.int32)[None]
    last = pl.pallas_call(
        functools.partial(last_kernel, coupling, len(pair_maps)),
        out_shape=jax.ShapeDtypeStruct((rows, width), jnp.float32),
        in_specs=[SMEM] + [VMEM] * (5 + len(pair_maps)),
        out_specs=VMEM,
        compiler_params=SWEEP_PARAMS,
        cost_estimate=cost(6 * 256 * 1024 * 1024, 6 * 1024 * 1024),
    )(odd, from_pair, from_own, packed[:rows], down_odd, merged, *pair_maps)
    upward = jnp.where(layer < 2, last, settled)
    ends = upward[:rows_here], upward[rows_here : 2 * rows_here]
    there = send(
        jnp.where(is_second, ends[0], ends[1]),
        route([(1, 1)], 1, 0) + route([move for move in every if move[0] != 1], 0, 1),
    )
    here = jnp.where(is_second, ends[1], ends[0])
    runs = jnp.logical_xor(is_second, layer != 1)
    return (merged[None], jnp.where(runs, here, there)[None])


def solution(mesh):
    return jax.shard_map(
        on_device,
        mesh=mesh,
        in_specs=(
            P("layer", "box", None),
            P("layer", "box", None),
            P("layer", None, None, None),
            P("layer", None),
            P("layer", "box", None),
        ),
        out_specs=(P("layer", None, None), P("layer", "box", None)),
        check_vma=False,
    )
```

```python
import functools

import jax
import jax.numpy as jnp
from jax import lax
from jax.experimental import pallas as pl
from jax.experimental.pallas import tpu as pltpu
from jax.sharding import PartitionSpec as P

AXES = ("layer", "box")
AHEAD = 2
SMALL_AT = 0
VMEM = pl.BlockSpec(memory_space=pltpu.VMEM)
SMEM = pl.BlockSpec(memory_space=pltpu.SMEM)
PARAMS = pltpu.CompilerParams(vmem_limit_bytes=24 * 1024 * 1024)
SWEEP_PARAMS = pltpu.CompilerParams(vmem_limit_bytes=10 * 1024 * 1024)
OWN, PAIR = 0, 1


def cost(flops, moved):
    return pl.CostEstimate(flops=flops, bytes_accessed=moved, transcendentals=0)


def dot32(a, b):
    return jnp.dot(a, b, preferred_element_type=jnp.float32)


def dot32_t(a, b):
    return lax.dot_general(a, b, (((1,), (1,)), ((), ())), preferred_element_type=jnp.float32)


def minus_face(joined, face_at, inverse, right):
    face = inverse.shape[0]
    left = joined[:, face_at : face_at + face].astype(jnp.bfloat16)
    product = dot32(left, inverse).astype(jnp.bfloat16)
    return (joined - dot32(product, right)).astype(jnp.bfloat16)


def masked(values, pattern, row_at, row_count, block_at):
    width = values.shape[1]
    block = width // pattern.shape[1]
    strips = []
    for r in range(row_count // block):
        at = slice(row_at + r * block, row_at + (r + 1) * block)
        strips.append(
            jnp.concatenate(
                [
                    values[at, c * block : (c + 1) * block].astype(jnp.float32)
                    * (0.5 * pattern[block_at + r, c].astype(jnp.float32))
                    for c in range(width // block)
                ],
                axis=1,
            )
        )
    return jnp.concatenate(strips, axis=0)


def mask_kernel(pattern, values, out):
    block = values.shape[1] // pattern.shape[1]
    for r in range(values.shape[0] // block):
        out[r * block : (r + 1) * block] = masked(values, pattern, r * block, block, r).astype(
            jnp.bfloat16
        )


def leaf_kernel(first_row, is_face, pieces, other_pattern, own, other, inverse, *refs):
    refs = list(refs)
    face = inverse.shape[0]
    right = None if is_face else refs.pop(0)[...]
    block = own.shape[1] // other_pattern.shape[1]
    for i in range(own.shape[0] // face):
        at = first_row + i * face
        joined = own[i * face : (i + 1) * face].astype(jnp.float32) + masked(
            other, other_pattern, i * face, face, at // block
        )
        if right is None:
            right = joined.astype(jnp.bfloat16)
            refs[-1][...] = right
        result = minus_face(joined, 0, inverse[...], right)
        for ref, (start, size) in zip(refs, pieces):
            low, high = max(start, at), min(start + size, at + face)
            if low < high:
                ref[low - start : high - start] = result[low - at : high - at]


def leaf_combine(other_pattern, own, other, inverse, face_rows, half, pieces):
    is_face = face_rows is None
    width = own.shape[1]
    rows = own.shape[0] // 2
    face = inverse.shape[0]
    shapes = [jax.ShapeDtypeStruct((size, width), jnp.bfloat16) for _, size in pieces]
    if is_face:
        shapes.append(jax.ShapeDtypeStruct((face, width), jnp.bfloat16))
    map_spec = pl.BlockSpec((rows, width), lambda i: (half, 0))
    extra = [] if is_face else [face_rows]
    return pl.pallas_call(
        functools.partial(leaf_kernel, half * rows, is_face, pieces),
        grid=(1,),
        out_shape=shapes,
        in_specs=[SMEM, map_spec, map_spec, VMEM] + [VMEM] * len(extra),
        out_specs=[VMEM] * len(shapes),
        compiler_params=PARAMS,
        cost_estimate=cost(2 * rows * face * (width + face), 6 * rows * width),
    )(other_pattern, own, other, inverse, *extra)


def combine_kernel(face_at, is_face, with_next, whole_rows, own, other, inverse, *refs):
    refs = list(refs)
    following = refs.pop(0) if with_next else None
    joined = 0.5 * (own[...].astype(jnp.float32) + other[...].astype(jnp.float32))
    if is_face:
        right = joined.astype(jnp.bfloat16)
    else:
        right = refs.pop(0)[...]
        refs.pop(0)
    piece = minus_face(joined, face_at, inverse[...], right)
    refs[1][whole_rows, :] = piece
    if is_face:
        refs[2][...] = right
    refs[0][...] = piece
    if with_next:

        @pl.when(lax.axis_index("box") % 2 == 0)
        def _():
            refs[0][...] = following[...]


def combine(own, other, inverse, following, state, face_at, row_at):
    is_face = state is None
    rows, width = own.shape
    extra = [] if following is None else [following]
    aliases = {} if is_face else {3 + len(extra) + 1: 1}
    extra += [] if is_face else list(state)
    piece = jax.ShapeDtypeStruct((rows, width), jnp.bfloat16)
    whole = jax.ShapeDtypeStruct((width, width), jnp.bfloat16)
    result = pl.pallas_call(
        functools.partial(
            combine_kernel,
            face_at,
            is_face,
            following is not None,
            slice(row_at, row_at + rows),
        ),
        out_shape=[piece, whole] + ([piece] if is_face else []),
        in_specs=[VMEM] * (3 + len(extra)),
        out_specs=[VMEM] * (3 if is_face else 2),
        input_output_aliases=aliases,
        compiler_params=PARAMS,
        cost_estimate=cost(0, 0),
    )(own, other, inverse, *extra)
    return result[0], ((result[2] if is_face else state[0]), result[1])


def spread(pieces, rows):
    return jnp.concatenate([dot32_t(rows, piece[...]) for piece in pieces], axis=1)


def gather_sum(pieces, rows):
    at, total = 0, None
    for piece in pieces:
        size = piece.shape[0]
        term = dot32(rows[:, at : at + size], piece[...])
        total = term if total is None else total + term
        at += size
    return total


def lanes_at(rows, index_row):
    lanes = 128
    count, width = rows.shape
    parts = [rows[:, at : at + lanes] for at in range(0, width, lanes)]
    outs = []
    for at in range(0, width, lanes):
        index = jnp.broadcast_to(index_row[:, at : at + lanes].astype(jnp.int32), (count, lanes))
        lane, part = index % lanes, index // lanes
        total = jnp.zeros((count, lanes), rows.dtype)
        for k, values in enumerate(parts):
            total = jnp.where(part == k, jnp.take_along_axis(values, lane, axis=1), total)
        outs.append(total)
    return jnp.concatenate(outs, axis=1)


def segment_kernel(coupling, at, pieces_of, down_steps, up_steps, *refs):
    @pl.when(lax.axis_index("layer") == at)
    def _():
        run_segment(coupling, pieces_of, down_steps, up_steps, *refs)


def run_segment(coupling, pieces_of, down_steps, up_steps, *refs):
    refs = list(refs)
    state = refs.pop(0)[...]
    maps, downs = {}, {}
    operands = []
    for slot in down_steps:
        operands.append(refs.pop(0))
        maps[slot] = [refs.pop(0) for _ in range(pieces_of[slot])]
    for slot in up_steps:
        if slot not in down_steps:
            downs[slot] = refs.pop(0)[...]
            maps[slot] = [refs.pop(0) for _ in range(pieces_of[slot])]
    for slot, packed in zip(down_steps, operands):
        count = state.shape[0]
        moved = lanes_at(state.astype(jnp.float32), packed[count:]).astype(jnp.bfloat16)
        downs[slot] = packed[:count] + coupling * spread(maps[slot], moved)
        state = downs[slot].astype(jnp.bfloat16)
        refs.pop(0)[...] = downs[slot]
    for slot in up_steps:
        value = downs[slot] + coupling * gather_sum(maps[slot], state)
        state = value.astype(jnp.bfloat16)
        refs.pop(0)[...] = value
    refs.pop(0)[...] = state


def segment(coupling, at, arrived, packed, downs, maps, down_steps, up_steps):
    operands = [arrived]
    for slot in down_steps:
        operands += [packed[slot], *maps[slot]]
    for slot in up_steps:
        if slot not in down_steps:
            operands += [downs[slot], *maps[slot]]
    rows = jax.ShapeDtypeStruct(arrived.shape, jnp.float32)
    steps = len(down_steps) + len(up_steps)
    results = pl.pallas_call(
        functools.partial(
            segment_kernel, coupling, at, [len(entry) for entry in maps], down_steps, up_steps
        ),
        out_shape=[rows] * steps + [jax.ShapeDtypeStruct(arrived.shape, jnp.bfloat16)],
        in_specs=[VMEM] * len(operands),
        out_specs=[VMEM] * (steps + 1),
        compiler_params=SWEEP_PARAMS,
        cost_estimate=cost(steps * 2 * 256 * 1024 * 1024, steps * 2 * 1024 * 1024),
    )(*operands)
    return results[:-1], results[-1]


def last_kernel(coupling, count, odd, from_pair, from_own, source, down_odd, *refs):
    own, pair, out = refs[:1], refs[1 : 1 + count], refs[1 + count]
    total = gather_sum(pair, from_pair[...]) + gather_sum(own, from_own[...])
    up_odd = down_odd[...] + coupling * total
    up_even = source[...] + coupling * gather_sum(own, up_odd.astype(jnp.bfloat16))
    out[...] = jnp.where(odd[0] == 1, up_odd, up_even)


def on_device(box_maps, block_pattern, face_inverses, index_map, sources):
    boxes = lax.axis_size("box")
    layers = lax.axis_size("layer")
    coupling = float(boxes) ** 0.5
    levels = boxes.bit_length() - 1
    face = face_inverses.shape[2]
    width = box_maps.shape[2]
    rows_here = sources.shape[1]
    position = lax.axis_index("box")
    layer = lax.axis_index("layer")
    is_second = position % 2 == 1

    chain = [(layer_at, (OWN, PAIR)) for layer_at in range(2, layers, 2)]
    pair_moves = [(layer_at + 1, layer_at) for layer_at in range(0, layers, 2)]

    def route(moves, source_core=0, target_core=0):
        return [
            (a * boxes + b + source_core, z * boxes + b + target_core)
            for a, z in moves
            for b in range(0, boxes, 2)
        ]

    def over_box(change, starts):
        return [(i * boxes + b, i * boxes + (b ^ change)) for i in range(layers) for b in starts]

    def send(value, pairs_of_devices):
        return lax.ppermute(value, AXES, pairs_of_devices)

    def after(value, *others):
        return lax.optimization_barrier((value, *others))[0]

    every = [(i, i) for i in range(layers)]

    raw = box_maps[0]
    pattern = block_pattern[0]
    raw_other = send(raw, over_box(1, range(boxes)))
    pattern_other = send(pattern, over_box(1, range(boxes)))
    other_sources = send(sources[0], over_box(1, range(boxes)))
    own_half = pl.pallas_call(
        mask_kernel,
        out_shape=jax.ShapeDtypeStruct(raw.shape, jnp.bfloat16),
        in_specs=[SMEM, VMEM],
        out_specs=VMEM,
        compiler_params=PARAMS,
        cost_estimate=cost(width * width, 4 * width * width),
    )(pattern, raw)

    def inverse_of(level):
        node = (boxes >> (level + 1)) - 1 + (position >> (level + 1))
        return lax.dynamic_index_in_dim(face_inverses[0], node, 0, keepdims=False).astype(
            jnp.bfloat16
        )

    rows = -(-2 * rows_here // 8) * 8
    packed = jnp.concatenate(
        [
            jnp.where(is_second, other_sources, sources[0]),
            jnp.where(is_second, sources[0], other_sources),
            jnp.zeros((rows - 2 * rows_here, width), jnp.float32),
            index_map.astype(jnp.float32),
        ],
        axis=0,
    )

    pieces = tuple((at, face) for at in range(0, width, face))
    upper = tuple(piece for piece in pieces if piece[0] < width // 2)
    lower = tuple(piece for piece in pieces if piece[0] >= width // 2)
    inverse = inverse_of(0)
    top = leaf_combine(pattern_other, own_half, raw_other, inverse, None, 0, upper)
    bottom = leaf_combine(pattern_other, own_half, raw_other, inverse, top[-1], 1, lower)
    current = dict(zip(upper + lower, [*top[:-1], *bottom]))

    for level in range(1, levels):
        final = level == levels - 1
        change = 1 << level
        inverse = inverse_of(level)
        order = sorted(pieces, key=lambda piece: (piece[0] != level * face, piece[0]))
        received = {}
        state = None
        if not final:
            for piece in order:
                received[piece] = send(current[piece], over_box(change, range(boxes)))
            renewed = {}
            for piece in order:
                renewed[piece], state = combine(
                    current[piece],
                    received[piece],
                    inverse,
                    None,
                    state,
                    level * face,
                    piece[0],
                )
            current = renewed
            continue
        over = over_box(change ^ 1, range(0, boxes, 2))
        forward = route(pair_moves, 1, 0)
        for piece in order[:AHEAD]:
            received[piece] = send(current[piece], over)
        pair_pieces = {}
        for k, piece in enumerate(order):
            following = order[k + AHEAD] if k + AHEAD < len(order) else None
            other = received[piece]
            if k == SMALL_AT + 2:
                other = after(other, pair_packed)
            if k > AHEAD:
                other = after(other, pair_pieces[order[k - 1]])
            payload, state = combine(
                current[piece],
                other,
                inverse,
                None if following is None else current[following],
                state,
                level * face,
                piece[0],
            )
            pair_pieces[piece] = send(payload, forward + ([] if following is None else over))
            if following is not None:
                received[following] = pair_pieces[piece]
            if k == SMALL_AT:
                sendable = after(packed, payload)
                pair_packed = send(sendable, route(pair_moves[1:]) + route([(0, 1)], 1, 1))
    merged = state[1]
    small = [packed, pair_packed]
    pair_maps = [pair_pieces[piece] for piece in pieces]

    first = pair_packed[:rows].astype(jnp.bfloat16)
    (down_odd,), state = segment(
        coupling, 1, first, small, {}, [[merged], pair_maps], (OWN,), ()
    )
    merged_first = send(after(merged, state), route(every, 1, 0))
    maps = [[merged_first], pair_maps]
    at, core = 1, 1
    kept = []
    ups = {}
    for k, (target, slots) in enumerate(chain):
        arrived = send(state, route([(at, target)], core, 0))
        at, core = target, 0
        turn = k == len(chain) - 1
        back = tuple(reversed(slots))
        results, state = segment(
            coupling, at, arrived, small, {}, maps, slots, back[1:] if turn else ()
        )
        kept.append(dict(zip(slots, results)))
        if k == 0:
            down_odd_pair = send(after(down_odd, state), route([(1, 0)], 1, 0))
            down_odd_first = send(after(down_odd, state), route([(1, 1)], 1, 0))
        if turn:
            ups[at] = dict(zip(back[1:], results[len(slots) :]))
            ups[at][back[0]] = results[len(slots) - 1]
    merged = jnp.where(is_second, merged, merged_first)
    down_odd = down_odd_pair + down_odd_first

    for k in reversed(range(len(chain) - 1)):
        target, slots = chain[k]
        arrived = send(state, route([(at, target)]))
        if k == len(chain) - 2:
            arrived, merged = lax.optimization_barrier((arrived, merged))
        at = target
        back = tuple(reversed(slots))
        results, state = segment(coupling, at, arrived, small, kept[k], maps, (), back)
        ups[at] = dict(zip(back, results))
    from_own = send(state, route([(at, 1)]))
    from_pair = send(state, route([(at, 0)]))

    mine = [jnp.zeros((rows, width), jnp.float32)] * 2
    for target, values in ups.items():
        for slot in (OWN, PAIR):
            mine[slot] = jnp.where(layer == target, values[slot], mine[slot])
    settled = mine[OWN] + send(mine[PAIR], route([(z, a) for a, z in pair_moves[1:]]))

    odd = (layer % 2).astype(jnp.int32)[None]
    last = pl.pallas_call(
        functools.partial(last_kernel, coupling, len(pair_maps)),
        out_shape=jax.ShapeDtypeStruct((rows, width), jnp.float32),
        in_specs=[SMEM] + [VMEM] * (5 + len(pair_maps)),
        out_specs=VMEM,
        compiler_params=SWEEP_PARAMS,
        cost_estimate=cost(6 * 256 * 1024 * 1024, 6 * 1024 * 1024),
    )(odd, from_pair, from_own, packed[:rows], down_odd, merged_first, *pair_maps)
    upward = jnp.where(layer < 2, last, settled)
    second_rows = send(upward[rows_here : 2 * rows_here], route(every, 0, 1))
    upward = jnp.where(is_second, second_rows, upward[:rows_here])
    return (merged[None], upward[None])


def solution(mesh):
    return jax.shard_map(
        on_device,
        mesh=mesh,
        in_specs=(
            P("layer", "box", None),
            P("layer", "box", None),
            P("layer", None, None, None),
            P("layer", None),
            P("layer", "box", None),
        ),
        out_specs=(P("layer", None, None), P("layer", "box", None)),
        check_vma=False,
    )
```

```python
import functools

import jax
import jax.numpy as jnp
from jax import lax
from jax.experimental import pallas as pl
from jax.experimental.pallas import tpu as pltpu
from jax.sharding import PartitionSpec as P

AXES = ("layer", "box")
AHEAD = 2
SMALL_AT = 0
VMEM = pl.BlockSpec(memory_space=pltpu.VMEM)
SMEM = pl.BlockSpec(memory_space=pltpu.SMEM)
PARAMS = pltpu.CompilerParams(vmem_limit_bytes=16 * 1024 * 1024)
SWEEP_PARAMS = pltpu.CompilerParams(vmem_limit_bytes=6 * 1024 * 1024)
COMBINE_PARAMS = pltpu.CompilerParams(vmem_limit_bytes=12 * 1024 * 1024)
OWN, PAIR = 0, 1


def cost(flops, moved):
    return pl.CostEstimate(flops=flops, bytes_accessed=moved, transcendentals=0)


def dot32(a, b):
    return jnp.dot(a, b, preferred_element_type=jnp.float32)


def dot32_t(a, b):
    return lax.dot_general(a, b, (((1,), (1,)), ((), ())), preferred_element_type=jnp.float32)


def minus_face(joined, face_at, inverse, right):
    face = inverse.shape[0]
    left = joined[:, face_at : face_at + face].astype(jnp.bfloat16)
    product = dot32(left, inverse).astype(jnp.bfloat16)
    return (joined - dot32(product, right)).astype(jnp.bfloat16)


def masked(values, pattern, row_at, row_count, block_at):
    width = values.shape[1]
    block = width // pattern.shape[1]
    strips = []
    for r in range(row_count // block):
        at = slice(row_at + r * block, row_at + (r + 1) * block)
        strips.append(
            jnp.concatenate(
                [
                    values[at, c * block : (c + 1) * block].astype(jnp.float32)
                    * (0.5 * pattern[block_at + r, c].astype(jnp.float32))
                    for c in range(width // block)
                ],
                axis=1,
            )
        )
    return jnp.concatenate(strips, axis=0)


def mask_kernel(pattern, values, out):
    block = values.shape[1] // pattern.shape[1]
    for r in range(values.shape[0] // block):
        out[r * block : (r + 1) * block] = masked(values, pattern, r * block, block, r).astype(
            jnp.bfloat16
        )


def leaf_kernel(first_row, is_face, pieces, other_pattern, own, other, inverse, *refs):
    refs = list(refs)
    face = inverse.shape[0]
    right = None if is_face else refs.pop(0)[...]
    block = own.shape[1] // other_pattern.shape[1]
    for i in range(own.shape[0] // face):
        at = first_row + i * face
        joined = own[i * face : (i + 1) * face].astype(jnp.float32) + masked(
            other, other_pattern, i * face, face, at // block
        )
        if right is None:
            right = joined.astype(jnp.bfloat16)
            refs[-1][...] = right
        result = minus_face(joined, 0, inverse[...], right)
        for ref, (start, size) in zip(refs, pieces):
            low, high = max(start, at), min(start + size, at + face)
            if low < high:
                ref[low - start : high - start] = result[low - at : high - at]


def leaf_combine(other_pattern, own, other, inverse, face_rows, half, pieces):
    is_face = face_rows is None
    width = own.shape[1]
    rows = own.shape[0] // 2
    face = inverse.shape[0]
    shapes = [jax.ShapeDtypeStruct((size, width), jnp.bfloat16) for _, size in pieces]
    if is_face:
        shapes.append(jax.ShapeDtypeStruct((face, width), jnp.bfloat16))
    map_spec = pl.BlockSpec((rows, width), lambda i: (half, 0))
    extra = [] if is_face else [face_rows]
    return pl.pallas_call(
        functools.partial(leaf_kernel, half * rows, is_face, pieces),
        grid=(1,),
        out_shape=shapes,
        in_specs=[SMEM, map_spec, map_spec, VMEM] + [VMEM] * len(extra),
        out_specs=[VMEM] * len(shapes),
        compiler_params=PARAMS,
        cost_estimate=cost(2 * rows * face * (width + face), 6 * rows * width),
    )(other_pattern, own, other, inverse, *extra)


def combine_kernel(face_at, is_face, with_next, whole_rows, own, other, inverse, *refs):
    refs = list(refs)
    following = refs.pop(0) if with_next else None
    joined = 0.5 * (own[...].astype(jnp.float32) + other[...].astype(jnp.float32))
    if is_face:
        right = joined.astype(jnp.bfloat16)
    else:
        right = refs.pop(0)[...]
        refs.pop(0)
    piece = minus_face(joined, face_at, inverse[...], right)
    refs[1][whole_rows, :] = piece
    if is_face:
        refs[2][...] = right
    refs[0][...] = piece
    if with_next:

        @pl.when(lax.axis_index("box") % 2 == 0)
        def _():
            refs[0][...] = following[...]


def combine(own, other, inverse, following, state, face_at, row_at):
    is_face = state is None
    rows, width = own.shape
    extra = [] if following is None else [following]
    aliases = {} if is_face else {3 + len(extra) + 1: 1}
    extra += [] if is_face else list(state)
    piece = jax.ShapeDtypeStruct((rows, width), jnp.bfloat16)
    whole = jax.ShapeDtypeStruct((width, width), jnp.bfloat16)
    result = pl.pallas_call(
        functools.partial(
            combine_kernel,
            face_at,
            is_face,
            following is not None,
            slice(row_at, row_at + rows),
        ),
        out_shape=[piece, whole] + ([piece] if is_face else []),
        in_specs=[VMEM] * (3 + len(extra)),
        out_specs=[VMEM] * (3 if is_face else 2),
        input_output_aliases=aliases,
        compiler_params=COMBINE_PARAMS,
        cost_estimate=cost(0, 0),
    )(own, other, inverse, *extra)
    return result[0], ((result[2] if is_face else state[0]), result[1])


def spread(pieces, rows):
    return jnp.concatenate([dot32_t(rows, piece[...]) for piece in pieces], axis=1)


def gather_sum(pieces, rows):
    at, total = 0, None
    for piece in pieces:
        size = piece.shape[0]
        term = dot32(rows[:, at : at + size], piece[...])
        total = term if total is None else total + term
        at += size
    return total


def lanes_at(rows, index_row):
    lanes = 128
    count, width = rows.shape
    parts = [rows[:, at : at + lanes] for at in range(0, width, lanes)]
    outs = []
    for at in range(0, width, lanes):
        index = jnp.broadcast_to(index_row[:, at : at + lanes].astype(jnp.int32), (count, lanes))
        lane, part = index % lanes, index // lanes
        total = jnp.zeros((count, lanes), rows.dtype)
        for k, values in enumerate(parts):
            total = jnp.where(part == k, jnp.take_along_axis(values, lane, axis=1), total)
        outs.append(total)
    return jnp.concatenate(outs, axis=1)


def segment_kernel(coupling, at, pieces_of, down_steps, up_steps, *refs):
    @pl.when(lax.axis_index("layer") == at)
    def _():
        run_segment(coupling, pieces_of, down_steps, up_steps, *refs)


def run_segment(coupling, pieces_of, down_steps, up_steps, *refs):
    refs = list(refs)
    state = refs.pop(0)[...]
    maps, downs = {}, {}
    operands = []
    for slot in down_steps:
        operands.append(refs.pop(0))
        maps[slot] = [refs.pop(0) for _ in range(pieces_of[slot])]
    for slot in up_steps:
        if slot not in down_steps:
            downs[slot] = refs.pop(0)[...]
            maps[slot] = [refs.pop(0) for _ in range(pieces_of[slot])]
    for slot, packed in zip(down_steps, operands):
        count = state.shape[0]
        moved = lanes_at(state.astype(jnp.float32), packed[count:]).astype(jnp.bfloat16)
        downs[slot] = packed[:count] + coupling * spread(maps[slot], moved)
        state = downs[slot].astype(jnp.bfloat16)
        refs.pop(0)[...] = downs[slot]
    for slot in up_steps:
        value = downs[slot] + coupling * gather_sum(maps[slot], state)
        state = value.astype(jnp.bfloat16)
        refs.pop(0)[...] = value
    refs.pop(0)[...] = state


def segment(coupling, at, arrived, packed, downs, maps, down_steps, up_steps):
    operands = [arrived]
    for slot in down_steps:
        operands += [packed[slot], *maps[slot]]
    for slot in up_steps:
        if slot not in down_steps:
            operands += [downs[slot], *maps[slot]]
    rows = jax.ShapeDtypeStruct(arrived.shape, jnp.float32)
    steps = len(down_steps) + len(up_steps)
    results = pl.pallas_call(
        functools.partial(
            segment_kernel, coupling, at, [len(entry) for entry in maps], down_steps, up_steps
        ),
        out_shape=[rows] * steps + [jax.ShapeDtypeStruct(arrived.shape, jnp.bfloat16)],
        in_specs=[VMEM] * len(operands),
        out_specs=[VMEM] * (steps + 1),
        compiler_params=SWEEP_PARAMS,
        cost_estimate=cost(steps * 2 * 256 * 1024 * 1024, steps * 2 * 1024 * 1024),
    )(*operands)
    return results[:-1], results[-1]


def last_kernel(coupling, count, odd, from_pair, from_own, source, down_odd, *refs):
    own, pair, out = refs[:1], refs[1 : 1 + count], refs[1 + count]
    total = gather_sum(pair, from_pair[...]) + gather_sum(own, from_own[...])
    up_odd = down_odd[...] + coupling * total
    up_even = source[...] + coupling * gather_sum(own, up_odd.astype(jnp.bfloat16))
    out[...] = jnp.where(odd[0] == 1, up_odd, up_even)


def on_device(box_maps, block_pattern, face_inverses, index_map, sources):
    boxes = lax.axis_size("box")
    layers = lax.axis_size("layer")
    coupling = float(boxes) ** 0.5
    levels = boxes.bit_length() - 1
    face = face_inverses.shape[2]
    width = box_maps.shape[2]
    rows_here = sources.shape[1]
    position = lax.axis_index("box")
    layer = lax.axis_index("layer")
    is_second = position % 2 == 1

    chain = [(layer_at, (OWN, PAIR)) for layer_at in range(2, layers, 2)]
    pair_moves = [(layer_at + 1, layer_at) for layer_at in range(0, layers, 2)]

    def route(moves, source_core=0, target_core=0):
        return [
            (a * boxes + b + source_core, z * boxes + b + target_core)
            for a, z in moves
            for b in range(0, boxes, 2)
        ]

    def over_box(change, starts):
        return [(i * boxes + b, i * boxes + (b ^ change)) for i in range(layers) for b in starts]

    def send(value, pairs_of_devices):
        return lax.ppermute(value, AXES, pairs_of_devices)

    def after(value, *others):
        return lax.optimization_barrier((value, *others))[0]

    every = [(i, i) for i in range(layers)]

    raw = box_maps[0]
    pattern = block_pattern[0]
    raw_other = send(raw, over_box(1, range(boxes)))
    pattern_other = send(pattern, over_box(1, range(boxes)))
    other_sources = send(sources[0], over_box(1, range(boxes)))
    own_half = pl.pallas_call(
        mask_kernel,
        out_shape=jax.ShapeDtypeStruct(raw.shape, jnp.bfloat16),
        in_specs=[SMEM, VMEM],
        out_specs=VMEM,
        compiler_params=PARAMS,
        cost_estimate=cost(width * width, 4 * width * width),
    )(pattern, raw)

    def inverse_of(level):
        node = (boxes >> (level + 1)) - 1 + (position >> (level + 1))
        return lax.dynamic_index_in_dim(face_inverses[0], node, 0, keepdims=False).astype(
            jnp.bfloat16
        )

    rows = -(-2 * rows_here // 8) * 8
    packed = jnp.concatenate(
        [
            jnp.where(is_second, other_sources, sources[0]),
            jnp.where(is_second, sources[0], other_sources),
            jnp.zeros((rows - 2 * rows_here, width), jnp.float32),
            index_map.astype(jnp.float32),
        ],
        axis=0,
    )

    pieces = tuple((at, face) for at in range(0, width, face))
    upper = tuple(piece for piece in pieces if piece[0] < width // 2)
    lower = tuple(piece for piece in pieces if piece[0] >= width // 2)
    inverse = inverse_of(0)
    top = leaf_combine(pattern_other, own_half, raw_other, inverse, None, 0, upper)
    bottom = leaf_combine(pattern_other, own_half, raw_other, inverse, top[-1], 1, lower)
    current = dict(zip(upper + lower, [*top[:-1], *bottom]))

    for level in range(1, levels):
        final = level == levels - 1
        change = 1 << level
        inverse = inverse_of(level)
        order = sorted(pieces, key=lambda piece: (piece[0] != level * face, piece[0]))
        received = {}
        state = None
        if not final:
            for piece in order:
                received[piece] = send(current[piece], over_box(change, range(boxes)))
            renewed = {}
            for piece in order:
                renewed[piece], state = combine(
                    current[piece],
                    received[piece],
                    inverse,
                    None,
                    state,
                    level * face,
                    piece[0],
                )
            current = renewed
            continue
        over = over_box(change ^ 1, range(0, boxes, 2))
        forward = route(pair_moves, 1, 0)
        for piece in order[:AHEAD]:
            received[piece] = send(current[piece], over)
        pair_pieces = {}
        for k, piece in enumerate(order):
            following = order[k + AHEAD] if k + AHEAD < len(order) else None
            other = received[piece]
            if k == SMALL_AT + 2:
                other = after(other, pair_packed)
            if k > AHEAD:
                other = after(other, pair_pieces[order[k - 1]])
            payload, state = combine(
                current[piece],
                other,
                inverse,
                None if following is None else current[following],
                state,
                level * face,
                piece[0],
            )
            pair_pieces[piece] = send(payload, forward + ([] if following is None else over))
            if following is not None:
                received[following] = pair_pieces[piece]
            if k == SMALL_AT:
                sendable = after(packed, payload)
                pair_packed = send(sendable, route(pair_moves[1:]) + route([(0, 1)], 1, 1))
    merged = state[1]
    small = [packed, pair_packed]
    pair_maps = [pair_pieces[piece] for piece in pieces]

    first = pair_packed[:rows].astype(jnp.bfloat16)
    (down_odd,), state = segment(
        coupling, 1, first, small, {}, [[merged], pair_maps], (OWN,), ()
    )
    merged_first = send(after(merged, state), route(every, 1, 0))
    maps = [[merged_first], pair_maps]
    at, core = 1, 1
    kept = []
    ups = {}
    for k, (target, slots) in enumerate(chain):
        arrived = send(state, route([(at, target)], core, 0))
        at, core = target, 0
        turn = k == len(chain) - 1
        back = tuple(reversed(slots))
        results, state = segment(
            coupling, at, arrived, small, {}, maps, slots, back[1:] if turn else ()
        )
        kept.append(dict(zip(slots, results)))
        if k == 0:
            down_odd_pair = send(after(down_odd, state), route([(1, 0)], 1, 0))
            down_odd_first = send(after(down_odd, state), route([(1, 1)], 1, 0))
        if turn:
            ups[at] = dict(zip(back[1:], results[len(slots) :]))
            ups[at][back[0]] = results[len(slots) - 1]
    merged = jnp.where(is_second, merged, merged_first)
    down_odd = down_odd_pair + down_odd_first

    for k in reversed(range(len(chain) - 1)):
        target, slots = chain[k]
        arrived = send(state, route([(at, target)]))
        if k == len(chain) - 2:
            arrived, merged = lax.optimization_barrier((arrived, merged))
        at = target
        back = tuple(reversed(slots))
        results, state = segment(coupling, at, arrived, small, kept[k], maps, (), back)
        ups[at] = dict(zip(back, results))
    from_own = send(state, route([(at, 1)]))
    from_pair = send(state, route([(at, 0)]))

    mine = [jnp.zeros((rows, width), jnp.float32)] * 2
    for target, values in ups.items():
        for slot in (OWN, PAIR):
            mine[slot] = jnp.where(layer == target, values[slot], mine[slot])
    settled = mine[OWN] + send(mine[PAIR], route([(z, a) for a, z in pair_moves[1:]]))

    odd = (layer % 2).astype(jnp.int32)[None]
    last = pl.pallas_call(
        functools.partial(last_kernel, coupling, len(pair_maps)),
        out_shape=jax.ShapeDtypeStruct((rows, width), jnp.float32),
        in_specs=[SMEM] + [VMEM] * (5 + len(pair_maps)),
        out_specs=VMEM,
        compiler_params=SWEEP_PARAMS,
        cost_estimate=cost(6 * 256 * 1024 * 1024, 6 * 1024 * 1024),
    )(odd, from_pair, from_own, packed[:rows], down_odd, merged_first, *pair_maps)
    upward = jnp.where(layer < 2, last, settled)
    second_rows = send(upward[rows_here : 2 * rows_here], route(every, 0, 1))
    upward = jnp.where(is_second, second_rows, upward[:rows_here])
    return (merged[None], upward[None])


def solution(mesh):
    return jax.shard_map(
        on_device,
        mesh=mesh,
        in_specs=(
            P("layer", "box", None),
            P("layer", "box", None),
            P("layer", None, None, None),
            P("layer", None),
            P("layer", "box", None),
        ),
        out_specs=(P("layer", None, None), P("layer", "box", None)),
        check_vma=False,
    )
```

```python
import functools

import jax
import jax.numpy as jnp
from jax import lax
from jax.experimental import pallas as pl
from jax.experimental.pallas import tpu as pltpu
from jax.sharding import PartitionSpec as P

AXES = ("layer", "box")
AHEAD = 2
SMALL_AT = 0
VMEM = pl.BlockSpec(memory_space=pltpu.VMEM)
SMEM = pl.BlockSpec(memory_space=pltpu.SMEM)
PARAMS = pltpu.CompilerParams(vmem_limit_bytes=16 * 1024 * 1024)
SWEEP_PARAMS = pltpu.CompilerParams(vmem_limit_bytes=6 * 1024 * 1024)
COMBINE_PARAMS = pltpu.CompilerParams(vmem_limit_bytes=12 * 1024 * 1024)
OWN, PAIR = 0, 1


def cost(flops, moved):
    return pl.CostEstimate(flops=flops, bytes_accessed=moved, transcendentals=0)


def dot32(a, b):
    return jnp.dot(a, b, preferred_element_type=jnp.float32)


def dot32_t(a, b):
    return lax.dot_general(a, b, (((1,), (1,)), ((), ())), preferred_element_type=jnp.float32)


def minus_face(joined, face_at, inverse, right):
    face = inverse.shape[0]
    left = joined[:, face_at : face_at + face].astype(jnp.bfloat16)
    product = dot32(left, inverse).astype(jnp.bfloat16)
    return (joined - dot32(product, right)).astype(jnp.bfloat16)


def masked(values, pattern, row_at, row_count, block_at):
    width = values.shape[1]
    block = width // pattern.shape[1]
    strips = []
    for r in range(row_count // block):
        at = slice(row_at + r * block, row_at + (r + 1) * block)
        strips.append(
            jnp.concatenate(
                [
                    values[at, c * block : (c + 1) * block].astype(jnp.float32)
                    * (0.5 * pattern[block_at + r, c].astype(jnp.float32))
                    for c in range(width // block)
                ],
                axis=1,
            )
        )
    return jnp.concatenate(strips, axis=0)


def mask_kernel(pattern, values, out):
    block = values.shape[1] // pattern.shape[1]
    for r in range(values.shape[0] // block):
        out[r * block : (r + 1) * block] = masked(values, pattern, r * block, block, r).astype(
            jnp.bfloat16
        )


def leaf_kernel(first_row, is_face, pieces, other_pattern, own, other, inverse, *refs):
    refs = list(refs)
    face = inverse.shape[0]
    right = None if is_face else refs.pop(0)[...]
    block = own.shape[1] // other_pattern.shape[1]
    for i in range(own.shape[0] // face):
        at = first_row + i * face
        joined = own[i * face : (i + 1) * face].astype(jnp.float32) + masked(
            other, other_pattern, i * face, face, at // block
        )
        if right is None:
            right = joined.astype(jnp.bfloat16)
            refs[-1][...] = right
        result = minus_face(joined, 0, inverse[...], right)
        for ref, (start, size) in zip(refs, pieces):
            low, high = max(start, at), min(start + size, at + face)
            if low < high:
                ref[low - start : high - start] = result[low - at : high - at]


def leaf_combine(other_pattern, own, other, inverse, face_rows, half, pieces):
    is_face = face_rows is None
    width = own.shape[1]
    rows = own.shape[0] // 2
    face = inverse.shape[0]
    shapes = [jax.ShapeDtypeStruct((size, width), jnp.bfloat16) for _, size in pieces]
    if is_face:
        shapes.append(jax.ShapeDtypeStruct((face, width), jnp.bfloat16))
    map_spec = pl.BlockSpec((rows, width), lambda i: (half, 0))
    extra = [] if is_face else [face_rows]
    return pl.pallas_call(
        functools.partial(leaf_kernel, half * rows, is_face, pieces),
        grid=(1,),
        out_shape=shapes,
        in_specs=[SMEM, map_spec, map_spec, VMEM] + [VMEM] * len(extra),
        out_specs=[VMEM] * len(shapes),
        compiler_params=PARAMS,
        cost_estimate=cost(2 * rows * face * (width + face), 6 * rows * width),
    )(other_pattern, own, other, inverse, *extra)


def combine_kernel(face_at, is_face, with_next, whole_rows, own, other, inverse, *refs):
    refs = list(refs)
    following = refs.pop(0) if with_next else None
    joined = 0.5 * (own[...].astype(jnp.float32) + other[...].astype(jnp.float32))
    if is_face:
        right = joined.astype(jnp.bfloat16)
    else:
        right = refs.pop(0)[...]
        refs.pop(0)
    piece = minus_face(joined, face_at, inverse[...], right)
    refs[1][whole_rows, :] = piece
    if is_face:
        refs[2][...] = right
    refs[0][...] = piece
    if with_next:

        @pl.when(lax.axis_index("box") % 2 == 0)
        def _():
            refs[0][...] = following[...]


def combine(own, other, inverse, following, state, face_at, row_at):
    is_face = state is None
    rows, width = own.shape
    extra = [] if following is None else [following]
    aliases = {} if is_face else {3 + len(extra) + 1: 1}
    extra += [] if is_face else list(state)
    piece = jax.ShapeDtypeStruct((rows, width), jnp.bfloat16)
    whole = jax.ShapeDtypeStruct((width, width), jnp.bfloat16)
    result = pl.pallas_call(
        functools.partial(
            combine_kernel,
            face_at,
            is_face,
            following is not None,
            slice(row_at, row_at + rows),
        ),
        out_shape=[piece, whole] + ([piece] if is_face else []),
        in_specs=[VMEM] * (3 + len(extra)),
        out_specs=[VMEM] * (3 if is_face else 2),
        input_output_aliases=aliases,
        compiler_params=COMBINE_PARAMS,
        cost_estimate=cost(0, 0),
    )(own, other, inverse, *extra)
    return result[0], ((result[2] if is_face else state[0]), result[1])


def spread(pieces, rows):
    return jnp.concatenate([dot32_t(rows, piece[...]) for piece in pieces], axis=1)


def gather_sum(pieces, rows):
    at, total = 0, None
    for piece in pieces:
        size = piece.shape[0]
        term = dot32(rows[:, at : at + size], piece[...])
        total = term if total is None else total + term
        at += size
    return total


def lanes_at(rows, index_row):
    lanes = 128
    count, width = rows.shape
    parts = [rows[:, at : at + lanes] for at in range(0, width, lanes)]
    outs = []
    for at in range(0, width, lanes):
        index = jnp.broadcast_to(index_row[:, at : at + lanes].astype(jnp.int32), (count, lanes))
        lane, part = index % lanes, index // lanes
        total = jnp.zeros((count, lanes), rows.dtype)
        for k, values in enumerate(parts):
            total = jnp.where(part == k, jnp.take_along_axis(values, lane, axis=1), total)
        outs.append(total)
    return jnp.concatenate(outs, axis=1)


def segment_kernel(coupling, at, pieces_of, down_steps, up_steps, *refs):
    @pl.when(lax.axis_index("layer") == at)
    def _():
        run_segment(coupling, pieces_of, down_steps, up_steps, *refs)


def run_segment(coupling, pieces_of, down_steps, up_steps, *refs):
    refs = list(refs)
    state = refs.pop(0)[...]
    maps, downs = {}, {}
    operands = []
    for slot in down_steps:
        operands.append(refs.pop(0))
        maps[slot] = [refs.pop(0) for _ in range(pieces_of[slot])]
    for slot in up_steps:
        if slot not in down_steps:
            downs[slot] = refs.pop(0)[...]
            maps[slot] = [refs.pop(0) for _ in range(pieces_of[slot])]
    for slot, packed in zip(down_steps, operands):
        count = state.shape[0]
        moved = lanes_at(state.astype(jnp.float32), packed[count:]).astype(jnp.bfloat16)
        downs[slot] = packed[:count] + coupling * spread(maps[slot], moved)
        state = downs[slot].astype(jnp.bfloat16)
        refs.pop(0)[...] = downs[slot]
    for slot in up_steps:
        value = downs[slot] + coupling * gather_sum(maps[slot], state)
        state = value.astype(jnp.bfloat16)
        refs.pop(0)[...] = value
    refs.pop(0)[...] = state


def segment(coupling, at, arrived, packed, downs, maps, down_steps, up_steps):
    operands = [arrived]
    for slot in down_steps:
        operands += [packed[slot], *maps[slot]]
    for slot in up_steps:
        if slot not in down_steps:
            operands += [downs[slot], *maps[slot]]
    rows = jax.ShapeDtypeStruct(arrived.shape, jnp.float32)
    steps = len(down_steps) + len(up_steps)
    results = pl.pallas_call(
        functools.partial(
            segment_kernel, coupling, at, [len(entry) for entry in maps], down_steps, up_steps
        ),
        out_shape=[rows] * steps + [jax.ShapeDtypeStruct(arrived.shape, jnp.bfloat16)],
        in_specs=[VMEM] * len(operands),
        out_specs=[VMEM] * (steps + 1),
        compiler_params=SWEEP_PARAMS,
        cost_estimate=cost(steps * 2 * 256 * 1024 * 1024, steps * 2 * 1024 * 1024),
    )(*operands)
    return results[:-1], results[-1]


def last_kernel(coupling, count, odd, from_pair, from_own, source, down_odd, *refs):
    own, pair, out = refs[:1], refs[1 : 1 + count], refs[1 + count]
    total = gather_sum(pair, from_pair[...]) + gather_sum(own, from_own[...])
    up_odd = down_odd[...] + coupling * total
    up_even = source[...] + coupling * gather_sum(own, up_odd.astype(jnp.bfloat16))
    out[...] = jnp.where(odd[0] == 1, up_odd, up_even)


def on_device(box_maps, block_pattern, face_inverses, index_map, sources):
    boxes = lax.axis_size("box")
    layers = lax.axis_size("layer")
    coupling = float(boxes) ** 0.5
    levels = boxes.bit_length() - 1
    face = face_inverses.shape[2]
    width = box_maps.shape[2]
    rows_here = sources.shape[1]
    position = lax.axis_index("box")
    layer = lax.axis_index("layer")
    is_second = position % 2 == 1

    chain = [(layer_at, (OWN, PAIR)) for layer_at in range(2, layers, 2)]
    pair_moves = [(layer_at + 1, layer_at) for layer_at in range(0, layers, 2)]

    def route(moves, source_core=0, target_core=0):
        return [
            (a * boxes + b + source_core, z * boxes + b + target_core)
            for a, z in moves
            for b in range(0, boxes, 2)
        ]

    def over_box(change, starts):
        return [(i * boxes + b, i * boxes + (b ^ change)) for i in range(layers) for b in starts]

    def send(value, pairs_of_devices):
        return lax.ppermute(value, AXES, pairs_of_devices)

    def after(value, *others):
        return lax.optimization_barrier((value, *others))[0]

    every = [(i, i) for i in range(layers)]

    raw = box_maps[0]
    pattern = block_pattern[0]
    raw_other = send(raw, over_box(1, range(boxes)))
    pattern_other = send(pattern, over_box(1, range(boxes)))
    other_sources = send(sources[0], over_box(1, range(boxes)))
    own_half = pl.pallas_call(
        mask_kernel,
        out_shape=jax.ShapeDtypeStruct(raw.shape, jnp.bfloat16),
        in_specs=[SMEM, VMEM],
        out_specs=VMEM,
        compiler_params=PARAMS,
        cost_estimate=cost(width * width, 4 * width * width),
    )(pattern, raw)

    def inverse_of(level):
        node = (boxes >> (level + 1)) - 1 + (position >> (level + 1))
        return lax.dynamic_index_in_dim(face_inverses[0], node, 0, keepdims=False).astype(
            jnp.bfloat16
        )

    rows = -(-2 * rows_here // 8) * 8
    packed = jnp.concatenate(
        [
            jnp.where(is_second, other_sources, sources[0]),
            jnp.where(is_second, sources[0], other_sources),
            jnp.zeros((rows - 2 * rows_here, width), jnp.float32),
            index_map.astype(jnp.float32),
        ],
        axis=0,
    )

    pieces = tuple((at, face) for at in range(0, width, face))
    upper = tuple(piece for piece in pieces if piece[0] < width // 2)
    lower = tuple(piece for piece in pieces if piece[0] >= width // 2)
    inverse = inverse_of(0)
    top = leaf_combine(pattern_other, own_half, raw_other, inverse, None, 0, upper)
    bottom = leaf_combine(pattern_other, own_half, raw_other, inverse, top[-1], 1, lower)
    current = dict(zip(upper + lower, [*top[:-1], *bottom]))

    for level in range(1, levels):
        final = level == levels - 1
        change = 1 << level
        inverse = inverse_of(level)
        order = sorted(pieces, key=lambda piece: (piece[0] != level * face, piece[0]))
        received = {}
        state = None
        if not final:
            for piece in order:
                received[piece] = send(current[piece], over_box(change, range(boxes)))
            renewed = {}
            for piece in order:
                renewed[piece], state = combine(
                    current[piece],
                    received[piece],
                    inverse,
                    None,
                    state,
                    level * face,
                    piece[0],
                )
            current = renewed
            continue
        over = over_box(change ^ 1, range(0, boxes, 2))
        forward = route(pair_moves, 1, 0)
        for piece in order[:AHEAD]:
            received[piece] = send(current[piece], over)
        pair_pieces = {}
        for k, piece in enumerate(order):
            following = order[k + AHEAD] if k + AHEAD < len(order) else None
            other = received[piece]
            if k == SMALL_AT + 2:
                other = after(other, pair_packed)
            payload, state = combine(
                current[piece],
                other,
                inverse,
                None if following is None else current[following],
                state,
                level * face,
                piece[0],
            )
            pair_pieces[piece] = send(payload, forward + ([] if following is None else over))
            if following is not None:
                received[following] = pair_pieces[piece]
            if k == SMALL_AT:
                sendable = after(packed, payload)
                pair_packed = send(sendable, route(pair_moves[1:]) + route([(0, 1)], 1, 1))
    merged = state[1]
    small = [packed, pair_packed]
    pair_maps = [pair_pieces[piece] for piece in pieces]

    first = pair_packed[:rows].astype(jnp.bfloat16)
    (down_odd,), state = segment(
        coupling, 1, first, small, {}, [[merged], pair_maps], (OWN,), ()
    )
    merged_first = send(merged, route(every, 1, 0))
    maps = [[merged_first], pair_maps]
    at, core = 1, 1
    kept = []
    ups = {}
    for k, (target, slots) in enumerate(chain):
        arrived = send(state, route([(at, target)], core, 0))
        at, core = target, 0
        turn = k == len(chain) - 1
        back = tuple(reversed(slots))
        results, state = segment(
            coupling, at, arrived, small, {}, maps, slots, back[1:] if turn else ()
        )
        kept.append(dict(zip(slots, results)))
        if k == 0:
            down_odd_pair = send(after(down_odd, state), route([(1, 0)], 1, 0))
            down_odd_first = send(after(down_odd, state), route([(1, 1)], 1, 0))
        if turn:
            ups[at] = dict(zip(back[1:], results[len(slots) :]))
            ups[at][back[0]] = results[len(slots) - 1]
    merged = jnp.where(is_second, merged, merged_first)
    down_odd = down_odd_pair + down_odd_first

    for k in reversed(range(len(chain) - 1)):
        target, slots = chain[k]
        arrived = send(state, route([(at, target)]))
        if k == len(chain) - 2:
            arrived, merged = lax.optimization_barrier((arrived, merged))
        at = target
        back = tuple(reversed(slots))
        results, state = segment(coupling, at, arrived, small, kept[k], maps, (), back)
        ups[at] = dict(zip(back, results))
    from_own = send(state, route([(at, 1)]))
    from_pair = send(state, route([(at, 0)]))

    mine = [jnp.zeros((rows, width), jnp.float32)] * 2
    for target, values in ups.items():
        for slot in (OWN, PAIR):
            mine[slot] = jnp.where(layer == target, values[slot], mine[slot])
    settled = mine[OWN] + send(mine[PAIR], route([(z, a) for a, z in pair_moves[1:]]))

    odd = (layer % 2).astype(jnp.int32)[None]
    last = pl.pallas_call(
        functools.partial(last_kernel, coupling, len(pair_maps)),
        out_shape=jax.ShapeDtypeStruct((rows, width), jnp.float32),
        in_specs=[SMEM] + [VMEM] * (5 + len(pair_maps)),
        out_specs=VMEM,
        compiler_params=SWEEP_PARAMS,
        cost_estimate=cost(6 * 256 * 1024 * 1024, 6 * 1024 * 1024),
    )(odd, from_pair, from_own, packed[:rows], down_odd, merged_first, *pair_maps)
    upward = jnp.where(layer < 2, last, settled)
    second_rows = send(upward[rows_here : 2 * rows_here], route(every, 0, 1))
    upward = jnp.where(is_second, second_rows, upward[:rows_here])
    return (merged[None], upward[None])


def solution(mesh):
    return jax.shard_map(
        on_device,
        mesh=mesh,
        in_specs=(
            P("layer", "box", None),
            P("layer", "box", None),
            P("layer", None, None, None),
            P("layer", None),
            P("layer", "box", None),
        ),
        out_specs=(P("layer", None, None), P("layer", "box", None)),
        check_vma=False,
    )
```

```python
import functools

import jax
import jax.numpy as jnp
from jax import lax
from jax.experimental import pallas as pl
from jax.experimental.pallas import tpu as pltpu
from jax.sharding import PartitionSpec as P

AXES = ("layer", "box")
AHEAD = 2
SMALL_AT = 0
VMEM = pl.BlockSpec(memory_space=pltpu.VMEM)
SMEM = pl.BlockSpec(memory_space=pltpu.SMEM)
PARAMS = pltpu.CompilerParams(vmem_limit_bytes=16 * 1024 * 1024)
SWEEP_PARAMS = pltpu.CompilerParams(vmem_limit_bytes=6 * 1024 * 1024)
COMBINE_PARAMS = pltpu.CompilerParams(vmem_limit_bytes=12 * 1024 * 1024)
OWN, PAIR = 0, 1


def cost(flops, moved):
    return pl.CostEstimate(flops=flops, bytes_accessed=moved, transcendentals=0)


def dot32(a, b):
    return jnp.dot(a, b, preferred_element_type=jnp.float32)


def dot32_t(a, b):
    return lax.dot_general(a, b, (((1,), (1,)), ((), ())), preferred_element_type=jnp.float32)


def minus_face(joined, face_at, inverse, right):
    face = inverse.shape[0]
    left = joined[:, face_at : face_at + face].astype(jnp.bfloat16)
    product = dot32(left, inverse).astype(jnp.bfloat16)
    return (joined - dot32(product, right)).astype(jnp.bfloat16)


def masked(values, pattern, row_at, row_count, block_at):
    width = values.shape[1]
    block = width // pattern.shape[1]
    strips = []
    for r in range(row_count // block):
        at = slice(row_at + r * block, row_at + (r + 1) * block)
        strips.append(
            jnp.concatenate(
                [
                    values[at, c * block : (c + 1) * block].astype(jnp.float32)
                    * (0.5 * pattern[block_at + r, c].astype(jnp.float32))
                    for c in range(width // block)
                ],
                axis=1,
            )
        )
    return jnp.concatenate(strips, axis=0)


def mask_kernel(pattern, values, out):
    block = values.shape[1] // pattern.shape[1]
    for r in range(values.shape[0] // block):
        out[r * block : (r + 1) * block] = masked(values, pattern, r * block, block, r).astype(
            jnp.bfloat16
        )


def leaf_kernel(first_row, is_face, pieces, other_pattern, own, other, inverse, *refs):
    refs = list(refs)
    face = inverse.shape[0]
    right = None if is_face else refs.pop(0)[...]
    block = own.shape[1] // other_pattern.shape[1]
    for i in range(own.shape[0] // face):
        at = first_row + i * face
        joined = own[i * face : (i + 1) * face].astype(jnp.float32) + masked(
            other, other_pattern, i * face, face, at // block
        )
        if right is None:
            right = joined.astype(jnp.bfloat16)
            refs[-1][...] = right
        result = minus_face(joined, 0, inverse[...], right)
        for ref, (start, size) in zip(refs, pieces):
            low, high = max(start, at), min(start + size, at + face)
            if low < high:
                ref[low - start : high - start] = result[low - at : high - at]


def leaf_combine(other_pattern, own, other, inverse, face_rows, half, pieces):
    is_face = face_rows is None
    width = own.shape[1]
    rows = own.shape[0] // 2
    face = inverse.shape[0]
    shapes = [jax.ShapeDtypeStruct((size, width), jnp.bfloat16) for _, size in pieces]
    if is_face:
        shapes.append(jax.ShapeDtypeStruct((face, width), jnp.bfloat16))
    map_spec = pl.BlockSpec((rows, width), lambda i: (half, 0))
    extra = [] if is_face else [face_rows]
    return pl.pallas_call(
        functools.partial(leaf_kernel, half * rows, is_face, pieces),
        grid=(1,),
        out_shape=shapes,
        in_specs=[SMEM, map_spec, map_spec, VMEM] + [VMEM] * len(extra),
        out_specs=[VMEM] * len(shapes),
        compiler_params=PARAMS,
        cost_estimate=cost(2 * rows * face * (width + face), 6 * rows * width),
    )(other_pattern, own, other, inverse, *extra)


def combine_kernel(face_at, is_face, with_next, whole_rows, own, other, inverse, *refs):
    refs = list(refs)
    following = refs.pop(0) if with_next else None
    joined = 0.5 * (own[...].astype(jnp.float32) + other[...].astype(jnp.float32))
    if is_face:
        right = joined.astype(jnp.bfloat16)
    else:
        right = refs.pop(0)[...]
        refs.pop(0)
    piece = minus_face(joined, face_at, inverse[...], right)
    refs[1][whole_rows, :] = piece
    if is_face:
        refs[2][...] = right
    refs[0][...] = piece
    if with_next:

        @pl.when(lax.axis_index("box") % 2 == 0)
        def _():
            refs[0][...] = following[...]


def combine(own, other, inverse, following, state, face_at, row_at):
    is_face = state is None
    rows, width = own.shape
    extra = [] if following is None else [following]
    aliases = {} if is_face else {3 + len(extra) + 1: 1}
    extra += [] if is_face else list(state)
    piece = jax.ShapeDtypeStruct((rows, width), jnp.bfloat16)
    whole = jax.ShapeDtypeStruct((width, width), jnp.bfloat16)
    result = pl.pallas_call(
        functools.partial(
            combine_kernel,
            face_at,
            is_face,
            following is not None,
            slice(row_at, row_at + rows),
        ),
        out_shape=[piece, whole] + ([piece] if is_face else []),
        in_specs=[VMEM] * (3 + len(extra)),
        out_specs=[VMEM] * (3 if is_face else 2),
        input_output_aliases=aliases,
        compiler_params=COMBINE_PARAMS,
        cost_estimate=cost(0, 0),
    )(own, other, inverse, *extra)
    return result[0], ((result[2] if is_face else state[0]), result[1])


def spread(pieces, rows):
    return jnp.concatenate([dot32_t(rows, piece[...]) for piece in pieces], axis=1)


def gather_sum(pieces, rows):
    at, total = 0, None
    for piece in pieces:
        size = piece.shape[0]
        term = dot32(rows[:, at : at + size], piece[...])
        total = term if total is None else total + term
        at += size
    return total


def lanes_at(rows, index_row):
    lanes = 128
    count, width = rows.shape
    parts = [rows[:, at : at + lanes] for at in range(0, width, lanes)]
    outs = []
    for at in range(0, width, lanes):
        index = jnp.broadcast_to(index_row[:, at : at + lanes].astype(jnp.int32), (count, lanes))
        lane, part = index % lanes, index // lanes
        total = jnp.zeros((count, lanes), rows.dtype)
        for k, values in enumerate(parts):
            total = jnp.where(part == k, jnp.take_along_axis(values, lane, axis=1), total)
        outs.append(total)
    return jnp.concatenate(outs, axis=1)


def segment_kernel(coupling, at, pieces_of, down_steps, up_steps, *refs):
    @pl.when(lax.axis_index("layer") == at)
    def _():
        run_segment(coupling, pieces_of, down_steps, up_steps, *refs)


def run_segment(coupling, pieces_of, down_steps, up_steps, *refs):
    refs = list(refs)
    state = refs.pop(0)[...]
    maps, downs = {}, {}
    operands = []
    for slot in down_steps:
        operands.append(refs.pop(0))
        maps[slot] = [refs.pop(0) for _ in range(pieces_of[slot])]
    for slot in up_steps:
        if slot not in down_steps:
            downs[slot] = refs.pop(0)[...]
            maps[slot] = [refs.pop(0) for _ in range(pieces_of[slot])]
    for slot, packed in zip(down_steps, operands):
        count = state.shape[0]
        moved = lanes_at(state.astype(jnp.float32), packed[count:]).astype(jnp.bfloat16)
        downs[slot] = packed[:count] + coupling * spread(maps[slot], moved)
        state = downs[slot].astype(jnp.bfloat16)
        refs.pop(0)[...] = downs[slot]
    for slot in up_steps:
        value = downs[slot] + coupling * gather_sum(maps[slot], state)
        state = value.astype(jnp.bfloat16)
        refs.pop(0)[...] = value
    refs.pop(0)[...] = state


def segment(coupling, at, arrived, packed, downs, maps, down_steps, up_steps):
    operands = [arrived]
    for slot in down_steps:
        operands += [packed[slot], *maps[slot]]
    for slot in up_steps:
        if slot not in down_steps:
            operands += [downs[slot], *maps[slot]]
    rows = jax.ShapeDtypeStruct(arrived.shape, jnp.float32)
    steps = len(down_steps) + len(up_steps)
    results = pl.pallas_call(
        functools.partial(
            segment_kernel, coupling, at, [len(entry) for entry in maps], down_steps, up_steps
        ),
        out_shape=[rows] * steps + [jax.ShapeDtypeStruct(arrived.shape, jnp.bfloat16)],
        in_specs=[VMEM] * len(operands),
        out_specs=[VMEM] * (steps + 1),
        compiler_params=SWEEP_PARAMS,
        cost_estimate=cost(steps * 2 * 256 * 1024 * 1024, steps * 2 * 1024 * 1024),
    )(*operands)
    return results[:-1], results[-1]


def last_kernel(coupling, count, from_pair, from_own, source, down_odd, *refs):
    own, pair, out = refs[:1], refs[1 : 1 + count], refs[1 + count]
    layer = lax.axis_index("layer")

    @pl.when(layer == 0)
    def _():
        up_odd = down_odd[...] + coupling * gather_sum(pair, from_pair[...])
        out[...] = source[...] + coupling * gather_sum(own, up_odd.astype(jnp.bfloat16))

    @pl.when(layer == 1)
    def _():
        out[...] = down_odd[...] + coupling * gather_sum(own, from_own[...])


def on_device(box_maps, block_pattern, face_inverses, index_map, sources):
    boxes = lax.axis_size("box")
    layers = lax.axis_size("layer")
    coupling = float(boxes) ** 0.5
    levels = boxes.bit_length() - 1
    face = face_inverses.shape[2]
    width = box_maps.shape[2]
    rows_here = sources.shape[1]
    position = lax.axis_index("box")
    layer = lax.axis_index("layer")
    is_second = position % 2 == 1

    chain = [(layer_at, (OWN, PAIR)) for layer_at in range(2, layers, 2)]
    pair_moves = [(layer_at + 1, layer_at) for layer_at in range(0, layers, 2)]

    def route(moves, source_core=0, target_core=0):
        return [
            (a * boxes + b + source_core, z * boxes + b + target_core)
            for a, z in moves
            for b in range(0, boxes, 2)
        ]

    def over_box(change, starts):
        return [(i * boxes + b, i * boxes + (b ^ change)) for i in range(layers) for b in starts]

    def send(value, pairs_of_devices):
        return lax.ppermute(value, AXES, pairs_of_devices)

    def after(value, *others):
        return lax.optimization_barrier((value, *others))[0]

    every = [(i, i) for i in range(layers)]

    raw = box_maps[0]
    pattern = block_pattern[0]
    raw_other = send(raw, over_box(1, range(boxes)))
    pattern_other = send(pattern, over_box(1, range(boxes)))
    other_sources = send(sources[0], over_box(1, range(boxes)))
    own_half = pl.pallas_call(
        mask_kernel,
        out_shape=jax.ShapeDtypeStruct(raw.shape, jnp.bfloat16),
        in_specs=[SMEM, VMEM],
        out_specs=VMEM,
        compiler_params=PARAMS,
        cost_estimate=cost(width * width, 4 * width * width),
    )(pattern, raw)

    def inverse_of(level):
        node = (boxes >> (level + 1)) - 1 + (position >> (level + 1))
        return lax.dynamic_index_in_dim(face_inverses[0], node, 0, keepdims=False).astype(
            jnp.bfloat16
        )

    rows = -(-2 * rows_here // 8) * 8
    packed = jnp.concatenate(
        [
            jnp.where(is_second, other_sources, sources[0]),
            jnp.where(is_second, sources[0], other_sources),
            jnp.zeros((rows - 2 * rows_here, width), jnp.float32),
            index_map.astype(jnp.float32),
        ],
        axis=0,
    )

    pieces = tuple((at, face) for at in range(0, width, face))
    upper = tuple(piece for piece in pieces if piece[0] < width // 2)
    lower = tuple(piece for piece in pieces if piece[0] >= width // 2)
    inverse = inverse_of(0)
    top = leaf_combine(pattern_other, own_half, raw_other, inverse, None, 0, upper)
    bottom = leaf_combine(pattern_other, own_half, raw_other, inverse, top[-1], 1, lower)
    current = dict(zip(upper + lower, [*top[:-1], *bottom]))

    for level in range(1, levels):
        final = level == levels - 1
        change = 1 << level
        inverse = inverse_of(level)
        order = sorted(pieces, key=lambda piece: (piece[0] != level * face, piece[0]))
        received = {}
        state = None
        if not final:
            for piece in order:
                received[piece] = send(current[piece], over_box(change, range(boxes)))
            renewed = {}
            for piece in order:
                renewed[piece], state = combine(
                    current[piece],
                    received[piece],
                    inverse,
                    None,
                    state,
                    level * face,
                    piece[0],
                )
            current = renewed
            continue
        over = over_box(change ^ 1, range(0, boxes, 2))
        forward = route(pair_moves, 1, 0)
        for piece in order[:AHEAD]:
            received[piece] = send(current[piece], over)
        pair_pieces = {}
        for k, piece in enumerate(order):
            following = order[k + AHEAD] if k + AHEAD < len(order) else None
            other = received[piece]
            if k == SMALL_AT + 2:
                other = after(other, pair_packed)
            if k > AHEAD:
                other = after(other, pair_pieces[order[k - 1]])
            payload, state = combine(
                current[piece],
                other,
                inverse,
                None if following is None else current[following],
                state,
                level * face,
                piece[0],
            )
            pair_pieces[piece] = send(payload, forward + ([] if following is None else over))
            if following is not None:
                received[following] = pair_pieces[piece]
            if k == SMALL_AT:
                sendable = after(packed, payload)
                pair_packed = send(sendable, route(pair_moves[1:]) + route([(0, 1)], 1, 1))
    merged = state[1]
    small = [packed, pair_packed]
    pair_maps = [pair_pieces[piece] for piece in pieces]

    first = pair_packed[:rows].astype(jnp.bfloat16)
    (down_odd,), state = segment(
        coupling, 1, first, small, {}, [[merged], pair_maps], (OWN,), ()
    )
    merged_first = send(after(merged, state), route(every, 1, 0))
    maps = [[merged_first], pair_maps]
    at, core = 1, 1
    kept = []
    ups = {}
    for k, (target, slots) in enumerate(chain):
        arrived = send(state, route([(at, target)], core, 0))
        at, core = target, 0
        turn = k == len(chain) - 1
        back = tuple(reversed(slots))
        results, state = segment(
            coupling, at, arrived, small, {}, maps, slots, back[1:] if turn else ()
        )
        kept.append(dict(zip(slots, results)))
        if k == 0:
            down_odd_pair = send(after(down_odd, state), route([(1, 0)], 1, 0))
            down_odd_first = send(after(down_odd, state), route([(1, 1)], 1, 0))
        if turn:
            ups[at] = dict(zip(back[1:], results[len(slots) :]))
            ups[at][back[0]] = results[len(slots) - 1]
    merged = jnp.where(is_second, merged, merged_first)
    down_odd = down_odd_pair + down_odd_first

    for k in reversed(range(len(chain) - 1)):
        target, slots = chain[k]
        arrived = send(state, route([(at, target)]))
        if k == len(chain) - 2:
            arrived, merged = lax.optimization_barrier((arrived, merged))
        at = target
        back = tuple(reversed(slots))
        results, state = segment(coupling, at, arrived, small, kept[k], maps, (), back)
        ups[at] = dict(zip(back, results))
    from_own = send(state, route([(at, 1)]))
    from_pair = send(state, route([(at, 0)]))

    mine = [jnp.zeros((rows, width), jnp.float32)] * 2
    for target, values in ups.items():
        for slot in (OWN, PAIR):
            mine[slot] = jnp.where(layer == target, values[slot], mine[slot])
    settled = mine[OWN] + send(mine[PAIR], route([(z, a) for a, z in pair_moves[1:]]))

    last = pl.pallas_call(
        functools.partial(last_kernel, coupling, len(pair_maps)),
        out_shape=jax.ShapeDtypeStruct((rows, width), jnp.float32),
        in_specs=[VMEM] * (5 + len(pair_maps)),
        out_specs=VMEM,
        compiler_params=SWEEP_PARAMS,
        cost_estimate=cost(6 * 256 * 1024 * 1024, 6 * 1024 * 1024),
    )(from_pair, from_own, packed[:rows], down_odd, merged_first, *pair_maps)
    upward = jnp.where(layer < 2, last, settled)
    second_rows = send(upward[rows_here : 2 * rows_here], route(every, 0, 1))
    upward = jnp.where(is_second, second_rows, upward[:rows_here])
    return (merged[None], upward[None])


def solution(mesh):
    return jax.shard_map(
        on_device,
        mesh=mesh,
        in_specs=(
            P("layer", "box", None),
            P("layer", "box", None),
            P("layer", None, None, None),
            P("layer", None),
            P("layer", "box", None),
        ),
        out_specs=(P("layer", None, None), P("layer", "box", None)),
        check_vma=False,
    )
```

```python
import functools

import jax
import jax.numpy as jnp
from jax import lax
from jax.experimental import pallas as pl
from jax.experimental.pallas import tpu as pltpu
from jax.sharding import PartitionSpec as P

AXES = ("layer", "box")
AHEAD = 2
SMALL_AT = 0
VMEM = pl.BlockSpec(memory_space=pltpu.VMEM)
SMEM = pl.BlockSpec(memory_space=pltpu.SMEM)
PARAMS = pltpu.CompilerParams(vmem_limit_bytes=16 * 1024 * 1024)
SWEEP_PARAMS = pltpu.CompilerParams(vmem_limit_bytes=6 * 1024 * 1024)
COMBINE_PARAMS = pltpu.CompilerParams(vmem_limit_bytes=12 * 1024 * 1024)
OWN, PAIR = 0, 1


def cost(flops, moved):
    return pl.CostEstimate(flops=flops, bytes_accessed=moved, transcendentals=0)


def dot32(a, b):
    return jnp.dot(a, b, preferred_element_type=jnp.float32)


def dot32_t(a, b):
    return lax.dot_general(a, b, (((1,), (1,)), ((), ())), preferred_element_type=jnp.float32)


def minus_face(joined, face_at, inverse, right):
    face = inverse.shape[0]
    left = joined[:, face_at : face_at + face].astype(jnp.bfloat16)
    product = dot32(left, inverse).astype(jnp.bfloat16)
    return (joined - dot32(product, right)).astype(jnp.bfloat16)


def masked(values, pattern, row_at, row_count, block_at):
    width = values.shape[1]
    block = width // pattern.shape[1]
    strips = []
    for r in range(row_count // block):
        at = slice(row_at + r * block, row_at + (r + 1) * block)
        strips.append(
            jnp.concatenate(
                [
                    values[at, c * block : (c + 1) * block].astype(jnp.float32)
                    * (0.5 * pattern[block_at + r, c].astype(jnp.float32))
                    for c in range(width // block)
                ],
                axis=1,
            )
        )
    return jnp.concatenate(strips, axis=0)


def mask_kernel(pattern, values, out):
    block = values.shape[1] // pattern.shape[1]
    for r in range(values.shape[0] // block):
        out[r * block : (r + 1) * block] = masked(values, pattern, r * block, block, r).astype(
            jnp.bfloat16
        )


def leaf_kernel(first_row, is_face, pieces, other_pattern, own, other, inverse, *refs):
    refs = list(refs)
    face = inverse.shape[0]
    right = None if is_face else refs.pop(0)[...]
    block = own.shape[1] // other_pattern.shape[1]
    for i in range(own.shape[0] // face):
        at = first_row + i * face
        joined = own[i * face : (i + 1) * face].astype(jnp.float32) + masked(
            other, other_pattern, i * face, face, at // block
        )
        if right is None:
            right = joined.astype(jnp.bfloat16)
            refs[-1][...] = right
        result = minus_face(joined, 0, inverse[...], right)
        for ref, (start, size) in zip(refs, pieces):
            low, high = max(start, at), min(start + size, at + face)
            if low < high:
                ref[low - start : high - start] = result[low - at : high - at]


def leaf_combine(other_pattern, own, other, inverse, face_rows, half, pieces):
    is_face = face_rows is None
    width = own.shape[1]
    rows = own.shape[0] // 2
    face = inverse.shape[0]
    shapes = [jax.ShapeDtypeStruct((size, width), jnp.bfloat16) for _, size in pieces]
    if is_face:
        shapes.append(jax.ShapeDtypeStruct((face, width), jnp.bfloat16))
    map_spec = pl.BlockSpec((rows, width), lambda i: (half, 0))
    extra = [] if is_face else [face_rows]
    return pl.pallas_call(
        functools.partial(leaf_kernel, half * rows, is_face, pieces),
        grid=(1,),
        out_shape=shapes,
        in_specs=[SMEM, map_spec, map_spec, VMEM] + [VMEM] * len(extra),
        out_specs=[VMEM] * len(shapes),
        compiler_params=PARAMS,
        cost_estimate=cost(2 * rows * face * (width + face), 6 * rows * width),
    )(other_pattern, own, other, inverse, *extra)


def combine_kernel(face_at, is_face, with_next, whole_rows, done, own, other, inverse, *refs):
    refs = list(refs)
    following = refs.pop(0) if with_next else None
    joined = 0.5 * (own[...].astype(jnp.float32) + other[...].astype(jnp.float32))
    if is_face:
        right = joined.astype(jnp.bfloat16)
    else:
        right = refs.pop(0)[...]
        before = refs.pop(0)
        for rows in done:
            refs[1][rows, :] = before[rows, :]
    piece = minus_face(joined, face_at, inverse[...], right)
    refs[1][whole_rows, :] = piece
    if is_face:
        refs[2][...] = right
    refs[0][...] = piece
    if with_next:

        @pl.when(lax.axis_index("box") % 2 == 0)
        def _():
            refs[0][...] = following[...]


def combine(own, other, inverse, following, state, face_at, row_at, done):
    is_face = state is None
    rows, width = own.shape
    extra = [] if following is None else [following]
    aliases = {} if is_face else {3 + len(extra) + 1: 1}
    extra += [] if is_face else list(state)
    piece = jax.ShapeDtypeStruct((rows, width), jnp.bfloat16)
    whole = jax.ShapeDtypeStruct((width, width), jnp.bfloat16)
    result = pl.pallas_call(
        functools.partial(
            combine_kernel,
            face_at,
            is_face,
            following is not None,
            slice(row_at, row_at + rows),
            [slice(at, at + size) for at, size in done],
        ),
        out_shape=[piece, whole] + ([piece] if is_face else []),
        in_specs=[VMEM] * (3 + len(extra)),
        out_specs=[VMEM] * (3 if is_face else 2),
        input_output_aliases=aliases,
        compiler_params=COMBINE_PARAMS,
        cost_estimate=cost(0, 0),
    )(own, other, inverse, *extra)
    return result[0], ((result[2] if is_face else state[0]), result[1])


def spread(pieces, rows):
    return jnp.concatenate([dot32_t(rows, piece[...]) for piece in pieces], axis=1)


def gather_sum(pieces, rows):
    at, total = 0, None
    for piece in pieces:
        size = piece.shape[0]
        term = dot32(rows[:, at : at + size], piece[...])
        total = term if total is None else total + term
        at += size
    return total


def lanes_at(rows, index_row):
    lanes = 128
    count, width = rows.shape
    parts = [rows[:, at : at + lanes] for at in range(0, width, lanes)]
    outs = []
    for at in range(0, width, lanes):
        index = jnp.broadcast_to(index_row[:, at : at + lanes].astype(jnp.int32), (count, lanes))
        lane, part = index % lanes, index // lanes
        total = jnp.zeros((count, lanes), rows.dtype)
        for k, values in enumerate(parts):
            total = jnp.where(part == k, jnp.take_along_axis(values, lane, axis=1), total)
        outs.append(total)
    return jnp.concatenate(outs, axis=1)


def segment_kernel(coupling, at, pieces_of, down_steps, up_steps, *refs):
    @pl.when(lax.axis_index("layer") == at)
    def _():
        run_segment(coupling, pieces_of, down_steps, up_steps, *refs)


def run_segment(coupling, pieces_of, down_steps, up_steps, *refs):
    refs = list(refs)
    state = refs.pop(0)[...]
    maps, downs = {}, {}
    operands = []
    for slot in down_steps:
        operands.append(refs.pop(0))
        maps[slot] = [refs.pop(0) for _ in range(pieces_of[slot])]
    for slot in up_steps:
        if slot not in down_steps:
            downs[slot] = refs.pop(0)[...]
            maps[slot] = [refs.pop(0) for _ in range(pieces_of[slot])]
    for slot, packed in zip(down_steps, operands):
        count = state.shape[0]
        moved = lanes_at(state.astype(jnp.float32), packed[count:]).astype(jnp.bfloat16)
        downs[slot] = packed[:count] + coupling * spread(maps[slot], moved)
        state = downs[slot].astype(jnp.bfloat16)
        refs.pop(0)[...] = downs[slot]
    for slot in up_steps:
        value = downs[slot] + coupling * gather_sum(maps[slot], state)
        state = value.astype(jnp.bfloat16)
        refs.pop(0)[...] = value
    refs.pop(0)[...] = state


def segment(coupling, at, arrived, packed, downs, maps, down_steps, up_steps):
    operands = [arrived]
    for slot in down_steps:
        operands += [packed[slot], *maps[slot]]
    for slot in up_steps:
        if slot not in down_steps:
            operands += [downs[slot], *maps[slot]]
    rows = jax.ShapeDtypeStruct(arrived.shape, jnp.float32)
    steps = len(down_steps) + len(up_steps)
    results = pl.pallas_call(
        functools.partial(
            segment_kernel, coupling, at, [len(entry) for entry in maps], down_steps, up_steps
        ),
        out_shape=[rows] * steps + [jax.ShapeDtypeStruct(arrived.shape, jnp.bfloat16)],
        in_specs=[VMEM] * len(operands),
        out_specs=[VMEM] * (steps + 1),
        compiler_params=SWEEP_PARAMS,
        cost_estimate=cost(steps * 2 * 256 * 1024 * 1024, steps * 2 * 1024 * 1024),
    )(*operands)
    return results[:-1], results[-1]


def last_kernel(coupling, count, from_pair, from_own, source, down_odd, *refs):
    own, pair, out = refs[:1], refs[1 : 1 + count], refs[1 + count]
    layer = lax.axis_index("layer")

    @pl.when(layer == 0)
    def _():
        up_odd = down_odd[...] + coupling * gather_sum(pair, from_pair[...])
        out[...] = source[...] + coupling * gather_sum(own, up_odd.astype(jnp.bfloat16))

    @pl.when(layer == 1)
    def _():
        out[...] = down_odd[...] + coupling * gather_sum(own, from_own[...])


def on_device(box_maps, block_pattern, face_inverses, index_map, sources):
    boxes = lax.axis_size("box")
    layers = lax.axis_size("layer")
    coupling = float(boxes) ** 0.5
    levels = boxes.bit_length() - 1
    face = face_inverses.shape[2]
    width = box_maps.shape[2]
    rows_here = sources.shape[1]
    position = lax.axis_index("box")
    layer = lax.axis_index("layer")
    is_second = position % 2 == 1

    chain = [(layer_at, (OWN, PAIR)) for layer_at in range(2, layers, 2)]
    pair_moves = [(layer_at + 1, layer_at) for layer_at in range(0, layers, 2)]

    def route(moves, source_core=0, target_core=0):
        return [
            (a * boxes + b + source_core, z * boxes + b + target_core)
            for a, z in moves
            for b in range(0, boxes, 2)
        ]

    def over_box(change, starts):
        return [(i * boxes + b, i * boxes + (b ^ change)) for i in range(layers) for b in starts]

    def send(value, pairs_of_devices):
        return lax.ppermute(value, AXES, pairs_of_devices)

    def after(value, *others):
        return lax.optimization_barrier((value, *others))[0]

    every = [(i, i) for i in range(layers)]

    raw = box_maps[0]
    pattern = block_pattern[0]
    raw_other = send(raw, over_box(1, range(boxes)))
    pattern_other = send(pattern, over_box(1, range(boxes)))
    other_sources = send(sources[0], over_box(1, range(boxes)))
    own_half = pl.pallas_call(
        mask_kernel,
        out_shape=jax.ShapeDtypeStruct(raw.shape, jnp.bfloat16),
        in_specs=[SMEM, VMEM],
        out_specs=VMEM,
        compiler_params=PARAMS,
        cost_estimate=cost(width * width, 4 * width * width),
    )(pattern, raw)

    def inverse_of(level):
        node = (boxes >> (level + 1)) - 1 + (position >> (level + 1))
        return lax.dynamic_index_in_dim(face_inverses[0], node, 0, keepdims=False).astype(
            jnp.bfloat16
        )

    rows = -(-2 * rows_here // 8) * 8
    packed = jnp.concatenate(
        [
            jnp.where(is_second, other_sources, sources[0]),
            jnp.where(is_second, sources[0], other_sources),
            jnp.zeros((rows - 2 * rows_here, width), jnp.float32),
            index_map.astype(jnp.float32),
        ],
        axis=0,
    )

    pieces = tuple((at, face) for at in range(0, width, face))
    upper = tuple(piece for piece in pieces if piece[0] < width // 2)
    lower = tuple(piece for piece in pieces if piece[0] >= width // 2)
    inverse = inverse_of(0)
    top = leaf_combine(pattern_other, own_half, raw_other, inverse, None, 0, upper)
    bottom = leaf_combine(pattern_other, own_half, raw_other, inverse, top[-1], 1, lower)
    current = dict(zip(upper + lower, [*top[:-1], *bottom]))

    for level in range(1, levels):
        final = level == levels - 1
        change = 1 << level
        inverse = inverse_of(level)
        order = sorted(pieces, key=lambda piece: (piece[0] != level * face, piece[0]))
        received = {}
        state = None
        if not final:
            for piece in order:
                received[piece] = send(current[piece], over_box(change, range(boxes)))
            renewed = {}
            for piece in order:
                renewed[piece], state = combine(
                    current[piece],
                    received[piece],
                    inverse,
                    None,
                    state,
                    level * face,
                    piece[0],
                    order[: order.index(piece)],
                )
            current = renewed
            continue
        over = over_box(change ^ 1, range(0, boxes, 2))
        forward = route(pair_moves, 1, 0)
        for piece in order[:AHEAD]:
            received[piece] = send(current[piece], over)
        pair_pieces = {}
        for k, piece in enumerate(order):
            following = order[k + AHEAD] if k + AHEAD < len(order) else None
            other = received[piece]
            if k == SMALL_AT + 2:
                other = after(other, pair_packed)
            if k > AHEAD:
                other = after(other, pair_pieces[order[k - 1]])
            payload, state = combine(
                current[piece],
                other,
                inverse,
                None if following is None else current[following],
                state,
                level * face,
                piece[0],
                order[:k],
            )
            pair_pieces[piece] = send(payload, forward + ([] if following is None else over))
            if following is not None:
                received[following] = pair_pieces[piece]
            if k == SMALL_AT:
                sendable = after(packed, payload)
                pair_packed = send(sendable, route(pair_moves[1:]) + route([(0, 1)], 1, 1))
    merged = state[1]
    small = [packed, pair_packed]
    pair_maps = [pair_pieces[piece] for piece in pieces]

    first = pair_packed[:rows].astype(jnp.bfloat16)
    (down_odd,), state = segment(
        coupling, 1, first, small, {}, [[merged], pair_maps], (OWN,), ()
    )
    merged_first = send(after(merged, state), route(every, 1, 0))
    maps = [[merged_first], pair_maps]
    at, core = 1, 1
    kept = []
    ups = {}
    for k, (target, slots) in enumerate(chain):
        arrived = send(state, route([(at, target)], core, 0))
        at, core = target, 0
        turn = k == len(chain) - 1
        back = tuple(reversed(slots))
        results, state = segment(
            coupling, at, arrived, small, {}, maps, slots, back[1:] if turn else ()
        )
        kept.append(dict(zip(slots, results)))
        if k == 0:
            down_odd_pair = send(after(down_odd, state), route([(1, 0)], 1, 0))
            down_odd_first = send(after(down_odd, state), route([(1, 1)], 1, 0))
        if turn:
            ups[at] = dict(zip(back[1:], results[len(slots) :]))
            ups[at][back[0]] = results[len(slots) - 1]
    merged = jnp.where(is_second, merged, merged_first)
    down_odd = down_odd_pair + down_odd_first

    for k in reversed(range(len(chain) - 1)):
        target, slots = chain[k]
        arrived = send(state, route([(at, target)]))
        if k == len(chain) - 2:
            arrived, merged = lax.optimization_barrier((arrived, merged))
        at = target
        back = tuple(reversed(slots))
        results, state = segment(coupling, at, arrived, small, kept[k], maps, (), back)
        ups[at] = dict(zip(back, results))
    from_own = send(state, route([(at, 1)]))
    from_pair = send(state, route([(at, 0)]))

    mine = [jnp.zeros((rows, width), jnp.float32)] * 2
    for target, values in ups.items():
        for slot in (OWN, PAIR):
            mine[slot] = jnp.where(layer == target, values[slot], mine[slot])
    settled = mine[OWN] + send(mine[PAIR], route([(z, a) for a, z in pair_moves[1:]]))

    last = pl.pallas_call(
        functools.partial(last_kernel, coupling, len(pair_maps)),
        out_shape=jax.ShapeDtypeStruct((rows, width), jnp.float32),
        in_specs=[VMEM] * (5 + len(pair_maps)),
        out_specs=VMEM,
        compiler_params=SWEEP_PARAMS,
        cost_estimate=cost(6 * 256 * 1024 * 1024, 6 * 1024 * 1024),
    )(from_pair, from_own, packed[:rows], down_odd, merged_first, *pair_maps)
    upward = jnp.where(layer < 2, last, settled)
    second_rows = send(upward[rows_here : 2 * rows_here], route(every, 0, 1))
    upward = jnp.where(is_second, second_rows, upward[:rows_here])
    return (merged[None], upward[None])


def solution(mesh):
    return jax.shard_map(
        on_device,
        mesh=mesh,
        in_specs=(
            P("layer", "box", None),
            P("layer", "box", None),
            P("layer", None, None, None),
            P("layer", None),
            P("layer", "box", None),
        ),
        out_specs=(P("layer", None, None), P("layer", "box", None)),
        check_vma=False,
    )
```
